32 devices in a mesh: st: 8 (over z, x), sb: 4 (over y, core).
Axes of the slice: x: 2, y: 2, z: 4, core: 2. Of those that a mesh axis runs over, the one named last changes fastest.
Arguments:
- volts: bfloat16 [2, 1024, 126976], P(None, 'st'), may hold values from -6 to 6
- prototype: float32 [16, 4096], replicated, may hold values from -1.5 to 1.5
- beam_channels: int32 [384], replicated, may hold values from 0 to 4095, as said below
- station_index: int32 [256], replicated, may hold values from 0 to 511, as said below
- delays: float32 [256, 256], replicated, may hold values from -64 to 64
- gains: float32 [256, 256], replicated, may hold values from 0.5 to 2
- assign: int32 [384, 1], replicated, may hold values from 0 to 3; in each aligned block of 384 rows (0 to 383, 384 to 767, ...) at most 160 rows name the same one
Outputs:
- visibility: float32 [2, 4, 8, 1024, 1024], P(None, 'sb', 'st')
- beam_out: float32 [4, 160, 2, 16, 512], P('sb', 'st')
The draws below stay inside these ranges and needn't reach their ends.
Inputs may be any that keep to these rules, and one draw needn't show every extreme that they name: `beam_channels`: 384 different channels. `station_index`: 256 different stations. `assign`: no index of sb receives more than 160 list entries, and some index receives exactly 160; every index receives at least one.
All inputs are finite; a program needn't handle non-finite values.
Results may differ from the reference program's by a relative error of at most 0.0054.
Values may be sent and summed in bfloat16 or wider, within the bound.
No kernel may reach another device: no remote copies, remote signals or barrier semaphores. Data moves between devices by JAX's collectives and lax.ppermute only.
A program may use at most 320 MiB of HBM per device.

```python
import math
import jax
import jax.numpy as jnp
import numpy as np
from jax import lax

NCH = 4096
STATIONS = 512
TAPS = 16
FRAMES = 16
BEAMS = 256
BST = 256
BEAM_CH = 384
SLOTS = 160
SIGNALS = 1024
SAMPLES = 126976
CH_X = 128
N_ST = 8
N_SB = 4


def draw_beam_channels(key, part):
    return jax.random.permutation(jax.random.fold_in(key, 17), NCH)[:BEAM_CH].astype(jnp.int32)


def draw_station_index(key, part):
    return jax.random.permutation(jax.random.fold_in(key, 29), STATIONS)[:BST].astype(jnp.int32)


def level_of(stream_key, extent, cuts, low, largest):
    def one(dim, blocks):
        draws = jax.random.uniform(jax.random.fold_in(jax.random.fold_in(stream_key, 6), dim), (blocks,), jnp.float32, low / len(cuts), largest / len(cuts))
        return jnp.repeat(jnp.exp(draws), extent[dim] // blocks).reshape((-1,) + (1,) * (len(extent) - dim - 1))

    level = one(*cuts[0])
    for cut in cuts[1:]:
        level = level * one(*cut)
    return level


def shared_out(stream_key, own, number, rows, amount, top, bound, skew):
    sequence = jax.random.permutation(stream_key, amount)
    heavy_load, usual = load_shares(amount, rows * top, bound, skew, True), load_shares(amount, rows * top, bound, skew, False)
    places = jnp.arange(amount)

    def named(lengths, rotation):
        used = int((lengths > 0).sum())
        fixed = max(1, used // 4)
        passed = fixed + (places - fixed + rotation * (used - fixed)) % max(1, amount - fixed)
        return jnp.zeros((amount,), jnp.int32).at[sequence[jnp.where(places < fixed, places, passed)]].set(jnp.asarray(lengths, jnp.int32))

    lengths = jnp.where(number % 4 == 0, named(heavy_load, number // 4), named(usual, number - number // 4 - 1))
    mixed = jax.random.permutation(jax.random.fold_in(own, 3), amount)
    source_of, receiver = mixed[0:amount // 2 * 2:2], mixed[1:amount // 2 * 2:2]
    margin = jnp.minimum(lengths[source_of] - 1, bound - lengths[receiver]) // 2
    margin = jnp.where((source_of == sequence[0]) | (receiver == sequence[0]) | (lengths[receiver] == 0), 0, jnp.maximum(margin, 0))
    passed = jax.random.randint(jax.random.fold_in(own, 4), (amount // 2,), 0, 1 << 20) % (margin + 1)
    lengths = lengths.at[source_of].add(-passed).at[receiver].add(passed)
    labels = jnp.searchsorted(jnp.cumsum(lengths), jnp.arange(rows * top), side="right").astype(jnp.int32)
    grid = labels.reshape(top, rows).T
    grid = grid[jax.random.permutation(jax.random.fold_in(own, 1), rows)]
    rotation = jax.random.randint(jax.random.fold_in(own, 2), (rows, 1), 0, top)
    return jnp.take_along_axis(grid, (jnp.arange(top)[None, :] + rotation) % top, axis=1)


def load_shares(amount, total, most, lean, full):
    loads = [(1 << 20) // math.isqrt(standing ** lean) + 1 for standing in range(1, amount + 1)]
    largest = most if full else min(most, max(-(-total // amount), total * loads[0] // sum(loads)))
    least = 1 if total - largest >= amount - 1 else 0
    holding, rest = [largest] + [least] * (amount - 1), total - largest - least * (amount - 1)
    while rest > 0:
        movable = [i for i in range(1, amount) if holding[i] < largest] or [i for i in range(1, amount) if holding[i] < most]
        whole, remaining = sum([loads[i] for i in movable]), rest
        for i in movable:
            more = min(most - holding[i], max(1, remaining * loads[i] // whole), rest)
            holding[i] = holding[i] + more
            rest = rest - more
    return np.array(holding)


def scatter_about(key, dims, deviation, reach, shards=(), kind=jnp.bfloat16):
    array = jax.random.normal(key, dims, jnp.float32) * deviation
    if len(shards) > 0:
        array = level_of(key, dims, shards, -0.22, 0.18) * array
    return jnp.clip(array, min=-reach, max=reach).astype(kind)


def setup_inputs(seed: int = 0) -> dict:
    seeds = jax.random.split(jax.random.key(seed), 8)
    volts = scatter_about(seeds[0], (2, SIGNALS, SAMPLES), 1.0, 6.0, ((1, 8),))
    prototype = scatter_about(seeds[1], (TAPS, NCH), 0.25, 1.5, (), jnp.float32)
    beam_channels = draw_beam_channels(jax.random.fold_in(seeds[7], 71), 0)
    station_index = draw_station_index(jax.random.fold_in(seeds[7], 71), 0)
    delays = jnp.clip(jax.random.uniform(seeds[4], (BEAMS, BST), jnp.float32, -64.0, 64.0), -64.0, 64.0)
    gains = jnp.clip(jnp.exp(jax.random.uniform(seeds[5], (BEAMS, BST), jnp.float32, math.log(0.5), math.log(2.0))), 0.5, 2.0)
    assign_keys = jax.random.split(jax.random.fold_in(seeds[6], 1), BEAM_CH // BEAM_CH)
    assign_turns = jax.random.permutation(jax.random.fold_in(seeds[6], 3), BEAM_CH // BEAM_CH)
    assign = jax.vmap(lambda own, number: shared_out(jax.random.fold_in(seeds[6], 2), own, number, BEAM_CH, N_SB, 1, SLOTS, 2))(assign_keys, assign_turns).reshape((BEAM_CH, 1))
    return dict(volts=volts, prototype=prototype, beam_channels=beam_channels, station_index=station_index, delays=delays, gains=gains, assign=assign)


TWO_PI = 2.0 * math.pi

def polyphase(volts, prototype, frame_count):
    tap_count = prototype.shape[0]
    length = prototype.shape[1]
    segments = volts.reshape(2, volts.shape[1], frame_count + tap_count - 1, length)
    summed = jnp.zeros((2, volts.shape[1], frame_count, length), jnp.float32)
    for tap_idx in range(tap_count):
        summed = summed + prototype[tap_idx] * segments[:, :, tap_idx:tap_idx + frame_count, :].astype(jnp.float32)
    return summed.astype(jnp.bfloat16)

def dft_tables(channels, length):
    sample_ids = jnp.arange(length, dtype=jnp.int32)
    phase_ids = sample_ids[:, None] * channels[None, :].astype(jnp.int32) % length
    angles = phase_ids.astype(jnp.float32) * (TWO_PI / length)
    scale_dft = 1.0 / math.sqrt(length)
    return ((jnp.cos(angles) * scale_dft).astype(jnp.bfloat16), (jnp.sin(angles) * scale_dft).astype(jnp.bfloat16))

def transform(flat_rows, cos_t, sin_t):
    real_part = jnp.dot(flat_rows[0], cos_t, preferred_element_type=jnp.float32) + jnp.dot(flat_rows[1], sin_t, preferred_element_type=jnp.float32)
    imag_part = jnp.dot(flat_rows[1], cos_t, preferred_element_type=jnp.float32) - jnp.dot(flat_rows[0], sin_t, preferred_element_type=jnp.float32)
    return jnp.stack([real_part, imag_part]).astype(jnp.bfloat16)

def correlate(grouped):
    stacked = jnp.concatenate([grouped[0], grouped[1]], axis=1)
    turned = jnp.concatenate([grouped[1], -grouped[0]], axis=1)
    inverse = 1.0 / grouped.shape[2]
    vis_re = jnp.dot(stacked, stacked.T, preferred_element_type=jnp.float32) * inverse
    vis_im = jnp.dot(turned, stacked.T, preferred_element_type=jnp.float32) * inverse
    return jnp.stack([vis_re, vis_im])

def beam_weights(delays, gains, channel, length, listed):
    angles = delays * (channel.astype(jnp.float32) * (TWO_PI / length))
    scaling = gains * (1.0 / math.sqrt(listed))
    return ((scaling * jnp.cos(angles)).astype(jnp.bfloat16), (-scaling * jnp.sin(angles)).astype(jnp.bfloat16))

def combine(spectrum, w_re, w_im):
    real_in = spectrum[:, 0]
    imag_in = spectrum[:, 1]

    def product(operand, weight):
        return jnp.einsum('sfjp,sbj->sfpb', operand, weight, preferred_element_type=jnp.float32)
    out_re = product(real_in, w_re) - product(imag_in, w_im)
    out_im = product(imag_in, w_re) + product(real_in, w_im)
    stacked = jnp.stack([out_re, out_im], axis=1)
    return stacked.reshape(stacked.shape[0], 2, stacked.shape[2], -1)

def reference(volts, prototype, beam_channels, station_index, delays, gains, assign):
    signals = volts.shape[1]
    filtered = polyphase(volts, prototype, FRAMES)
    flat_rows = filtered.reshape(2, signals * FRAMES, NCH)
    cos_t, sin_t = dft_tables(jnp.arange(NCH, dtype=jnp.int32), NCH)
    spectra = transform(flat_rows, cos_t, sin_t).reshape(2, signals, FRAMES, NCH)
    groups = NCH // CH_X
    grouped = jnp.moveaxis(spectra.reshape(2, signals, FRAMES, groups, CH_X), 3, 0).reshape(groups, 2, signals, FRAMES * CH_X)
    visibility = lax.map(correlate, grouped)
    visibility = jnp.moveaxis(visibility, 1, 0).reshape(2, N_SB, N_ST, signals, signals)
    chosen = jnp.moveaxis(jnp.take(spectra, beam_channels, axis=3), 3, 0)
    listed = station_index.shape[0]

    def one_entry(packed):
        spectrum, channel = packed
        stations = jnp.swapaxes(spectrum, 1, 2).reshape(1, 2, FRAMES, signals // 2, 2)
        picked = jnp.take(stations, station_index, axis=3)
        w_re, w_im = beam_weights(delays[None], gains[None], channel.reshape(1, 1, 1), NCH, listed)
        return combine(picked.astype(jnp.float32), w_re.astype(jnp.float32), w_im.astype(jnp.float32))[0]
    entries = lax.map(one_entry, (chosen, beam_channels))
    owners = assign[:, 0]
    order = jnp.arange(BEAM_CH, dtype=jnp.int32)
    earlier = (owners[:, None] == owners[None, :]) & (order[None, :] < order[:, None])
    position = lax.optimization_barrier(jnp.sum(earlier.astype(jnp.int32), axis=1))
    beam_out = jnp.zeros((N_SB, SLOTS, 2, FRAMES, 2 * BEAMS), jnp.float32).at[owners, position].set(entries)
    return (visibility, beam_out)
```

```python
import functools
import math

import jax
import jax.numpy as jnp
from jax import lax
from jax.experimental import pallas as pl
from jax.experimental.pallas import tpu as pltpu
from jax.sharding import PartitionSpec as P

NCH = 4096
FRAMES = 16
SLOTS = 160
RADIX = 8
LANES = 128
ROWS = 16
CHUNK = 32
VMEM = 56 * 1024 * 1024

TWO_PI = 2.0 * math.pi
NT = (((1,), (1,)), ((), ()))


def phase(turns, length):
    angles = (turns % length).astype(jnp.float32) * (TWO_PI / length)
    return jnp.cos(angles), jnp.sin(angles)


def table_kernel(hi_c, hi_s, lo_c, lo_s, out):
    coarse = hi_c.shape[1]
    fine = lo_c.shape[1]
    width = lo_c.shape[2]
    depth = coarse * fine

    def branch(b, carry):
        low_c, low_s = lo_c[b], lo_s[b]

        def block(a, inner):
            high_c, high_s = hi_c[b, pl.ds(a, 1), :], hi_s[b, pl.ds(a, 1), :]
            cos_t = high_c * low_c - high_s * low_s
            sin_t = high_s * low_c + high_c * low_s
            top = pl.multiple_of(a * fine, fine)
            out[b, pl.ds(top, fine), :width] = cos_t.astype(out.dtype)
            out[b, pl.ds(top, fine), width:] = (-sin_t).astype(out.dtype)
            out[b, pl.ds(depth + top, fine), :width] = sin_t.astype(out.dtype)
            out[b, pl.ds(depth + top, fine), width:] = cos_t.astype(out.dtype)
            return inner

        return lax.fori_loop(0, coarse, block, carry)

    lax.fori_loop(0, hi_c.shape[0], branch, 0)


def radix8(re, im):
    half = math.sqrt(0.5)

    def four(xr, xi):
        ar, ai, br, bi = xr[0] + xr[2], xi[0] + xi[2], xr[0] - xr[2], xi[0] - xi[2]
        cr, ci, dr, di = xr[1] + xr[3], xi[1] + xi[3], xr[1] - xr[3], xi[1] - xi[3]
        return [ar + cr, br + di, ar - cr, br - di], [ai + ci, bi - dr, ai - ci, bi + dr]

    er, ei = four(re[0::2], im[0::2])
    odd_r, odd_i = four(re[1::2], im[1::2])
    tr = [odd_r[0], (odd_r[1] + odd_i[1]) * half, odd_i[2], (odd_i[3] - odd_r[3]) * half]
    ti = [odd_i[0], (odd_i[1] - odd_r[1]) * half, -odd_r[2], (odd_r[3] + odd_i[3]) * -half]
    return (
        [e + t for e, t in zip(er, tr)] + [e - t for e, t in zip(er, tr)],
        [e + t for e, t in zip(ei, ti)] + [e - t for e, t in zip(ei, ti)],
    )


def swap_blocks(parts, lane_ids):
    count = len(parts)
    width = LANES // count
    parts = list(parts)
    step = 1
    while step < count:
        keep = (lane_ids // width) % (2 * step) < step
        for b in range(count):
            if b & step == 0:
                low, high = parts[b], parts[b + step]
                parts[b] = jnp.where(keep, low, pltpu.roll(high, step * width, 1))
                parts[b + step] = jnp.where(keep, pltpu.roll(low, LANES - step * width, 1), high)
        step *= 2
    return parts


def channel_kernel(volts, prototype, table, *rest):
    outs = rest[:RADIX]
    branches, filtered, product = rest[RADIX:]
    taps = prototype.shape[0]
    length = prototype.shape[1]
    frames = filtered.shape[2]
    depth = length // RADIX

    def column(j, carry):
        def strip(n1, inner):
            base = pl.multiple_of(n1 * depth + j * LANES, LANES)
            coefs = [prototype[t : t + 1, pl.ds(base, LANES)] for t in range(taps)]
            for part in range(2):
                sums = [None] * frames
                for seg in range(frames + taps - 1):
                    start = pl.multiple_of(seg * length + base, LANES)
                    value = volts[part, :, pl.ds(start, LANES)].astype(jnp.float32)
                    for f in range(max(0, seg - taps + 1), min(frames, seg + 1)):
                        term = coefs[seg - f] * value
                        sums[f] = term if sums[f] is None else sums[f] + term
                    if seg >= taps - 1:
                        filtered[part, n1, seg - taps + 1] = sums[seg - taps + 1]
            return inner

        lax.fori_loop(0, RADIX, strip, 0)

        def butterfly(f, inner):
            re, im = radix8(
                [filtered[0, n1, f] for n1 in range(RADIX)],
                [filtered[1, n1, f] for n1 in range(RADIX)],
            )
            for b in range(RADIX):
                branches[b, f, :, pl.ds(pl.multiple_of(j * LANES, LANES), LANES)] = re[b].astype(branches.dtype)
                branches[b, f, :, pl.ds(pl.multiple_of(depth + j * LANES, LANES), LANES)] = im[b].astype(branches.dtype)
            return inner

        lax.fori_loop(0, frames, butterfly, 0)
        return carry

    lax.fori_loop(0, depth // LANES, column, 0)

    def multiply(b, carry):
        rows = branches[b].reshape(frames * ROWS, 2 * depth)
        product[b] = jnp.dot(rows, table[b], preferred_element_type=jnp.float32)
        return carry

    lax.fori_loop(0, RADIX, multiply, 0)
    lane_ids = lax.broadcasted_iota(jnp.int32, (ROWS, LANES), 1)

    def regroup(f, carry):
        top = pl.multiple_of(f * ROWS, ROWS)
        for part in range(2):
            pieces = [product[b, pl.ds(top, ROWS), part * LANES : (part + 1) * LANES] for b in range(RADIX)]
            for g, piece in enumerate(swap_blocks(pieces, lane_ids)):
                lane = pl.multiple_of(part * frames * LANES + f * LANES, LANES)
                outs[g][:, pl.ds(lane, LANES)] = piece.astype(outs[g].dtype)
        return carry

    lax.fori_loop(0, frames, regroup, 0)


def channelise(volts, prototype, table, first, count):
    length = volts.shape[2]
    steps = count // ROWS
    depth = NCH // RADIX
    wide = 2 * FRAMES * LANES
    work = 2 * count * FRAMES * NCH
    return pl.pallas_call(
        channel_kernel,
        grid=(steps,),
        in_specs=[
            pl.BlockSpec((2, ROWS, length), lambda i: (0, first // ROWS + i, 0)),
            pl.BlockSpec(prototype.shape, lambda i: (0, 0)),
            pl.BlockSpec(table.shape, lambda i: (0, 0, 0)),
        ],
        out_specs=[pl.BlockSpec((ROWS, wide), lambda i: (i, 0))] * RADIX
        + [pl.BlockSpec((RADIX, FRAMES, ROWS, 2 * depth), lambda i: (0, 0, i, 0))],
        out_shape=[jax.ShapeDtypeStruct((count, wide), jnp.bfloat16)] * RADIX
        + [jax.ShapeDtypeStruct((RADIX, FRAMES, count, 2 * depth), jnp.bfloat16)],
        scratch_shapes=[
            pltpu.VMEM((2, RADIX, FRAMES, ROWS, LANES), jnp.float32),
            pltpu.VMEM((RADIX, FRAMES * ROWS, 2 * LANES), jnp.float32),
        ],
        compiler_params=pltpu.CompilerParams(vmem_limit_bytes=VMEM),
        cost_estimate=pl.CostEstimate(
            flops=work * 2 * depth, bytes_accessed=2 * count * length * 2 + 4 * work, transcendentals=0
        ),
    )(volts, prototype, table)


def slot_kernel(row_branch, hi_c, hi_s, lo_c, lo_s, *rest):
    chunks = rest[: len(rest) - 2]
    table, total = rest[len(rest) - 2 :]
    chunks, outs = [c for c in chunks if len(c.shape) == 4], [c for c in chunks if len(c.shape) == 2]
    depth = chunks[0].shape[3] // 2
    f_step = chunks[0].shape[1]

    @pl.when(pl.program_id(0) == 0)
    def _():
        for a in range(hi_c.shape[1]):
            high_c, high_s = hi_c[:, a : a + 1], hi_s[:, a : a + 1]
            table[:, a * LANES : (a + 1) * LANES] = (high_c * lo_c[...] - high_s * lo_s[...]).astype(table.dtype)
            table[:, depth + a * LANES : depth + (a + 1) * LANES] = (
                high_s * lo_c[...] + high_c * lo_s[...]
            ).astype(table.dtype)

    total[...] = jnp.zeros_like(total)

    def branch(b, carry):
        rows = jnp.concatenate([c[b, f] for f in range(f_step) for c in chunks], axis=0)
        got = lax.dot_general(table[...], rows, NT, preferred_element_type=jnp.float32)
        total[...] = jnp.where(row_branch[...] == b, got, total[...])
        return carry

    lax.fori_loop(0, RADIX, branch, 0)
    sig = total.shape[1] // f_step
    per = total.shape[0] // len(outs)
    for s, out in enumerate(outs):
        out[...] = jnp.concatenate(
            [total[s * per : (s + 1) * per, f * sig : (f + 1) * sig] for f in range(f_step)], axis=0
        ).astype(out.dtype)


def slot_spectra(row_channel, row_filled, row_turned, chunks, st_count):
    depth = NCH // RADIX
    rows = row_channel.shape[0]
    sig_dev = sum(c.shape[2] for c in chunks)
    f_step = 2 * LANES // sig_dev
    per = rows // st_count
    coarse = jnp.arange(depth // LANES, dtype=jnp.int32) * LANES
    fine = jnp.arange(LANES, dtype=jnp.int32)
    hi_c, hi_s = phase(row_channel[:, None] * coarse[None, :] + row_turned[:, None] * (NCH // 4), NCH)
    lo_c, lo_s = phase(row_channel[:, None] * fine[None, :], NCH)
    scaling = row_filled.astype(jnp.float32)[:, None] * (1.0 / math.sqrt(NCH))
    row_branch = (row_channel % RADIX)[:, None]
    small = [row_branch, hi_c * scaling, hi_s * scaling, lo_c, lo_s]
    return pl.pallas_call(
        slot_kernel,
        grid=(FRAMES // f_step,),
        in_specs=[pl.BlockSpec(x.shape, lambda i: (0, 0)) for x in small]
        + [pl.BlockSpec((RADIX, f_step, c.shape[2], 2 * depth), lambda i: (0, i, 0, 0)) for c in chunks],
        out_specs=[pl.BlockSpec((f_step * per, sig_dev), lambda i: (i, 0))] * st_count,
        out_shape=[jax.ShapeDtypeStruct((FRAMES * per, sig_dev), jnp.bfloat16)] * st_count,
        scratch_shapes=[
            pltpu.VMEM((rows, 2 * depth), jnp.bfloat16),
            pltpu.VMEM((rows, f_step * sig_dev), jnp.float32),
        ],
        compiler_params=pltpu.CompilerParams(vmem_limit_bytes=VMEM),
        cost_estimate=pl.CostEstimate(
            flops=2 * rows * 2 * NCH * FRAMES * sig_dev,
            bytes_accessed=4 * NCH * FRAMES * sig_dev,
            transcendentals=0,
        ),
    )(*small, *chunks)


def correlate(here, received, st_count):
    flat = [(c, s, piece) for c, row in enumerate(received) for s, piece in enumerate(row)]
    rows = [row[0].shape[0] for row in received]
    sig_dev = sum(rows)
    signals = sig_dev * st_count
    wide = flat[0][2].shape[1]
    block = min(256, signals)
    blocks = signals // block
    half = wide // 2

    def kernel(here_ref, *refs):
        pieces, (out, held, sems) = refs[:-3], refs[-3:]
        copies = []
        for index, (c, s, _) in enumerate(flat):
            top = (here_ref[0] ^ s) * sig_dev + sum(rows[:c])
            dst = held.at[pl.ds(pl.multiple_of(top, ROWS), rows[c])]
            copies.append(pltpu.make_async_copy(pieces[index], dst, sems.at[index]))
        for copy in copies:
            copy.start()
        for copy in copies:
            copy.wait()
        inverse = 1.0 / half

        def product(left, right):
            return lax.dot_general(left, right, NT, preferred_element_type=jnp.float32)

        for i in range(blocks):
            for j in range(i + 1):
                at_i, at_j = slice(i * block, (i + 1) * block), slice(j * block, (j + 1) * block)
                re = (
                    product(held[at_i, :half], held[at_j, :half]) + product(held[at_i, half:], held[at_j, half:])
                ) * inverse
                im = (
                    product(held[at_i, half:], held[at_j, :half]) - product(held[at_i, :half], held[at_j, half:])
                ) * inverse
                out[0, at_i, at_j] = re
                out[1, at_i, at_j] = im
                if i != j:
                    out[0, at_j, at_i] = re.T
                    out[1, at_j, at_i] = -im.T

    return pl.pallas_call(
        kernel,
        in_specs=[pl.BlockSpec(memory_space=pltpu.SMEM)] + [pl.BlockSpec(memory_space=pl.ANY)] * len(flat),
        out_specs=pl.BlockSpec(memory_space=pltpu.VMEM),
        out_shape=jax.ShapeDtypeStruct((2, signals, signals), jnp.float32),
        scratch_shapes=[
            pltpu.VMEM((signals, wide), jnp.bfloat16),
            pltpu.SemaphoreType.DMA((len(flat),)),
        ],
        compiler_params=pltpu.CompilerParams(vmem_limit_bytes=VMEM),
        cost_estimate=pl.CostEstimate(
            flops=2 * signals * signals * wide,
            bytes_accessed=2 * signals * wide + 8 * signals * signals,
            transcendentals=0,
        ),
    )(here, *[piece for _, _, piece in flat])


def weight_kernel(channel, delays, gains, out):
    beams = delays.shape[0]
    turns = delays[...] * (channel[pl.program_id(0)].astype(jnp.float32) * (1.0 / NCH))
    part = turns - jnp.floor(turns + 0.5)
    square = part * part
    cos_t = jnp.full_like(part, TWO_PI**16 / math.factorial(16))
    sin_t = jnp.full_like(part, -(TWO_PI**15) / math.factorial(15))
    for power in range(14, -1, -2):
        sign = -1.0 if power % 4 == 2 else 1.0
        cos_t = cos_t * square + sign * TWO_PI**power / math.factorial(power)
        if power > 0:
            sign = -1.0 if (power - 1) % 4 == 3 else 1.0
            sin_t = sin_t * square + sign * TWO_PI ** (power - 1) / math.factorial(power - 1)
    scaled = gains[...] * (1.0 / math.sqrt(gains.shape[1]))
    out[0, :beams] = (scaled * cos_t).astype(out.dtype)
    out[0, beams:] = (-scaled * sin_t * part).astype(out.dtype)


def beam_weights(channel, delays, gains):
    beams, listed = delays.shape
    slots = channel.shape[0]
    return pl.pallas_call(
        weight_kernel,
        grid=(slots,),
        in_specs=[
            pl.BlockSpec(memory_space=pltpu.SMEM),
            pl.BlockSpec(delays.shape, lambda i: (0, 0)),
            pl.BlockSpec(gains.shape, lambda i: (0, 0)),
        ],
        out_specs=pl.BlockSpec((1, 2 * beams, listed), lambda i: (i, 0, 0)),
        out_shape=jax.ShapeDtypeStruct((slots, 2 * beams, listed), jnp.bfloat16),
        cost_estimate=pl.CostEstimate(
            flops=40 * slots * beams * listed, bytes_accessed=4 * slots * beams * listed, transcendentals=0
        ),
    )(channel, delays, gains)


def combine(pieces, chooser, weights):
    slots, beams2, listed = weights.shape
    beams = beams2 // 2
    sig_dev = pieces[0].shape[1]
    total_rows = pieces[0].shape[0]
    tiles = 2 * listed // LANES

    def kernel(*refs):
        got, (choose, weight, out, picked) = refs[: len(pieces)], refs[len(pieces) :]
        acc = None
        for s, piece in enumerate(got):
            term = jnp.dot(
                piece[...], choose[s * sig_dev : (s + 1) * sig_dev, :], preferred_element_type=jnp.float32
            )
            acc = term if acc is None else acc + term
        for lane in range(tiles):
            picked[lane] = acc[:, lane * LANES : (lane + 1) * LANES]
        for i in range(slots):
            rows = jnp.concatenate(
                [
                    jnp.concatenate(
                        [
                            picked[p * tiles // 2 + lane, pl.ds(part * slots + i, FRAMES, 2 * slots), :]
                            for lane in range(tiles // 2)
                        ],
                        axis=1,
                    )
                    for p in range(2)
                    for part in range(2)
                ],
                axis=0,
            )
            mixed = lax.dot_general(rows.astype(jnp.bfloat16), weight[i], NT, preferred_element_type=jnp.float32)
            for p in range(2):
                at = 2 * FRAMES * p
                of_re, of_im = mixed[at : at + FRAMES], mixed[at + FRAMES : at + 2 * FRAMES]
                out[0, i, 0, :, p * beams : (p + 1) * beams] = of_re[:, :beams] - of_im[:, beams:]
                out[0, i, 1, :, p * beams : (p + 1) * beams] = of_im[:, :beams] + of_re[:, beams:]

    return pl.pallas_call(
        kernel,
        out_shape=jax.ShapeDtypeStruct((1, slots, 2, FRAMES, 2 * beams), jnp.float32),
        scratch_shapes=[pltpu.VMEM((tiles, total_rows, LANES), jnp.float32)],
        compiler_params=pltpu.CompilerParams(vmem_limit_bytes=VMEM),
        cost_estimate=pl.CostEstimate(
            flops=2 * total_rows * 2 * listed * (sig_dev * len(pieces) + 2 * beams),
            bytes_accessed=8 * total_rows * listed,
            transcendentals=0,
        ),
    )(*pieces, chooser, weights)


def exchange(pieces, st_count):
    return [pieces[0]] + [
        lax.ppermute(pieces[s], "st", [(i, i ^ s) for i in range(st_count)]) for s in range(1, st_count)
    ]


def after(value, other):
    return lax.optimization_barrier((value, other))[0]


def body(volts, prototype, beam_channels, station_index, delays, gains, assign):
    sig_dev = volts.shape[1]
    st_count = lax.axis_size("st")
    sb_count = lax.axis_size("sb")
    sb_here = lax.axis_index("sb").astype(jnp.int32)
    st_here = lax.axis_index("st").astype(jnp.int32)
    partner = st_here ^ jnp.arange(st_count, dtype=jnp.int32)

    band = NCH // sb_count
    fine = band // RADIX // st_count
    depth = NCH // RADIX
    low = (partner[:, None] * fine + jnp.arange(fine, dtype=jnp.int32)[None, :]).reshape(-1)
    channels = sb_here * band + jnp.arange(RADIX, dtype=jnp.int32)[:, None] + RADIX * low[None, :]
    lo_ids = jnp.arange(ROWS, dtype=jnp.int32)
    hi_ids = jnp.arange(depth // ROWS, dtype=jnp.int32) * ROWS
    lo_c, lo_s = phase(channels[:, None, :] * lo_ids[None, :, None], NCH)
    hi_c, hi_s = phase(channels[:, None, :] * hi_ids[None, :, None], NCH)
    scale = 1.0 / math.sqrt(NCH)
    table = pl.pallas_call(
        table_kernel,
        out_shape=jax.ShapeDtypeStruct((RADIX, 2 * depth, 2 * LANES), jnp.bfloat16),
        compiler_params=pltpu.CompilerParams(vmem_limit_bytes=VMEM),
    )(hi_c * scale, hi_s * scale, lo_c, lo_s)

    chunk = min(CHUNK, sig_dev)
    received, branches = [], []
    for first in range(0, sig_dev, chunk):
        if len(received) > 1:
            table = after(table, received[-2])
        *groups, kept = channelise(volts, prototype, table, first, chunk)
        table = after(table, groups[0])
        branches.append(kept)
        if st_count > RADIX:
            inner = st_count // RADIX
            split = [
                jnp.moveaxis(g.reshape(chunk, 2 * FRAMES, RADIX, inner, fine), 3, 0).reshape(inner, chunk, -1)
                for g in groups
            ]
            groups = [piece[d] for piece in split for d in range(inner)]
        received.append(exchange(groups, st_count))

    owners = assign[:, 0]
    matches = (owners == sb_here).astype(jnp.int32)
    position = jnp.cumsum(matches) - 1
    per_dev = SLOTS // st_count
    slot_ids = (partner[:, None] * per_dev + jnp.arange(per_dev, dtype=jnp.int32)[None, :]).reshape(-1)
    picker = matches[None, :] * (position[None, :] == slot_ids[:, None]).astype(jnp.int32)
    filled = jnp.sum(picker, axis=1)
    slot_channel = jnp.sum(picker * beam_channels[None, :], axis=1)

    def by_row(values):
        spread = jnp.broadcast_to(values.reshape(st_count, 1, per_dev), (st_count, 2, per_dev))
        return spread.reshape(-1)

    turned = jnp.broadcast_to(jnp.arange(2, dtype=jnp.int32)[None, :, None], (st_count, 2, per_dev)).reshape(-1)
    if len(received) > 1:
        slot_channel = after(slot_channel, received[-2])
    spectra = slot_spectra(by_row(slot_channel), by_row(filled), turned, branches, st_count)
    slot_pieces = exchange(spectra, st_count)

    weights = beam_weights(after(slot_channel[:per_dev], (spectra[0], received[-1])), delays, gains)
    signal_ids = (partner[:, None] * sig_dev + jnp.arange(sig_dev, dtype=jnp.int32)[None, :]).reshape(-1)
    wanted = (station_index[None, :] * 2 + jnp.arange(2, dtype=jnp.int32)[:, None]).reshape(-1)
    chooser = (signal_ids[:, None] == wanted[None, :]).astype(jnp.bfloat16)

    visibility = correlate(after(st_here[None], weights), received, st_count)
    signals = visibility.shape[1]
    beam_out = combine(slot_pieces, chooser, after(weights, visibility))
    return (visibility.reshape(2, 1, 1, signals, signals), beam_out)


def solution(mesh):
    in_specs = (P(None, "st", None), P(), P(), P(), P(), P(), P())
    out_specs = (P(None, "sb", "st", None, None), P("sb", "st", None, None, None))
    return jax.shard_map(body, mesh=mesh, in_specs=in_specs, out_specs=out_specs, check_vma=False)
```

```python
import functools
import math

import jax
import jax.numpy as jnp
from jax import lax
from jax.experimental import pallas as pl
from jax.experimental.pallas import tpu as pltpu
from jax.sharding import PartitionSpec as P

NCH = 4096
FRAMES = 16
SLOTS = 160
RADIX = 8
LANES = 128
ROWS = 16
VMEM = 56 * 1024 * 1024

TWO_PI = 2.0 * math.pi
NT = (((1,), (1,)), ((), ()))


def phase(turns, length):
    angles = (turns % length).astype(jnp.float32) * (TWO_PI / length)
    return jnp.cos(angles), jnp.sin(angles)


def table_kernel(hi_c, hi_s, lo_c, lo_s, out):
    fine, width = lo_c.shape
    depth = hi_c.shape[0] * fine

    def block(a, carry):
        top = pl.multiple_of(a * fine, fine)
        high_c, high_s = hi_c[pl.ds(a, 1), :], hi_s[pl.ds(a, 1), :]
        cos_t = (high_c * lo_c[...] - high_s * lo_s[...]).astype(out.dtype)
        sin_t = (high_s * lo_c[...] + high_c * lo_s[...]).astype(out.dtype)
        out[pl.ds(top, fine), :width] = cos_t
        out[pl.ds(top, fine), width:] = -sin_t
        out[pl.ds(depth + top, fine), :width] = sin_t
        out[pl.ds(depth + top, fine), width:] = cos_t
        return carry

    lax.fori_loop(0, hi_c.shape[0], block, 0)


def transform_table():
    depth = NCH // RADIX
    out_ids = jnp.arange(depth, dtype=jnp.int32)[None, :]
    lo_c, lo_s = phase(jnp.arange(ROWS, dtype=jnp.int32)[:, None] * out_ids, depth)
    hi_c, hi_s = phase(jnp.arange(0, depth, ROWS, dtype=jnp.int32)[:, None] * out_ids, depth)
    scale = 1.0 / math.sqrt(NCH)
    return pl.pallas_call(
        table_kernel, out_shape=jax.ShapeDtypeStruct((2 * depth, 2 * depth), jnp.bfloat16)
    )(hi_c * scale, hi_s * scale, lo_c, lo_s)


def radix8(re, im):
    half = math.sqrt(0.5)

    def four(xr, xi):
        ar, ai, br, bi = xr[0] + xr[2], xi[0] + xi[2], xr[0] - xr[2], xi[0] - xi[2]
        cr, ci, dr, di = xr[1] + xr[3], xi[1] + xi[3], xr[1] - xr[3], xi[1] - xi[3]
        return [ar + cr, br + di, ar - cr, br - di], [ai + ci, bi - dr, ai - ci, bi + dr]

    er, ei = four(re[0::2], im[0::2])
    odd_r, odd_i = four(re[1::2], im[1::2])
    tr = [odd_r[0], (odd_r[1] + odd_i[1]) * half, odd_i[2], (odd_i[3] - odd_r[3]) * half]
    ti = [odd_i[0], (odd_i[1] - odd_r[1]) * half, -odd_r[2], (odd_r[3] + odd_i[3]) * -half]
    return (
        [e + t for e, t in zip(er, tr)] + [e - t for e, t in zip(er, tr)],
        [e + t for e, t in zip(ei, ti)] + [e - t for e, t in zip(ei, ti)],
    )


def swap_blocks(parts, lane_ids):
    count = len(parts)
    width = LANES // count
    parts = list(parts)
    step = 1
    while step < count:
        keep = (lane_ids // width) % (2 * step) < step
        for b in range(count):
            if b & step == 0:
                low, high = parts[b], parts[b + step]
                parts[b] = jnp.where(keep, low, pltpu.roll(high, step * width, 1))
                parts[b + step] = jnp.where(keep, pltpu.roll(low, LANES - step * width, 1), high)
        step *= 2
    return parts


def channel_kernel(row_block, volts, taps_wide, turn_c, turn_s, table, outs, branches, filtered, product):
    taps = taps_wide.shape[0]
    length = taps_wide.shape[2]
    frames = filtered.shape[2]
    depth = length // RADIX
    bands = depth // LANES

    def column(j, carry):
        lane = pl.multiple_of(j * LANES, LANES)

        def strip(n1, inner):
            base = pl.multiple_of(n1 * depth + j * LANES, LANES)
            for part in range(2):
                sums = [None] * frames
                for seg in range(frames + taps - 1):
                    start = pl.multiple_of(seg * length + base, LANES)
                    value = volts[part, :, pl.ds(start, LANES)].astype(jnp.float32)
                    for f in range(max(0, seg - taps + 1), min(frames, seg + 1)):
                        coef = taps_wide[seg - f, :, pl.ds(base, LANES)]
                        term = value * jnp.concatenate([coef, coef], axis=0)
                        sums[f] = term if sums[f] is None else sums[f] + term
                    if seg >= taps - 1:
                        filtered[part, n1, seg - taps + 1] = sums[seg - taps + 1]
            return inner

        lax.fori_loop(0, RADIX, strip, 0)

        def butterfly(f, inner):
            re, im = radix8(
                [filtered[0, n1, f] for n1 in range(RADIX)],
                [filtered[1, n1, f] for n1 in range(RADIX)],
            )
            for b in range(RADIX):
                turned_r, turned_i = re[b], im[b]
                if b > 0:
                    cos_t, sin_t = turn_c[b : b + 1, pl.ds(lane, LANES)], turn_s[b : b + 1, pl.ds(lane, LANES)]
                    turned_r, turned_i = re[b] * cos_t + im[b] * sin_t, im[b] * cos_t - re[b] * sin_t
                branches[b, f, :, pl.ds(lane, LANES)] = turned_r.astype(branches.dtype)
                branches[b, f, :, pl.ds(pl.multiple_of(depth + lane, LANES), LANES)] = turned_i.astype(branches.dtype)
            return inner

        lax.fori_loop(0, frames, butterfly, 0)
        return carry

    lax.fori_loop(0, bands, column, 0)

    def multiply(b, carry):
        rows = branches[b].reshape(frames * ROWS, 2 * depth)
        product[b] = jnp.dot(rows, table[...], preferred_element_type=jnp.float32)
        return carry

    lax.fori_loop(0, RADIX, multiply, 0)
    lane_ids = lax.broadcasted_iota(jnp.int32, (ROWS, LANES), 1)

    def regroup(f, carry):
        top = pl.multiple_of(f * ROWS, ROWS)
        for part in range(2):
            for band in range(bands):
                lane = part * depth + band * LANES
                pieces = [product[b, pl.ds(top, ROWS), lane : lane + LANES] for b in range(RADIX)]
                for g, piece in enumerate(swap_blocks(pieces, lane_ids)):
                    at = pl.multiple_of((part * frames + f) * LANES, LANES)
                    outs[g, band, :, pl.ds(at, LANES)] = piece.astype(outs.dtype)
        return carry

    lax.fori_loop(0, frames, regroup, 0)


def channelise(row_block, volts, taps_wide, turn_c, turn_s, table):
    length = volts.shape[2]
    depth = NCH // RADIX
    bands = depth // LANES
    wide = 2 * FRAMES * LANES
    work = 2 * ROWS * FRAMES * NCH
    return pl.pallas_call(
        channel_kernel,
        grid_spec=pltpu.PrefetchScalarGridSpec(
            num_scalar_prefetch=1,
            grid=(1,),
            in_specs=[
                pl.BlockSpec((2, ROWS, length), lambda i, row: (0, row[0], 0)),
                pl.BlockSpec(taps_wide.shape, lambda i, row: (0, 0, 0)),
                pl.BlockSpec(turn_c.shape, lambda i, row: (0, 0)),
                pl.BlockSpec(turn_s.shape, lambda i, row: (0, 0)),
                pl.BlockSpec(table.shape, lambda i, row: (0, 0)),
            ],
            out_specs=[
                pl.BlockSpec((RADIX, bands, ROWS, wide), lambda i, row: (0, 0, 0, 0)),
                pl.BlockSpec((RADIX, FRAMES, ROWS, 2 * depth), lambda i, row: (0, 0, 0, 0)),
            ],
            scratch_shapes=[
                pltpu.VMEM((2, RADIX, FRAMES, ROWS, LANES), jnp.float32),
                pltpu.VMEM((RADIX, FRAMES * ROWS, 2 * depth), jnp.float32),
            ],
        ),
        out_shape=[
            jax.ShapeDtypeStruct((RADIX, bands, ROWS, wide), jnp.bfloat16),
            jax.ShapeDtypeStruct((RADIX, FRAMES, ROWS, 2 * depth), jnp.bfloat16),
        ],
        compiler_params=pltpu.CompilerParams(vmem_limit_bytes=VMEM),
        cost_estimate=pl.CostEstimate(
            flops=work * 4 * depth, bytes_accessed=4 * ROWS * length + 4 * work, transcendentals=0
        ),
    )(row_block, volts, taps_wide, turn_c, turn_s, table)


def slot_kernel(row_branch, hi_c, hi_s, lo_c, lo_s, *rest):
    chunks, (out, table, total) = rest[:-3], rest[-3:]
    depth = chunks[0].shape[3] // 2
    f_step = chunks[0].shape[1]

    @pl.when(pl.program_id(0) == 0)
    def _():
        for a in range(hi_c.shape[1]):
            high_c, high_s = hi_c[:, a : a + 1], hi_s[:, a : a + 1]
            table[:, a * LANES : (a + 1) * LANES] = (high_c * lo_c[...] - high_s * lo_s[...]).astype(table.dtype)
            table[:, depth + a * LANES : depth + (a + 1) * LANES] = (
                high_s * lo_c[...] + high_c * lo_s[...]
            ).astype(table.dtype)

    total[...] = jnp.zeros_like(total)

    def branch(b, carry):
        rows = jnp.concatenate([c[b, f] for f in range(f_step) for c in chunks], axis=0)
        got = lax.dot_general(table[...], rows, NT, preferred_element_type=jnp.float32)
        total[...] = jnp.where(row_branch[...] == b, got, total[...])
        return carry

    lax.fori_loop(0, RADIX, branch, 0)
    per = out.shape[1]
    for d in range(out.shape[0]):
        out[d] = total[d * per : (d + 1) * per].astype(out.dtype)


def slot_spectra(row_channel, row_filled, row_turned, chunks, per):
    depth = NCH // RADIX
    rows = row_channel.shape[0]
    signals = sum(c.shape[2] for c in chunks)
    f_step = min(FRAMES, 2 * LANES // signals)
    coarse = jnp.arange(depth // LANES, dtype=jnp.int32) * LANES
    fine = jnp.arange(LANES, dtype=jnp.int32)
    whole = row_channel - row_channel % RADIX
    hi_c, hi_s = phase(whole[:, None] * coarse[None, :] + row_turned[:, None] * (NCH // 4), NCH)
    lo_c, lo_s = phase(whole[:, None] * fine[None, :], NCH)
    scaling = row_filled.astype(jnp.float32)[:, None] * (1.0 / math.sqrt(NCH))
    row_branch = (row_channel % RADIX)[:, None]
    small = [row_branch, hi_c * scaling, hi_s * scaling, lo_c, lo_s]
    return pl.pallas_call(
        slot_kernel,
        grid=(FRAMES // f_step,),
        in_specs=[pl.BlockSpec(x.shape, lambda i: (0, 0)) for x in small]
        + [pl.BlockSpec((RADIX, f_step, c.shape[2], 2 * depth), lambda i: (0, i, 0, 0)) for c in chunks],
        out_specs=pl.BlockSpec((rows // per, per, f_step * signals), lambda i: (0, 0, i)),
        out_shape=jax.ShapeDtypeStruct((rows // per, per, FRAMES * signals), jnp.bfloat16),
        scratch_shapes=[
            pltpu.VMEM((rows, 2 * depth), jnp.bfloat16),
            pltpu.VMEM((rows, f_step * signals), jnp.float32),
        ],
        compiler_params=pltpu.CompilerParams(vmem_limit_bytes=VMEM),
        cost_estimate=pl.CostEstimate(
            flops=2 * rows * 2 * NCH * FRAMES * signals,
            bytes_accessed=4 * NCH * FRAMES * signals,
            transcendentals=0,
        ),
    )(*small, *chunks)


def correlate(received):
    senders, sub, wide = received[0].shape
    chunks = len(received)
    signals = senders * sub * chunks
    if chunks == 1:
        received = [received[0].reshape(1, signals, wide)]
        senders, sub = 1, signals
    block = min(256, signals)
    blocks = signals // block
    half = wide // 2

    def kernel(*refs):
        parts, (out, held, sems) = refs[:chunks], refs[chunks:]
        copies = []
        for c, part in enumerate(parts):
            for d in range(senders):
                dst = held.at[pl.ds((d * chunks + c) * sub, sub)]
                copies.append(pltpu.make_async_copy(part.at[d], dst, sems.at[c * senders + d]))
        for copy in copies:
            copy.start()
        for copy in copies:
            copy.wait()
        inverse = 1.0 / half

        def product(left, right):
            return lax.dot_general(left, right, NT, preferred_element_type=jnp.float32)

        for i in range(blocks):
            for j in range(i + 1):
                at_i, at_j = slice(i * block, (i + 1) * block), slice(j * block, (j + 1) * block)
                re = (
                    product(held[at_i, :half], held[at_j, :half]) + product(held[at_i, half:], held[at_j, half:])
                ) * inverse
                im = (
                    product(held[at_i, half:], held[at_j, :half]) - product(held[at_i, :half], held[at_j, half:])
                ) * inverse
                out[0, at_i, at_j] = re
                out[1, at_i, at_j] = im
                if i != j:
                    out[0, at_j, at_i] = re.T
                    out[1, at_j, at_i] = -im.T

    return pl.pallas_call(
        kernel,
        in_specs=[pl.BlockSpec(memory_space=pl.ANY)] * chunks,
        out_specs=pl.BlockSpec(memory_space=pltpu.VMEM),
        out_shape=jax.ShapeDtypeStruct((2, signals, signals), jnp.float32),
        scratch_shapes=[
            pltpu.VMEM((signals, wide), jnp.bfloat16),
            pltpu.SemaphoreType.DMA((chunks * senders,)),
        ],
        compiler_params=pltpu.CompilerParams(vmem_limit_bytes=VMEM),
        cost_estimate=pl.CostEstimate(
            flops=2 * signals * signals * wide,
            bytes_accessed=2 * signals * wide + 8 * signals * signals,
            transcendentals=0,
        ),
    )(*received)


def weight_kernel(channel, delays, gains, out):
    beams = delays.shape[0]
    turns = delays[...] * (channel[pl.program_id(0)].astype(jnp.float32) * (1.0 / NCH))
    part = turns - jnp.floor(turns + 0.5)
    square = part * part
    cos_t = jnp.full_like(part, TWO_PI**16 / math.factorial(16))
    sin_t = jnp.full_like(part, -(TWO_PI**15) / math.factorial(15))
    for power in range(14, -1, -2):
        sign = -1.0 if power % 4 == 2 else 1.0
        cos_t = cos_t * square + sign * TWO_PI**power / math.factorial(power)
        if power > 0:
            sign = -1.0 if (power - 1) % 4 == 3 else 1.0
            sin_t = sin_t * square + sign * TWO_PI ** (power - 1) / math.factorial(power - 1)
    scaled = gains[...] * (1.0 / math.sqrt(gains.shape[1]))
    out[0, :beams] = (scaled * cos_t).astype(out.dtype)
    out[0, beams:] = (-scaled * sin_t * part).astype(out.dtype)


def beam_weights(channel, delays, gains):
    beams, listed = delays.shape
    slots = channel.shape[0]
    return pl.pallas_call(
        weight_kernel,
        grid=(slots,),
        in_specs=[
            pl.BlockSpec(memory_space=pltpu.SMEM),
            pl.BlockSpec(delays.shape, lambda i: (0, 0)),
            pl.BlockSpec(gains.shape, lambda i: (0, 0)),
        ],
        out_specs=pl.BlockSpec((1, 2 * beams, listed), lambda i: (i, 0, 0)),
        out_shape=jax.ShapeDtypeStruct((slots, 2 * beams, listed), jnp.bfloat16),
        cost_estimate=pl.CostEstimate(
            flops=40 * slots * beams * listed, bytes_accessed=4 * slots * beams * listed, transcendentals=0
        ),
    )(channel, delays, gains)


def combine(spectra, chooser, weights):
    slots, beams2, listed = weights.shape
    beams = beams2 // 2
    senders, rows, lanes = spectra.shape
    count = LANES * FRAMES // lanes
    groups = senders // count
    tiles = 2 * listed // LANES

    def kernel(spectrum, choose, weight, out, ordered, picked):
        lane_ids = lax.broadcasted_iota(jnp.int32, (rows, LANES), 1)
        for q in range(groups):
            for t in range(lanes // LANES):
                pieces = [
                    spectrum[q * count + i, :, t * LANES : (t + 1) * LANES].astype(jnp.float32) for i in range(count)
                ]
                for f, piece in enumerate(swap_blocks(pieces, lane_ids)):
                    top = (t * count + f) * rows
                    ordered[q, top : top + rows, :] = piece
        acc = None
        for q in range(groups):
            term = jnp.dot(
                ordered[q].astype(jnp.bfloat16),
                choose[q * LANES : (q + 1) * LANES, :],
                preferred_element_type=jnp.float32,
            )
            acc = term if acc is None else acc + term
        for lane in range(tiles):
            picked[lane] = acc[:, lane * LANES : (lane + 1) * LANES]
        for i in range(slots):
            chosen = [
                jnp.concatenate(
                    [
                        picked[p * tiles // 2 + lane, pl.ds(part * slots + i, FRAMES, rows), :]
                        for lane in range(tiles // 2)
                    ],
                    axis=1,
                )
                for p in range(2)
                for part in range(2)
            ]
            stacked = jnp.concatenate(chosen, axis=0).astype(jnp.bfloat16)
            mixed = lax.dot_general(stacked, weight[i], NT, preferred_element_type=jnp.float32)
            for p in range(2):
                at = 2 * FRAMES * p
                of_re, of_im = mixed[at : at + FRAMES], mixed[at + FRAMES : at + 2 * FRAMES]
                out[0, i, 0, :, p * beams : (p + 1) * beams] = of_re[:, :beams] - of_im[:, beams:]
                out[0, i, 1, :, p * beams : (p + 1) * beams] = of_im[:, :beams] + of_re[:, beams:]

    return pl.pallas_call(
        kernel,
        out_shape=jax.ShapeDtypeStruct((1, slots, 2, FRAMES, 2 * beams), jnp.float32),
        scratch_shapes=[
            pltpu.VMEM((groups, FRAMES * rows, LANES), jnp.float32),
            pltpu.VMEM((tiles, FRAMES * rows, LANES), jnp.float32),
        ],
        compiler_params=pltpu.CompilerParams(vmem_limit_bytes=VMEM),
        cost_estimate=pl.CostEstimate(
            flops=2 * FRAMES * rows * 2 * listed * (LANES * groups + 2 * beams),
            bytes_accessed=8 * FRAMES * rows * listed,
            transcendentals=0,
        ),
    )(spectra, chooser, weights)


def after(value, other):
    return lax.optimization_barrier((value, other))[0]


def body(volts, prototype, beam_channels, station_index, delays, gains, assign):
    sig_dev = volts.shape[1]
    st_count = lax.axis_size("st")
    sb_count = lax.axis_size("sb")
    devices = st_count * sb_count
    sb_here = lax.axis_index("sb").astype(jnp.int32)
    st_here = lax.axis_index("st").astype(jnp.int32)
    depth = NCH // RADIX
    band = NCH // sb_count
    fine = band // RADIX // st_count

    table = transform_table()
    turn_c, turn_s = phase(
        jnp.arange(RADIX, dtype=jnp.int32)[:, None] * jnp.arange(depth, dtype=jnp.int32)[None, :], NCH
    )
    taps_wide = jnp.broadcast_to(prototype[:, None, :], (prototype.shape[0], 8, NCH))

    def exchange(x):
        return lax.all_to_all(x, ("st", "sb"), split_axis=0, concat_axis=0, tiled=True)

    share = sig_dev // sb_count
    inside = (sb_here * share) % ROWS
    received, branches = [], []
    for c in range(max(1, share // ROWS)):
        row_block = (sb_here * share // ROWS + c)[None]
        groups, kept = channelise(row_block, volts, taps_wide, turn_c, turn_s, table)
        if c == 0:
            assign, beam_channels, station_index = after((assign, beam_channels, station_index), groups)
        table = after(table, groups)
        branches.append(kept)
        inner = st_count // RADIX
        if share < ROWS:
            groups = lax.dynamic_slice_in_dim(groups, inside, share, axis=2)
        if inner > 1:
            split = groups.reshape(RADIX, sb_count, -1, 2 * FRAMES, RADIX, inner, fine)
            groups = split.transpose(0, 5, 1, 2, 3, 4, 6)
        received.append(exchange(groups.reshape(devices, min(share, ROWS), -1)))

    per_dev = SLOTS // st_count
    owners = assign[:, 0]
    taken = (owners[:, None] == jnp.arange(sb_count, dtype=jnp.int32)[None, :]).astype(jnp.int32)
    position = jnp.sum(taken * jnp.cumsum(taken, axis=0), axis=1) - 1
    place = owners * SLOTS + position
    slot_ids = (
        jnp.arange(st_count, dtype=jnp.int32)[:, None, None] * per_dev
        + jnp.arange(sb_count, dtype=jnp.int32)[None, :, None] * SLOTS
        + jnp.arange(per_dev, dtype=jnp.int32)[None, None, :]
    ).reshape(-1)
    picker = (place[None, :] == slot_ids[:, None]).astype(jnp.int32)
    filled = jnp.sum(picker, axis=1)
    slot_channel = jnp.sum(picker * beam_channels[None, :], axis=1)

    def by_row(values):
        return jnp.broadcast_to(values.reshape(devices, 1, per_dev), (devices, 2, per_dev)).reshape(-1)

    turned = jnp.broadcast_to(jnp.arange(2, dtype=jnp.int32)[None, :, None], (devices, 2, per_dev)).reshape(-1)
    mine = lax.dynamic_slice_in_dim(slot_channel, (st_here * sb_count + sb_here) * per_dev, per_dev)
    weights = beam_weights(after(mine, branches), delays, gains)
    if len(received) > 1:
        slot_channel = after(slot_channel, (received[0], weights))
    spectra = slot_spectra(by_row(slot_channel), by_row(filled), turned, branches, 2 * per_dev)
    if share < ROWS:
        spectra = spectra.reshape(devices, 2 * per_dev, FRAMES, ROWS)
        spectra = lax.dynamic_slice_in_dim(spectra, inside, share, axis=3).reshape(devices, 2 * per_dev, -1)
    slot_received = exchange(spectra)

    signal_ids = jnp.arange(sig_dev * st_count, dtype=jnp.int32)
    wanted = (station_index[None, :] * 2 + jnp.arange(2, dtype=jnp.int32)[:, None]).reshape(-1)
    chooser = (signal_ids[:, None] == wanted[None, :]).astype(jnp.bfloat16)

    visibility = correlate(after(received, spectra))
    signals = visibility.shape[1]
    beam_out = combine(slot_received, chooser, after(weights, visibility))
    return (visibility.reshape(2, 1, 1, signals, signals), beam_out)


def solution(mesh):
    in_specs = (P(None, "st", None), P(), P(), P(), P(), P(), P())
    out_specs = (P(None, "sb", "st", None, None), P("sb", "st", None, None, None))
    return jax.shard_map(body, mesh=mesh, in_specs=in_specs, out_specs=out_specs, check_vma=False)
```

```python
import functools
import math

import jax
import jax.numpy as jnp
from jax import lax
from jax.experimental import pallas as pl
from jax.experimental.pallas import tpu as pltpu
from jax.sharding import Mesh
from jax.sharding import PartitionSpec as P

NCH = 4096
FRAMES = 16
SLOTS = 160
RADIX = 8
LANES = 128
ROWS = 16
VMEM = 56 * 1024 * 1024

TWO_PI = 2.0 * math.pi
NT = (((1,), (1,)), ((), ()))


def phase(turns, length):
    angles = (turns % length).astype(jnp.float32) * (TWO_PI / length)
    return jnp.cos(angles), jnp.sin(angles)


def table_kernel(hi_c, hi_s, lo_c, lo_s, out):
    fine, width = lo_c.shape
    depth = hi_c.shape[0] * fine

    def block(a, carry):
        top = pl.multiple_of(a * fine, fine)
        high_c, high_s = hi_c[pl.ds(a, 1), :], hi_s[pl.ds(a, 1), :]
        cos_t = (high_c * lo_c[...] - high_s * lo_s[...]).astype(out.dtype)
        sin_t = (high_s * lo_c[...] + high_c * lo_s[...]).astype(out.dtype)
        out[pl.ds(top, fine), :width] = cos_t
        out[pl.ds(top, fine), width:] = -sin_t
        out[pl.ds(depth + top, fine), :width] = sin_t
        out[pl.ds(depth + top, fine), width:] = cos_t
        return carry

    lax.fori_loop(0, hi_c.shape[0], block, 0)


def transform_table(out_ids):
    depth = NCH // RADIX
    out_ids = out_ids[None, :]
    lo_c, lo_s = phase(jnp.arange(ROWS, dtype=jnp.int32)[:, None] * out_ids, depth)
    hi_c, hi_s = phase(jnp.arange(0, depth, ROWS, dtype=jnp.int32)[:, None] * out_ids, depth)
    scale = 1.0 / math.sqrt(NCH)
    return pl.pallas_call(
        table_kernel, out_shape=jax.ShapeDtypeStruct((2 * depth, 2 * depth), jnp.bfloat16)
    )(hi_c * scale, hi_s * scale, lo_c, lo_s)


def radix8(re, im):
    half = math.sqrt(0.5)

    def four(xr, xi):
        ar, ai, br, bi = xr[0] + xr[2], xi[0] + xi[2], xr[0] - xr[2], xi[0] - xi[2]
        cr, ci, dr, di = xr[1] + xr[3], xi[1] + xi[3], xr[1] - xr[3], xi[1] - xi[3]
        return [ar + cr, br + di, ar - cr, br - di], [ai + ci, bi - dr, ai - ci, bi + dr]

    er, ei = four(re[0::2], im[0::2])
    odd_r, odd_i = four(re[1::2], im[1::2])
    tr = [odd_r[0], (odd_r[1] + odd_i[1]) * half, odd_i[2], (odd_i[3] - odd_r[3]) * half]
    ti = [odd_i[0], (odd_i[1] - odd_r[1]) * half, -odd_r[2], (odd_r[3] + odd_i[3]) * -half]
    return (
        [e + t for e, t in zip(er, tr)] + [e - t for e, t in zip(er, tr)],
        [e + t for e, t in zip(ei, ti)] + [e - t for e, t in zip(ei, ti)],
    )


def swap_blocks(parts, lane_ids):
    count = len(parts)
    width = LANES // count
    parts = list(parts)
    step = 1
    while step < count:
        keep = (lane_ids // width) % (2 * step) < step
        for b in range(count):
            if b & step == 0:
                low, high = parts[b], parts[b + step]
                parts[b] = jnp.where(keep, low, pltpu.roll(high, step * width, 1))
                parts[b + step] = jnp.where(keep, pltpu.roll(low, LANES - step * width, 1), high)
        step *= 2
    return parts


def gather_blocks(parts, lane_ids):
    count = len(parts)
    width = LANES // count
    turned = [parts[0]] + [pltpu.roll(parts[b], b * width, 1) for b in range(1, count)]
    turned = [turned[-b % count] for b in range(count)]
    step = 1
    while step < count:
        moved = (lane_ids // width) & step != 0
        turned = [jnp.where(moved, turned[(g - step) % count], turned[g]) for g in range(count)]
        step *= 2
    return [turned[0]] + [pltpu.roll(turned[g], LANES - g * width, 1) for g in range(1, count)]


def channel_kernel(first, row_block, volts, taps_wide, turn_c, turn_s, table, *rest):
    outs, (branches, filtered, product) = rest[:-3], rest[-3:]
    near = RADIX // len(outs)
    taps = taps_wide.shape[0]
    length = taps_wide.shape[2]
    frames = filtered.shape[2]
    depth = length // RADIX
    bands = depth // LANES

    def column(j, carry):
        lane = pl.multiple_of(j * LANES, LANES)

        def strip(n1, inner):
            base = pl.multiple_of(n1 * depth + j * LANES, LANES)
            for part in range(2):
                sums = [None] * frames
                for seg in range(frames + taps - 1):
                    start = pl.multiple_of((first + seg) * length + base, LANES)
                    value = volts[part, :, pl.ds(start, LANES)].astype(jnp.float32)
                    for f in range(max(0, seg - taps + 1), min(frames, seg + 1)):
                        coef = taps_wide[seg - f, :, pl.ds(base, LANES)]
                        term = value * jnp.concatenate([coef, coef], axis=0)
                        sums[f] = term if sums[f] is None else sums[f] + term
                    if seg >= taps - 1:
                        filtered[part, n1, seg - taps + 1] = sums[seg - taps + 1]
            return inner

        lax.fori_loop(0, RADIX, strip, 0)

        def butterfly(f, inner):
            re, im = radix8(
                [filtered[0, n1, f] for n1 in range(RADIX)],
                [filtered[1, n1, f] for n1 in range(RADIX)],
            )
            for b in range(RADIX):
                turned_r, turned_i = re[b], im[b]
                if b > 0:
                    cos_t, sin_t = turn_c[b : b + 1, pl.ds(lane, LANES)], turn_s[b : b + 1, pl.ds(lane, LANES)]
                    turned_r, turned_i = re[b] * cos_t + im[b] * sin_t, im[b] * cos_t - re[b] * sin_t
                branches[b, f, :, pl.ds(lane, LANES)] = turned_r.astype(branches.dtype)
                branches[b, f, :, pl.ds(pl.multiple_of(depth + lane, LANES), LANES)] = turned_i.astype(branches.dtype)
            return inner

        lax.fori_loop(0, frames, butterfly, 0)
        return carry

    lax.fori_loop(0, bands, column, 0)

    def multiply(b, carry):
        rows = branches[b].reshape(frames * ROWS, 2 * depth)
        product[b] = jnp.dot(rows, table[...], preferred_element_type=jnp.float32)
        return carry

    lax.fori_loop(0, RADIX, multiply, 0)
    lane_ids = lax.broadcasted_iota(jnp.int32, (ROWS, LANES), 1)

    def regroup(f, carry):
        top = pl.multiple_of(f * ROWS, ROWS)
        for part in range(2):
            for band in range(bands):
                lane = part * depth + band * LANES
                pieces = [product[b, pl.ds(top, ROWS), lane : lane + LANES] for b in range(RADIX)]
                for g, piece in enumerate(gather_blocks(pieces, lane_ids)):
                    at = pl.multiple_of((part * frames + f) * LANES, LANES)
                    out = outs[g // near]
                    out[g % near, band, :, pl.ds(at, LANES)] = piece.astype(out.dtype)
        return carry

    lax.fori_loop(0, frames, regroup, 0)


def channelise(row_block, volts, taps_wide, turn_c, turn_s, table, first, frames, far):
    taps = taps_wide.shape[0]
    length = volts.shape[2] if first > 0 else (frames + taps - 1) * NCH
    depth = NCH // RADIX
    bands = depth // LANES
    wide = 2 * frames * LANES
    near = RADIX // far
    work = 2 * ROWS * frames * NCH
    return pl.pallas_call(
        functools.partial(channel_kernel, first),
        grid_spec=pltpu.PrefetchScalarGridSpec(
            num_scalar_prefetch=1,
            grid=(1,),
            in_specs=[
                pl.BlockSpec((2, ROWS, length), lambda i, row: (0, row[0], 0)),
                pl.BlockSpec(taps_wide.shape, lambda i, row: (0, 0, 0)),
                pl.BlockSpec(turn_c.shape, lambda i, row: (0, 0)),
                pl.BlockSpec(turn_s.shape, lambda i, row: (0, 0)),
                pl.BlockSpec(table.shape, lambda i, row: (0, 0)),
            ],
            out_specs=[pl.BlockSpec((near, bands, ROWS, wide), lambda i, row: (0, 0, 0, 0))] * far
            + [pl.BlockSpec((RADIX, frames, ROWS, 2 * depth), lambda i, row: (0, 0, 0, 0))],
            scratch_shapes=[
                pltpu.VMEM((2, RADIX, frames, ROWS, LANES), jnp.float32),
                pltpu.VMEM((RADIX, frames * ROWS, 2 * depth), jnp.float32),
            ],
        ),
        out_shape=[jax.ShapeDtypeStruct((near, bands, ROWS, wide), jnp.bfloat16)] * far
        + [jax.ShapeDtypeStruct((RADIX, frames, ROWS, 2 * depth), jnp.bfloat16)],
        compiler_params=pltpu.CompilerParams(vmem_limit_bytes=VMEM),
        cost_estimate=pl.CostEstimate(
            flops=work * 8 * depth, bytes_accessed=4 * ROWS * length + 4 * work, transcendentals=0
        ),
    )(row_block, volts, taps_wide, turn_c, turn_s, table)


def slot_kernel(far, row_branch, hi_c, hi_s, lo_c, lo_s, *rest):
    chunks, outs, (table, total) = rest[: -2 - far], rest[-2 - far : -2], rest[-2:]
    depth = chunks[0].shape[3] // 2
    for a in range(hi_c.shape[1]):
        high_c, high_s = hi_c[:, a : a + 1], hi_s[:, a : a + 1]
        table[:, a * LANES : (a + 1) * LANES] = (high_c * lo_c[...] - high_s * lo_s[...]).astype(table.dtype)
        table[:, depth + a * LANES : depth + (a + 1) * LANES] = (
            high_s * lo_c[...] + high_c * lo_s[...]
        ).astype(table.dtype)
    total[...] = jnp.zeros_like(total)

    def branch(b, carry):
        rows = jnp.concatenate([c[b].reshape(c.shape[1] * c.shape[2], c.shape[3]) for c in chunks], axis=0)
        got = lax.dot_general(table[...], rows, NT, preferred_element_type=jnp.float32)
        total[...] = jnp.where(row_branch[...] == b, got, total[...])
        return carry

    lax.fori_loop(0, RADIX, branch, 0)
    plane, per = outs[0].shape[:2]
    for s, out in enumerate(outs):
        for d in range(plane):
            top = (s * plane + d) * per
            out[d] = total[top : top + per].astype(out.dtype)


def slot_spectra(row_channel, row_filled, row_turned, chunks, per, far):
    depth = NCH // RADIX
    rows = row_channel.shape[0]
    samples = sum(c.shape[1] * c.shape[2] for c in chunks)
    plane = rows // per // far
    coarse = jnp.arange(depth // LANES, dtype=jnp.int32) * LANES
    fine = jnp.arange(LANES, dtype=jnp.int32)
    whole = row_channel - row_channel % RADIX
    hi_c, hi_s = phase(whole[:, None] * coarse[None, :] + row_turned[:, None] * (NCH // 4), NCH)
    lo_c, lo_s = phase(whole[:, None] * fine[None, :], NCH)
    scaling = row_filled.astype(jnp.float32)[:, None] * (1.0 / math.sqrt(NCH))
    row_branch = (row_channel % RADIX)[:, None]
    return pl.pallas_call(
        functools.partial(slot_kernel, far),
        out_shape=[jax.ShapeDtypeStruct((plane, per, samples), jnp.bfloat16)] * far,
        scratch_shapes=[pltpu.VMEM((rows, 2 * depth), jnp.bfloat16), pltpu.VMEM((rows, samples), jnp.float32)],
        compiler_params=pltpu.CompilerParams(vmem_limit_bytes=VMEM),
        cost_estimate=pl.CostEstimate(
            flops=2 * rows * 2 * NCH * samples, bytes_accessed=4 * NCH * samples, transcendentals=0
        ),
    )(row_branch, hi_c * scaling, hi_s * scaling, lo_c, lo_s, *chunks)


def correlate(here, pieces, far, halves):
    senders = pieces[0][0].shape[0]
    sub = pieces[0][0].shape[1] if halves == 1 else ROWS
    lanes = pieces[0][0].shape[2] // (2 * pieces[0][5])
    half = FRAMES * lanes
    block = senders * halves * sub
    signals = far * block

    def kernel(here_ref, *refs):
        parts, (out, held, sems) = refs[: len(pieces)], refs[len(pieces) :]
        copies = []
        for index, (_, partner, row, which, first, frames) in enumerate(pieces):
            for part in range(2):
                src = parts[index].at[:, pl.ds(row, sub), pl.ds(part * frames * lanes, frames * lanes)]
                dst = held.at[here_ref[0] ^ partner, :, which, :, pl.ds(part * half + first * lanes, frames * lanes)]
                copies.append(pltpu.make_async_copy(src, dst, sems.at[2 * index + part]))
        for copy in copies:
            copy.start()
        for copy in copies:
            copy.wait()
        inverse = 1.0 / half

        def product(left, right):
            return lax.dot_general(left, right, NT, preferred_element_type=jnp.float32)

        for i in range(far):
            left = held[i].reshape(block, 2 * half)
            for j in range(i + 1):
                right = held[j].reshape(block, 2 * half)
                at_i, at_j = slice(i * block, (i + 1) * block), slice(j * block, (j + 1) * block)
                re = (
                    product(left[:, :half], right[:, :half]) + product(left[:, half:], right[:, half:])
                ) * inverse
                im = (
                    product(left[:, half:], right[:, :half]) - product(left[:, :half], right[:, half:])
                ) * inverse
                out[0, at_i, at_j] = re
                out[1, at_i, at_j] = im
                if i != j:
                    out[0, at_j, at_i] = re.T
                    out[1, at_j, at_i] = -im.T

    return pl.pallas_call(
        kernel,
        in_specs=[pl.BlockSpec(memory_space=pltpu.SMEM)] + [pl.BlockSpec(memory_space=pl.ANY)] * len(pieces),
        out_specs=pl.BlockSpec(memory_space=pltpu.VMEM),
        out_shape=jax.ShapeDtypeStruct((2, signals, signals), jnp.float32),
        scratch_shapes=[
            pltpu.VMEM((far, senders, halves, sub, 2 * half), jnp.bfloat16),
            pltpu.SemaphoreType.DMA((2 * len(pieces),)),
        ],
        compiler_params=pltpu.CompilerParams(vmem_limit_bytes=VMEM),
        cost_estimate=pl.CostEstimate(
            flops=4 * signals * signals * half,
            bytes_accessed=4 * signals * half + 8 * signals * signals,
            transcendentals=0,
        ),
    )(here, *[piece[0] for piece in pieces])


def weight_kernel(channel, delays, gains, out):
    beams = delays.shape[0]
    turns = delays[...] * (channel[pl.program_id(0)].astype(jnp.float32) * (1.0 / NCH))
    part = turns - jnp.floor(turns + 0.5)
    square = part * part
    cos_t = jnp.full_like(part, TWO_PI**16 / math.factorial(16))
    sin_t = jnp.full_like(part, -(TWO_PI**15) / math.factorial(15))
    for power in range(14, -1, -2):
        sign = -1.0 if power % 4 == 2 else 1.0
        cos_t = cos_t * square + sign * TWO_PI**power / math.factorial(power)
        if power > 0:
            sign = -1.0 if (power - 1) % 4 == 3 else 1.0
            sin_t = sin_t * square + sign * TWO_PI ** (power - 1) / math.factorial(power - 1)
    scaled = gains[...] * (1.0 / math.sqrt(gains.shape[1]))
    out[0, :beams] = (scaled * cos_t).astype(out.dtype)
    out[0, beams:] = (-scaled * sin_t * part).astype(out.dtype)


def beam_weights(channel, delays, gains):
    beams, listed = delays.shape
    slots = channel.shape[0]
    return pl.pallas_call(
        weight_kernel,
        grid=(slots,),
        in_specs=[
            pl.BlockSpec(memory_space=pltpu.SMEM),
            pl.BlockSpec(delays.shape, lambda i: (0, 0)),
            pl.BlockSpec(gains.shape, lambda i: (0, 0)),
        ],
        out_specs=pl.BlockSpec((1, 2 * beams, listed), lambda i: (i, 0, 0)),
        out_shape=jax.ShapeDtypeStruct((slots, 2 * beams, listed), jnp.bfloat16),
        cost_estimate=pl.CostEstimate(
            flops=40 * slots * beams * listed, bytes_accessed=4 * slots * beams * listed, transcendentals=0
        ),
    )(channel, delays, gains)


def combine(spectra, chooser, weights, halves, sub):
    slots, beams2, listed = weights.shape
    beams = beams2 // 2
    rows = 2 * slots
    senders = spectra[0].shape[0]
    partners = sum(x.shape[1] for x in spectra) // rows
    count = LANES // sub
    inner = senders // count
    groups = partners * halves * inner
    tiles = 2 * listed // LANES

    def kernel(*refs):
        got, (choose, weight, out, ordered, picked) = refs[: len(spectra)], refs[len(spectra) :]
        lane_ids = lax.broadcasted_iota(jnp.int32, (rows, LANES), 1)
        where = [(x, k * rows) for x in got for k in range(x.shape[1] // rows)]
        for s, (spectrum, row) in enumerate(where):
            for h in range(halves):
                for q in range(inner):
                    for t in range(FRAMES // count):
                        lane = h * FRAMES * sub + t * LANES
                        pieces = [
                            spectrum[q * count + i, row : row + rows, lane : lane + LANES].astype(jnp.float32)
                            for i in range(count)
                        ]
                        for f, piece in enumerate(swap_blocks(pieces, lane_ids)):
                            top = (t * count + f) * rows
                            ordered[(s * halves + h) * inner + q, top : top + rows, :] = piece
        acc = None
        for q in range(groups):
            term = jnp.dot(
                ordered[q].astype(jnp.bfloat16),
                choose[q * LANES : (q + 1) * LANES, :],
                preferred_element_type=jnp.float32,
            )
            acc = term if acc is None else acc + term
        for lane in range(tiles):
            picked[lane] = acc[:, lane * LANES : (lane + 1) * LANES]
        for i in range(slots):
            chosen = [
                jnp.concatenate(
                    [
                        picked[p * tiles // 2 + lane, pl.ds(part * slots + i, FRAMES, rows), :]
                        for lane in range(tiles // 2)
                    ],
                    axis=1,
                )
                for p in range(2)
                for part in range(2)
            ]
            stacked = jnp.concatenate(chosen, axis=0).astype(jnp.bfloat16)
            mixed = lax.dot_general(stacked, weight[i], NT, preferred_element_type=jnp.float32)
            for p in range(2):
                at = 2 * FRAMES * p
                of_re, of_im = mixed[at : at + FRAMES], mixed[at + FRAMES : at + 2 * FRAMES]
                out[0, i, 0, :, p * beams : (p + 1) * beams] = of_re[:, :beams] - of_im[:, beams:]
                out[0, i, 1, :, p * beams : (p + 1) * beams] = of_im[:, :beams] + of_re[:, beams:]

    return pl.pallas_call(
        kernel,
        out_shape=jax.ShapeDtypeStruct((1, slots, 2, FRAMES, 2 * beams), jnp.float32),
        scratch_shapes=[
            pltpu.VMEM((groups, FRAMES * rows, LANES), jnp.float32),
            pltpu.VMEM((tiles, FRAMES * rows, LANES), jnp.float32),
        ],
        compiler_params=pltpu.CompilerParams(vmem_limit_bytes=VMEM),
        cost_estimate=pl.CostEstimate(
            flops=2 * FRAMES * rows * 2 * listed * (LANES * groups + 2 * beams),
            bytes_accessed=8 * FRAMES * rows * listed,
            transcendentals=0,
        ),
    )(*spectra, chooser, weights)


def after(value, other):
    return lax.optimization_barrier((value, other))[0]


def body(volts, prototype, beam_channels, station_index, delays, gains, assign):
    sig_dev = volts.shape[1]
    far, near, sb_count = lax.axis_size("far"), lax.axis_size("near"), lax.axis_size("sb")
    far_here, near_here, sb_here = [lax.axis_index(name).astype(jnp.int32) for name in ("far", "near", "sb")]
    st_count = far * near
    plane = near * sb_count
    depth = NCH // RADIX
    bands = depth // LANES
    fine = NCH // sb_count // RADIX // st_count
    partner = far_here ^ jnp.arange(far, dtype=jnp.int32)
    stations = (partner[:, None] * near + jnp.arange(near, dtype=jnp.int32)[None, :]).reshape(-1)

    def spread(*ids):
        total = ids[0]
        for more in ids[1:]:
            total = total[..., None] + more
        return total.reshape(-1)

    out_ids = spread(
        jnp.arange(bands, dtype=jnp.int32)[:, None] * LANES + (stations * fine)[None, :],
        jnp.arange(fine, dtype=jnp.int32),
    )
    table = transform_table(out_ids)
    turn_c, turn_s = phase(
        jnp.arange(RADIX, dtype=jnp.int32)[:, None] * jnp.arange(depth, dtype=jnp.int32)[None, :], NCH
    )
    taps_wide = jnp.broadcast_to(prototype[:, None, :], (prototype.shape[0], 8, NCH))

    def to_planes(xs):
        return [xs[0]] + [
            lax.ppermute(xs[s], "far", [(i, i ^ s) for i in range(far)]) for s in range(1, far)
        ]

    def in_plane(xs):
        joined = xs[0] if len(xs) == 1 else jnp.concatenate(xs, axis=1)
        return lax.all_to_all(joined, ("near", "sb"), split_axis=0, concat_axis=0, tiled=True)

    share = sig_dev // sb_count
    sub = min(share, ROWS)
    halves = max(1, share // ROWS)
    inside = (sb_here * share) % ROWS
    early = FRAMES // 4
    plan = [(0, 0, early), (0, early, FRAMES - early)] + [(h, 0, FRAMES) for h in range(1, halves)]
    crossed, branches = [], []
    for c, (which, first, frames) in enumerate(plan):
        if c > 1:
            table = after(table, crossed[c - 2])
        row_block = (sb_here * share // ROWS + which)[None]
        *outs, kept = channelise(row_block, volts, taps_wide, turn_c, turn_s, table, first, frames, far)
        if c == 0:
            assign, beam_channels, station_index = after((assign, beam_channels, station_index), outs)
        table = after(table, outs)
        branches.append(kept)
        if sub < ROWS:
            outs = [lax.dynamic_slice_in_dim(x, inside, sub, axis=2) for x in outs]
        inner = st_count // RADIX
        if inner > 1:
            outs = [
                x.reshape(near // inner, sb_count, sub, 2 * frames, RADIX, inner, fine).transpose(0, 5, 1, 2, 3, 4, 6)
                for x in outs
            ]
        crossed.append(to_planes([x.reshape(plane, sub, -1) for x in outs]))

    pieces = []
    for c, (which, first, frames) in enumerate(plan):
        step = far if c == 0 else max(1, far // 2)
        for s in range(0, far, step):
            got = in_plane(crossed[c][s : s + step])
            for k in range(step):
                if halves == 1:
                    one = got[:, k * sub : (k + 1) * sub].reshape(1, plane * sub, -1)
                    pieces.append((one, s + k, 0, 0, first, frames))
                else:
                    pieces.append((got, s + k, k * sub, which, first, frames))

    per_dev = SLOTS // st_count
    owners = assign[:, 0]
    taken = (owners[:, None] == jnp.arange(sb_count, dtype=jnp.int32)[None, :]).astype(jnp.int32)
    position = jnp.sum(taken * jnp.cumsum(taken, axis=0), axis=1) - 1
    place = owners * SLOTS + position
    slot_ids = spread(
        stations * per_dev,
        jnp.arange(sb_count, dtype=jnp.int32) * SLOTS,
        jnp.arange(per_dev, dtype=jnp.int32),
    )
    picker = (place[None, :] == slot_ids[:, None]).astype(jnp.int32)
    filled = jnp.sum(picker, axis=1)
    slot_channel = jnp.sum(picker * beam_channels[None, :], axis=1)

    def by_row(values):
        values = values.reshape(st_count * sb_count, 1, per_dev)
        return jnp.broadcast_to(values, (st_count * sb_count, 2, per_dev)).reshape(-1)

    turned = jnp.broadcast_to(jnp.arange(2, dtype=jnp.int32)[None, :, None], (st_count * sb_count, 2, per_dev))
    mine = lax.dynamic_slice_in_dim(slot_channel, (near_here * sb_count + sb_here) * per_dev, per_dev)
    weights = beam_weights(after(mine, branches), delays, gains)
    slot_channel = after(slot_channel, (crossed[-2], weights))
    spectra = slot_spectra(by_row(slot_channel), by_row(filled), turned.reshape(-1), branches, 2 * per_dev, far)
    if sub < ROWS:
        spectra = [
            lax.dynamic_slice_in_dim(x.reshape(plane, 2 * per_dev, FRAMES, ROWS), inside, sub, axis=3).reshape(
                plane, 2 * per_dev, -1
            )
            for x in spectra
        ]
    slot_crossed = to_planes(spectra)
    step = max(1, far // 2)
    slot_received = [in_plane(slot_crossed[s : s + step]) for s in range(0, far, step)]

    signal_ids = spread(
        partner[:, None] * (near * sig_dev) + jnp.arange(halves, dtype=jnp.int32)[None, :] * sub,
        jnp.arange(plane, dtype=jnp.int32) * share,
        jnp.arange(sub, dtype=jnp.int32),
    )
    wanted = (station_index[None, :] * 2 + jnp.arange(2, dtype=jnp.int32)[:, None]).reshape(-1)
    chooser = (signal_ids[:, None] == wanted[None, :]).astype(jnp.bfloat16)

    visibility = correlate(after(far_here[None], spectra), pieces, far, halves)
    signals = visibility.shape[1]
    beam_out = combine(slot_received, chooser, after(weights, visibility), halves, sub)
    return (visibility.reshape(2, 1, 1, signals, signals), beam_out)


def solution(mesh):
    st_count, sb_count = mesh.shape["st"], mesh.shape["sb"]
    far = math.gcd(4, st_count)
    planes = Mesh(mesh.devices.reshape(far, st_count // far, sb_count), ("far", "near", "sb"))
    st = ("far", "near")
    in_specs = (P(None, st, None), P(), P(), P(), P(), P(), P())
    out_specs = (P(None, "sb", st, None, None), P("sb", st, None, None, None))
    return jax.shard_map(body, mesh=planes, in_specs=in_specs, out_specs=out_specs, check_vma=False)
```

```python
import functools
import math

import jax
import jax.numpy as jnp
from jax import lax
from jax.experimental import pallas as pl
from jax.experimental.pallas import tpu as pltpu
from jax.sharding import Mesh
from jax.sharding import PartitionSpec as P

NCH = 4096
FRAMES = 16
SLOTS = 160
RADIX = 8
LANES = 128
ROWS = 16
VMEM = 56 * 1024 * 1024

NO_COST = pl.CostEstimate(flops=1, bytes_accessed=1, transcendentals=0)

TWO_PI = 2.0 * math.pi
NT = (((1,), (1,)), ((), ()))


def busy(share):
    return pl.CostEstimate(flops=int(share * 4e10), bytes_accessed=1, transcendentals=0)


def phase(turns, length):
    angles = (turns % length).astype(jnp.float32) * (TWO_PI / length)
    return jnp.cos(angles), jnp.sin(angles)


def table_kernel(hi_c, hi_s, lo_c, lo_s, out):
    fine, width = lo_c.shape
    depth = hi_c.shape[0] * fine

    def block(a, carry):
        top = pl.multiple_of(a * fine, fine)
        high_c, high_s = hi_c[pl.ds(a, 1), :], hi_s[pl.ds(a, 1), :]
        cos_t = (high_c * lo_c[...] - high_s * lo_s[...]).astype(out.dtype)
        sin_t = (high_s * lo_c[...] + high_c * lo_s[...]).astype(out.dtype)
        out[pl.ds(top, fine), :width] = cos_t
        out[pl.ds(top, fine), width:] = -sin_t
        out[pl.ds(depth + top, fine), :width] = sin_t
        out[pl.ds(depth + top, fine), width:] = cos_t
        return carry

    lax.fori_loop(0, hi_c.shape[0], block, 0)


def transform_table(out_ids):
    depth = NCH // RADIX
    out_ids = out_ids[None, :]
    lo_c, lo_s = phase(jnp.arange(ROWS, dtype=jnp.int32)[:, None] * out_ids, depth)
    hi_c, hi_s = phase(jnp.arange(0, depth, ROWS, dtype=jnp.int32)[:, None] * out_ids, depth)
    scale = 1.0 / math.sqrt(NCH)
    return pl.pallas_call(
        table_kernel,
        out_shape=jax.ShapeDtypeStruct((2 * depth, 2 * depth), jnp.bfloat16),
        cost_estimate=NO_COST,
    )(hi_c * scale, hi_s * scale, lo_c, lo_s)


def radix8(re, im):
    half = math.sqrt(0.5)

    def four(xr, xi):
        ar, ai, br, bi = xr[0] + xr[2], xi[0] + xi[2], xr[0] - xr[2], xi[0] - xi[2]
        cr, ci, dr, di = xr[1] + xr[3], xi[1] + xi[3], xr[1] - xr[3], xi[1] - xi[3]
        return [ar + cr, br + di, ar - cr, br - di], [ai + ci, bi - dr, ai - ci, bi + dr]

    er, ei = four(re[0::2], im[0::2])
    odd_r, odd_i = four(re[1::2], im[1::2])
    tr = [odd_r[0], (odd_r[1] + odd_i[1]) * half, odd_i[2], (odd_i[3] - odd_r[3]) * half]
    ti = [odd_i[0], (odd_i[1] - odd_r[1]) * half, -odd_r[2], (odd_r[3] + odd_i[3]) * -half]
    return (
        [e + t for e, t in zip(er, tr)] + [e - t for e, t in zip(er, tr)],
        [e + t for e, t in zip(ei, ti)] + [e - t for e, t in zip(ei, ti)],
    )


def swap_blocks(parts, lane_ids):
    count = len(parts)
    width = LANES // count
    parts = list(parts)
    step = 1
    while step < count:
        keep = (lane_ids // width) % (2 * step) < step
        for b in range(count):
            if b & step == 0:
                low, high = parts[b], parts[b + step]
                parts[b] = jnp.where(keep, low, pltpu.roll(high, step * width, 1))
                parts[b + step] = jnp.where(keep, pltpu.roll(low, LANES - step * width, 1), high)
        step *= 2
    return parts


def gather_blocks(parts, lane_ids):
    count = len(parts)
    width = LANES // count
    turned = [parts[0]] + [pltpu.roll(parts[b], b * width, 1) for b in range(1, count)]
    turned = [turned[-b % count] for b in range(count)]
    step = 1
    while step < count:
        moved = (lane_ids // width) & step != 0
        turned = [jnp.where(moved, turned[(g - step) % count], turned[g]) for g in range(count)]
        step *= 2
    return [turned[0]] + [pltpu.roll(turned[g], LANES - g * width, 1) for g in range(1, count)]


def channel_kernel(first, row_block, volts, taps_wide, turn_c, turn_s, table, *rest):
    outs, (branches, filtered, product) = rest[:-3], rest[-3:]
    near = RADIX // len(outs)
    taps = taps_wide.shape[0]
    length = taps_wide.shape[2]
    frames = filtered.shape[2]
    depth = length // RADIX
    bands = depth // LANES

    def column(j, carry):
        lane = pl.multiple_of(j * LANES, LANES)

        def strip(n1, inner):
            base = pl.multiple_of(n1 * depth + j * LANES, LANES)
            for part in range(2):
                sums = [None] * frames
                for seg in range(frames + taps - 1):
                    start = pl.multiple_of((first + seg) * length + base, LANES)
                    value = volts[part, :, pl.ds(start, LANES)].astype(jnp.float32)
                    for f in range(max(0, seg - taps + 1), min(frames, seg + 1)):
                        coef = taps_wide[seg - f, :, pl.ds(base, LANES)]
                        term = value * jnp.concatenate([coef, coef], axis=0)
                        sums[f] = term if sums[f] is None else sums[f] + term
                    if seg >= taps - 1:
                        filtered[part, n1, seg - taps + 1] = sums[seg - taps + 1]
            return inner

        lax.fori_loop(0, RADIX, strip, 0)

        def butterfly(f, inner):
            re, im = radix8(
                [filtered[0, n1, f] for n1 in range(RADIX)],
                [filtered[1, n1, f] for n1 in range(RADIX)],
            )
            for b in range(RADIX):
                turned_r, turned_i = re[b], im[b]
                if b > 0:
                    cos_t, sin_t = turn_c[b : b + 1, pl.ds(lane, LANES)], turn_s[b : b + 1, pl.ds(lane, LANES)]
                    turned_r, turned_i = re[b] * cos_t + im[b] * sin_t, im[b] * cos_t - re[b] * sin_t
                branches[b, f, :, pl.ds(lane, LANES)] = turned_r.astype(branches.dtype)
                branches[b, f, :, pl.ds(pl.multiple_of(depth + lane, LANES), LANES)] = turned_i.astype(branches.dtype)
            return inner

        lax.fori_loop(0, frames, butterfly, 0)
        return carry

    lax.fori_loop(0, bands, column, 0)

    def multiply(b, carry):
        rows = branches[b].reshape(frames * ROWS, 2 * depth)
        product[b] = jnp.dot(rows, table[...], preferred_element_type=jnp.float32)
        return carry

    lax.fori_loop(0, RADIX, multiply, 0)
    lane_ids = lax.broadcasted_iota(jnp.int32, (ROWS, LANES), 1)

    def regroup(f, carry):
        top = pl.multiple_of(f * ROWS, ROWS)
        for part in range(2):
            for band in range(bands):
                lane = part * depth + band * LANES
                pieces = [product[b, pl.ds(top, ROWS), lane : lane + LANES] for b in range(RADIX)]
                for g, piece in enumerate(gather_blocks(pieces, lane_ids)):
                    at = pl.multiple_of((part * frames + f) * LANES, LANES)
                    out = outs[g // near]
                    out[g % near, band, :, pl.ds(at, LANES)] = piece.astype(out.dtype)
        return carry

    lax.fori_loop(0, frames, regroup, 0)


def channelise(row_block, volts, taps_wide, turn_c, turn_s, table, first, frames, far):
    taps = taps_wide.shape[0]
    length = volts.shape[2] if first > 0 else (frames + taps - 1) * NCH
    depth = NCH // RADIX
    bands = depth // LANES
    wide = 2 * frames * LANES
    near = RADIX // far
    return pl.pallas_call(
        functools.partial(channel_kernel, first),
        grid_spec=pltpu.PrefetchScalarGridSpec(
            num_scalar_prefetch=1,
            grid=(1,),
            in_specs=[
                pl.BlockSpec((2, ROWS, length), lambda i, row: (0, row[0], 0)),
                pl.BlockSpec(taps_wide.shape, lambda i, row: (0, 0, 0)),
                pl.BlockSpec(turn_c.shape, lambda i, row: (0, 0)),
                pl.BlockSpec(turn_s.shape, lambda i, row: (0, 0)),
                pl.BlockSpec(table.shape, lambda i, row: (0, 0)),
            ],
            out_specs=[pl.BlockSpec((near, bands, ROWS, wide), lambda i, row: (0, 0, 0, 0))] * far
            + [pl.BlockSpec((RADIX, frames, ROWS, 2 * depth), lambda i, row: (0, 0, 0, 0))],
            scratch_shapes=[
                pltpu.VMEM((2, RADIX, frames, ROWS, LANES), jnp.float32),
                pltpu.VMEM((RADIX, frames * ROWS, 2 * depth), jnp.float32),
            ],
        ),
        out_shape=[jax.ShapeDtypeStruct((near, bands, ROWS, wide), jnp.bfloat16)] * far
        + [jax.ShapeDtypeStruct((RADIX, frames, ROWS, 2 * depth), jnp.bfloat16)],
        compiler_params=pltpu.CompilerParams(vmem_limit_bytes=VMEM),
        cost_estimate=busy(frames / FRAMES),
    )(row_block, volts, taps_wide, turn_c, turn_s, table)


def slot_kernel(far, row_branch, hi_c, hi_s, lo_c, lo_s, *rest):
    chunks, outs, (table, total) = rest[: -2 - far], rest[-2 - far : -2], rest[-2:]
    depth = chunks[0].shape[3] // 2
    for a in range(hi_c.shape[1]):
        high_c, high_s = hi_c[:, a : a + 1], hi_s[:, a : a + 1]
        table[:, a * LANES : (a + 1) * LANES] = (high_c * lo_c[...] - high_s * lo_s[...]).astype(table.dtype)
        table[:, depth + a * LANES : depth + (a + 1) * LANES] = (
            high_s * lo_c[...] + high_c * lo_s[...]
        ).astype(table.dtype)
    total[...] = jnp.zeros_like(total)

    def branch(b, carry):
        rows = jnp.concatenate([c[b].reshape(c.shape[1] * c.shape[2], c.shape[3]) for c in chunks], axis=0)
        got = lax.dot_general(table[...], rows, NT, preferred_element_type=jnp.float32)
        total[...] = jnp.where(row_branch[...] == b, got, total[...])
        return carry

    lax.fori_loop(0, RADIX, branch, 0)
    plane, per = outs[0].shape[:2]
    for s, out in enumerate(outs):
        for d in range(plane):
            top = (s * plane + d) * per
            out[d] = total[top : top + per].astype(out.dtype)


def slot_tables(row_channel, row_filled, row_turned):
    depth = NCH // RADIX
    coarse = jnp.arange(depth // LANES, dtype=jnp.int32) * LANES
    fine = jnp.arange(LANES, dtype=jnp.int32)
    whole = row_channel - row_channel % RADIX
    hi_c, hi_s = phase(whole[:, None] * coarse[None, :] + row_turned[:, None] * (NCH // 4), NCH)
    lo_c, lo_s = phase(whole[:, None] * fine[None, :], NCH)
    scaling = row_filled.astype(jnp.float32)[:, None] * (1.0 / math.sqrt(NCH))
    return (row_channel % RADIX)[:, None], hi_c * scaling, hi_s * scaling, lo_c, lo_s


def slot_spectra(tables, chunks, per, far):
    rows = tables[0].shape[0]
    samples = sum(c.shape[1] * c.shape[2] for c in chunks)
    plane = rows // per // far
    return pl.pallas_call(
        functools.partial(slot_kernel, far),
        out_shape=[jax.ShapeDtypeStruct((plane, per, samples), jnp.bfloat16)] * far,
        scratch_shapes=[
            pltpu.VMEM((rows, chunks[0].shape[3]), jnp.bfloat16),
            pltpu.VMEM((rows, samples), jnp.float32),
        ],
        compiler_params=pltpu.CompilerParams(vmem_limit_bytes=VMEM),
        cost_estimate=busy(1),
    )(*tables, *chunks)


def correlate(here, pieces, far, halves):
    senders = pieces[0][0].shape[0]
    sub = pieces[0][0].shape[1] if halves == 1 else ROWS
    lanes = pieces[0][0].shape[2] // (2 * pieces[0][5])
    half = FRAMES * lanes
    block = senders * halves * sub
    signals = far * block

    def kernel(here_ref, *refs):
        parts, (out, held, turned, made, in_sems, out_sems) = refs[: len(pieces)], refs[len(pieces) :]
        coming = [[] for _ in range(far)]
        for index, (_, partner, row, which, first, frames) in enumerate(pieces):
            for part in range(2):
                src = parts[index].at[:, pl.ds(row, sub), pl.ds(part * frames * lanes, frames * lanes)]
                dst = held.at[partner, :, which, :, pl.ds(part * half + first * lanes, frames * lanes)]
                coming[partner].append(pltpu.make_async_copy(src, dst, in_sems.at[2 * index + part]))
        for copies in coming:
            for copy in copies:
                copy.start()
        inverse = 1.0 / half
        going = [[], []]
        slot = 0
        for i in range(far):
            for copy in coming[i]:
                copy.wait()
            left = held[i].reshape(block, 2 * half)
            turned[:, :half] = left[:, half:]
            turned[:, half:] = -left[:, :half]
            at_i = pl.ds(pl.multiple_of((here_ref[0] ^ i) * block, block), block)
            for j in range(i + 1):
                right = held[j].reshape(block, 2 * half)
                at_j = pl.ds(pl.multiple_of((here_ref[0] ^ j) * block, block), block)
                for copy in going[slot]:
                    copy.wait()
                going[slot] = []
                for part, rows in enumerate((left, turned[...])):
                    got = lax.dot_general(rows, right, NT, preferred_element_type=jnp.float32) * inverse
                    made[slot, part, 0] = got
                    going[slot].append(
                        pltpu.make_async_copy(
                            made.at[slot, part, 0], out.at[part, at_i, at_j], out_sems.at[slot, part, 0]
                        )
                    )
                    if i != j:
                        made[slot, part, 1] = got.T if part == 0 else -got.T
                        going[slot].append(
                            pltpu.make_async_copy(
                                made.at[slot, part, 1], out.at[part, at_j, at_i], out_sems.at[slot, part, 1]
                            )
                        )
                for copy in going[slot]:
                    copy.start()
                slot = 1 - slot
        for copies in going:
            for copy in copies:
                copy.wait()

    return pl.pallas_call(
        kernel,
        in_specs=[pl.BlockSpec(memory_space=pltpu.SMEM)] + [pl.BlockSpec(memory_space=pl.ANY)] * len(pieces),
        out_specs=pl.BlockSpec(memory_space=pl.ANY),
        out_shape=jax.ShapeDtypeStruct((2, signals, signals), jnp.float32),
        scratch_shapes=[
            pltpu.VMEM((far, senders, halves, sub, 2 * half), jnp.bfloat16),
            pltpu.VMEM((block, 2 * half), jnp.bfloat16),
            pltpu.VMEM((2, 2, 2, block, block), jnp.float32),
            pltpu.SemaphoreType.DMA((2 * len(pieces),)),
            pltpu.SemaphoreType.DMA((2, 2, 2)),
        ],
        compiler_params=pltpu.CompilerParams(vmem_limit_bytes=VMEM),
        cost_estimate=NO_COST,
    )(here, *[piece[0] for piece in pieces])


def weight_kernel(channel, delays, gains, out):
    beams = delays.shape[0]
    turns = delays[...] * (channel[pl.program_id(0)].astype(jnp.float32) * (1.0 / NCH))
    part = turns - jnp.floor(turns + 0.5)
    square = part * part
    cos_t = jnp.full_like(part, TWO_PI**16 / math.factorial(16))
    sin_t = jnp.full_like(part, -(TWO_PI**15) / math.factorial(15))
    for power in range(14, -1, -2):
        sign = -1.0 if power % 4 == 2 else 1.0
        cos_t = cos_t * square + sign * TWO_PI**power / math.factorial(power)
        if power > 0:
            sign = -1.0 if (power - 1) % 4 == 3 else 1.0
            sin_t = sin_t * square + sign * TWO_PI ** (power - 1) / math.factorial(power - 1)
    scaled = gains[...] * (1.0 / math.sqrt(gains.shape[1]))
    out[0, :beams] = (scaled * cos_t).astype(out.dtype)
    out[0, beams:] = (-scaled * sin_t * part).astype(out.dtype)


def beam_weights(channel, delays, gains):
    beams, listed = delays.shape
    slots = channel.shape[0]
    return pl.pallas_call(
        weight_kernel,
        grid=(slots,),
        in_specs=[
            pl.BlockSpec(memory_space=pltpu.SMEM),
            pl.BlockSpec(delays.shape, lambda i: (0, 0)),
            pl.BlockSpec(gains.shape, lambda i: (0, 0)),
        ],
        out_specs=pl.BlockSpec((1, 2 * beams, listed), lambda i: (i, 0, 0)),
        out_shape=jax.ShapeDtypeStruct((slots, 2 * beams, listed), jnp.bfloat16),
        cost_estimate=NO_COST,
    )(channel, delays, gains)


def combine(spectra, chooser, weights, sub):
    halves = len(spectra)
    slots, beams2, listed = weights.shape
    beams = beams2 // 2
    rows = 2 * slots
    senders = spectra[0].shape[0]
    partners = spectra[0].shape[1] // rows
    count = LANES // sub
    inner = senders // count
    groups = partners * halves * inner
    tiles = 2 * listed // LANES

    def kernel(*refs):
        got, (choose, weight, out, ordered, picked) = refs[: len(spectra)], refs[len(spectra) :]
        lane_ids = lax.broadcasted_iota(jnp.int32, (rows, LANES), 1)
        for s in range(partners):
            for h, spectrum in enumerate(got):
                row = s * rows
                for q in range(inner):
                    for t in range(FRAMES // count):
                        lane = t * LANES
                        pieces = [
                            spectrum[q * count + i, row : row + rows, lane : lane + LANES].astype(jnp.float32)
                            for i in range(count)
                        ]
                        for f, piece in enumerate(swap_blocks(pieces, lane_ids)):
                            top = (t * count + f) * rows
                            ordered[(s * halves + h) * inner + q, top : top + rows, :] = piece
        acc = None
        for q in range(groups):
            term = jnp.dot(
                ordered[q].astype(jnp.bfloat16),
                choose[q * LANES : (q + 1) * LANES, :],
                preferred_element_type=jnp.float32,
            )
            acc = term if acc is None else acc + term
        for lane in range(tiles):
            picked[lane] = acc[:, lane * LANES : (lane + 1) * LANES]
        for i in range(slots):
            chosen = [
                jnp.concatenate(
                    [
                        picked[p * tiles // 2 + lane, pl.ds(part * slots + i, FRAMES, rows), :]
                        for lane in range(tiles // 2)
                    ],
                    axis=1,
                )
                for p in range(2)
                for part in range(2)
            ]
            stacked = jnp.concatenate(chosen, axis=0).astype(jnp.bfloat16)
            mixed = lax.dot_general(stacked, weight[i], NT, preferred_element_type=jnp.float32)
            for p in range(2):
                at = 2 * FRAMES * p
                of_re, of_im = mixed[at : at + FRAMES], mixed[at + FRAMES : at + 2 * FRAMES]
                out[0, i, 0, :, p * beams : (p + 1) * beams] = of_re[:, :beams] - of_im[:, beams:]
                out[0, i, 1, :, p * beams : (p + 1) * beams] = of_im[:, :beams] + of_re[:, beams:]

    return pl.pallas_call(
        kernel,
        out_shape=jax.ShapeDtypeStruct((1, slots, 2, FRAMES, 2 * beams), jnp.float32),
        scratch_shapes=[
            pltpu.VMEM((groups, FRAMES * rows, LANES), jnp.float32),
            pltpu.VMEM((tiles, FRAMES * rows, LANES), jnp.float32),
        ],
        compiler_params=pltpu.CompilerParams(vmem_limit_bytes=VMEM),
        cost_estimate=NO_COST,
    )(*spectra, chooser, weights)


def after(value, other):
    return lax.optimization_barrier((value, other))[0]


def body(volts, prototype, beam_channels, station_index, delays, gains, assign):
    sig_dev = volts.shape[1]
    far, near, sb_count = lax.axis_size("far"), lax.axis_size("near"), lax.axis_size("sb")
    far_here, near_here, sb_here = [lax.axis_index(name).astype(jnp.int32) for name in ("far", "near", "sb")]
    st_count = far * near
    plane = near * sb_count
    depth = NCH // RADIX
    bands = depth // LANES
    fine = NCH // sb_count // RADIX // st_count
    partner = far_here ^ jnp.arange(far, dtype=jnp.int32)
    stations = (partner[:, None] * near + jnp.arange(near, dtype=jnp.int32)[None, :]).reshape(-1)

    def spread(*ids):
        total = ids[0]
        for more in ids[1:]:
            total = total[..., None] + more
        return total.reshape(-1)

    out_ids = spread(
        jnp.arange(bands, dtype=jnp.int32)[:, None] * LANES + (stations * fine)[None, :],
        jnp.arange(fine, dtype=jnp.int32),
    )
    table = transform_table(out_ids)
    turn_c, turn_s = phase(
        jnp.arange(RADIX, dtype=jnp.int32)[:, None] * jnp.arange(depth, dtype=jnp.int32)[None, :], NCH
    )
    taps_wide = jnp.broadcast_to(prototype[:, None, :], (prototype.shape[0], 8, NCH))

    def to_planes(xs):
        return [xs[0]] + [lax.ppermute(xs[s], "far", [(i, i ^ s) for i in range(far)]) for s in range(1, far)]

    def in_plane(xs):
        joined = xs[0] if len(xs) == 1 else jnp.concatenate(xs, axis=1)
        return lax.all_to_all(joined, ("near", "sb"), split_axis=0, concat_axis=0, tiled=True)

    share = sig_dev // sb_count
    sub = min(share, ROWS)
    halves = max(1, share // ROWS)
    inside = (sb_here * share) % ROWS
    unit = max(1, LANES * st_count * sb_count // NCH)
    early = FRAMES * 3 // 8 // unit * unit
    plan = [(0, 0, early), (0, early, FRAMES - early)] + [(h, 0, FRAMES) for h in range(1, halves)]
    crossed, branches = [], []
    for c, (which, first, frames) in enumerate(plan):
        if c > 1:
            table = after(table, crossed[c - 2])
        row_block = (sb_here * share // ROWS + which)[None]
        *outs, kept = channelise(row_block, volts, taps_wide, turn_c, turn_s, table, first, frames, far)
        table = after(table, outs)
        branches.append(kept)
        if sub < ROWS:
            outs = [lax.dynamic_slice_in_dim(x, inside, sub, axis=2) for x in outs]
        inner = st_count // RADIX
        if inner > 1:
            outs = [
                x.reshape(near // inner, sb_count, sub, 2 * frames, RADIX, inner, fine).transpose(0, 5, 1, 2, 3, 4, 6)
                for x in outs
            ]
        crossed.append(to_planes([x.reshape(plane, sub, -1) for x in outs]))

    assign, beam_channels, station_index = after((assign, beam_channels, station_index), branches)

    pieces, in_place = [], []
    for c, (which, first, frames) in enumerate(plan):
        step = far if which < halves - 1 else max(1, far // 2)
        in_place.append([in_plane(crossed[c][s : s + step]) for s in range(0, far, step)])
        for s in range(far):
            got, row = in_place[c][s // step], s % step * sub
            if halves == 1:
                pieces.append((got[:, row : row + sub].reshape(1, plane * sub, -1), s, 0, 0, first, frames))
            else:
                pieces.append((got, s, row, which, first, frames))

    per_dev = SLOTS // st_count
    owners = assign[:, 0]
    taken = (owners[:, None] == jnp.arange(sb_count, dtype=jnp.int32)[None, :]).astype(jnp.int32)
    position = jnp.sum(taken * jnp.cumsum(taken, axis=0), axis=1) - 1
    place = owners * SLOTS + position
    slot_ids = spread(
        stations * per_dev,
        jnp.arange(sb_count, dtype=jnp.int32) * SLOTS,
        jnp.arange(per_dev, dtype=jnp.int32),
    )
    picker = (place[None, :] == slot_ids[:, None]).astype(jnp.int32)
    filled = jnp.sum(picker, axis=1)
    slot_channel = jnp.sum(picker * beam_channels[None, :], axis=1)

    def by_row(values):
        values = values.reshape(st_count * sb_count, 1, per_dev)
        return jnp.broadcast_to(values, (st_count * sb_count, 2, per_dev)).reshape(-1)

    turned = jnp.broadcast_to(jnp.arange(2, dtype=jnp.int32)[None, :, None], (st_count * sb_count, 2, per_dev))
    mine = lax.dynamic_slice_in_dim(slot_channel, (near_here * sb_count + sb_here) * per_dev, per_dev)
    row_branch, *tables = slot_tables(by_row(slot_channel), by_row(filled), turned.reshape(-1))
    slot_received = []
    for h in range(halves):
        own = [c for c, (which, _, _) in enumerate(plan) if which == h]
        done = [crossed[c] for c in own] + [in_place[c] for c in range(own[0] - 1 if h else 0, own[-1])]
        row_branch = after(row_branch, done)
        spectra = slot_spectra([row_branch, *tables], [branches[c] for c in own], 2 * per_dev, far)
        row_branch = after(row_branch, spectra)
        if h == 0:
            weights = beam_weights(after(mine, spectra), delays, gains)
        if sub < ROWS:
            spectra = [
                lax.dynamic_slice_in_dim(x.reshape(plane, 2 * per_dev, FRAMES, ROWS), inside, sub, axis=3).reshape(
                    plane, 2 * per_dev, -1
                )
                for x in spectra
            ]
        slot_received.append(in_plane(to_planes(spectra)))

    signal_ids = spread(
        partner[:, None] * (near * sig_dev) + jnp.arange(halves, dtype=jnp.int32)[None, :] * sub,
        jnp.arange(plane, dtype=jnp.int32) * share,
        jnp.arange(sub, dtype=jnp.int32),
    )
    wanted = (station_index[None, :] * 2 + jnp.arange(2, dtype=jnp.int32)[:, None]).reshape(-1)
    chooser = (signal_ids[:, None] == wanted[None, :]).astype(jnp.bfloat16)

    visibility = correlate(after(far_here[None], spectra), pieces, far, halves)
    signals = visibility.shape[1]
    beam_out = combine(slot_received, chooser, weights, sub)
    return (visibility.reshape(2, 1, 1, signals, signals), beam_out)


def solution(mesh):
    st_count, sb_count = mesh.shape["st"], mesh.shape["sb"]
    far = math.gcd(4, st_count)
    planes = Mesh(mesh.devices.reshape(far, st_count // far, sb_count), ("far", "near", "sb"))
    st = ("far", "near")
    in_specs = (P(None, st, None), P(), P(), P(), P(), P(), P())
    out_specs = (P(None, "sb", st, None, None), P("sb", st, None, None, None))
    return jax.shard_map(body, mesh=planes, in_specs=in_specs, out_specs=out_specs, check_vma=False)
```

```python
import functools
import math

import jax
import jax.numpy as jnp
from jax import lax
from jax.experimental import pallas as pl
from jax.experimental.pallas import tpu as pltpu
from jax.sharding import Mesh
from jax.sharding import PartitionSpec as P

NCH = 4096
FRAMES = 16
SLOTS = 160
RADIX = 8
LANES = 128
ROWS = 16
VMEM = 56 * 1024 * 1024

NO_COST = pl.CostEstimate(flops=1, bytes_accessed=1, transcendentals=0)

TWO_PI = 2.0 * math.pi
NT = (((1,), (1,)), ((), ()))


def busy(share):
    return pl.CostEstimate(flops=int(share * 1e10), bytes_accessed=1, transcendentals=0)


def phase(turns, length):
    angles = (turns % length).astype(jnp.float32) * (TWO_PI / length)
    return jnp.cos(angles), jnp.sin(angles)


def table_kernel(hi_c, hi_s, lo_c, lo_s, out):
    fine, width = lo_c.shape
    depth = hi_c.shape[0] * fine

    def block(a, carry):
        top = pl.multiple_of(a * fine, fine)
        high_c, high_s = hi_c[pl.ds(a, 1), :], hi_s[pl.ds(a, 1), :]
        cos_t = (high_c * lo_c[...] - high_s * lo_s[...]).astype(out.dtype)
        sin_t = (high_s * lo_c[...] + high_c * lo_s[...]).astype(out.dtype)
        out[pl.ds(top, fine), :width] = cos_t
        out[pl.ds(top, fine), width:] = -sin_t
        out[pl.ds(depth + top, fine), :width] = sin_t
        out[pl.ds(depth + top, fine), width:] = cos_t
        return carry

    lax.fori_loop(0, hi_c.shape[0], block, 0)


def transform_table(out_ids):
    depth = NCH // RADIX
    out_ids = out_ids[None, :]
    lo_c, lo_s = phase(jnp.arange(ROWS, dtype=jnp.int32)[:, None] * out_ids, depth)
    hi_c, hi_s = phase(jnp.arange(0, depth, ROWS, dtype=jnp.int32)[:, None] * out_ids, depth)
    scale = 1.0 / math.sqrt(NCH)
    return pl.pallas_call(
        table_kernel,
        out_shape=jax.ShapeDtypeStruct((2 * depth, 2 * depth), jnp.bfloat16),
        cost_estimate=NO_COST,
    )(hi_c * scale, hi_s * scale, lo_c, lo_s)


def radix8(re, im):
    half = math.sqrt(0.5)

    def four(xr, xi):
        ar, ai, br, bi = xr[0] + xr[2], xi[0] + xi[2], xr[0] - xr[2], xi[0] - xi[2]
        cr, ci, dr, di = xr[1] + xr[3], xi[1] + xi[3], xr[1] - xr[3], xi[1] - xi[3]
        return [ar + cr, br + di, ar - cr, br - di], [ai + ci, bi - dr, ai - ci, bi + dr]

    er, ei = four(re[0::2], im[0::2])
    odd_r, odd_i = four(re[1::2], im[1::2])
    tr = [odd_r[0], (odd_r[1] + odd_i[1]) * half, odd_i[2], (odd_i[3] - odd_r[3]) * half]
    ti = [odd_i[0], (odd_i[1] - odd_r[1]) * half, -odd_r[2], (odd_r[3] + odd_i[3]) * -half]
    return (
        [e + t for e, t in zip(er, tr)] + [e - t for e, t in zip(er, tr)],
        [e + t for e, t in zip(ei, ti)] + [e - t for e, t in zip(ei, ti)],
    )


def swap_blocks(parts, lane_ids):
    count = len(parts)
    width = LANES // count
    parts = list(parts)
    step = 1
    while step < count:
        keep = (lane_ids // width) % (2 * step) < step
        for b in range(count):
            if b & step == 0:
                low, high = parts[b], parts[b + step]
                parts[b] = jnp.where(keep, low, pltpu.roll(high, step * width, 1))
                parts[b + step] = jnp.where(keep, pltpu.roll(low, LANES - step * width, 1), high)
        step *= 2
    return parts


def gather_blocks(parts, lane_ids):
    count = len(parts)
    width = LANES // count
    turned = [parts[0]] + [pltpu.roll(parts[b], b * width, 1) for b in range(1, count)]
    turned = [turned[-b % count] for b in range(count)]
    step = 1
    while step < count:
        moved = (lane_ids // width) & step != 0
        turned = [jnp.where(moved, turned[(g - step) % count], turned[g]) for g in range(count)]
        step *= 2
    return [turned[0]] + [pltpu.roll(turned[g], LANES - g * width, 1) for g in range(1, count)]


def channel_kernel(first, row_block, volts, taps_wide, turn_c, turn_s, table, *rest):
    outs, (branches, filtered, product) = rest[:-3], rest[-3:]
    near = RADIX // len(outs)
    taps = taps_wide.shape[0]
    length = taps_wide.shape[2]
    frames = filtered.shape[2]
    depth = length // RADIX
    bands = depth // LANES

    def column(j, carry):
        lane = pl.multiple_of(j * LANES, LANES)

        def strip(n1, inner):
            base = pl.multiple_of(n1 * depth + j * LANES, LANES)
            for part in range(2):
                sums = [None] * frames
                for seg in range(frames + taps - 1):
                    start = pl.multiple_of((first + seg) * length + base, LANES)
                    value = volts[part, :, pl.ds(start, LANES)].astype(jnp.float32)
                    for f in range(max(0, seg - taps + 1), min(frames, seg + 1)):
                        coef = taps_wide[seg - f, :, pl.ds(base, LANES)]
                        term = value * jnp.concatenate([coef, coef], axis=0)
                        sums[f] = term if sums[f] is None else sums[f] + term
                    if seg >= taps - 1:
                        filtered[part, n1, seg - taps + 1] = sums[seg - taps + 1]
            return inner

        lax.fori_loop(0, RADIX, strip, 0)

        def butterfly(f, inner):
            re, im = radix8(
                [filtered[0, n1, f] for n1 in range(RADIX)],
                [filtered[1, n1, f] for n1 in range(RADIX)],
            )
            for b in range(RADIX):
                turned_r, turned_i = re[b], im[b]
                if b > 0:
                    cos_t, sin_t = turn_c[b : b + 1, pl.ds(lane, LANES)], turn_s[b : b + 1, pl.ds(lane, LANES)]
                    turned_r, turned_i = re[b] * cos_t + im[b] * sin_t, im[b] * cos_t - re[b] * sin_t
                branches[b, f, :, pl.ds(lane, LANES)] = turned_r.astype(branches.dtype)
                branches[b, f, :, pl.ds(pl.multiple_of(depth + lane, LANES), LANES)] = turned_i.astype(branches.dtype)
            return inner

        lax.fori_loop(0, frames, butterfly, 0)
        return carry

    lax.fori_loop(0, bands, column, 0)

    def multiply(b, carry):
        rows = branches[b].reshape(frames * ROWS, 2 * depth)
        product[b] = jnp.dot(rows, table[...], preferred_element_type=jnp.float32)
        return carry

    lax.fori_loop(0, RADIX, multiply, 0)
    lane_ids = lax.broadcasted_iota(jnp.int32, (ROWS, LANES), 1)

    def regroup(f, carry):
        top = pl.multiple_of(f * ROWS, ROWS)
        for part in range(2):
            for band in range(bands):
                lane = part * depth + band * LANES
                pieces = [product[b, pl.ds(top, ROWS), lane : lane + LANES] for b in range(RADIX)]
                for g, piece in enumerate(gather_blocks(pieces, lane_ids)):
                    at = pl.multiple_of((part * frames + f) * LANES, LANES)
                    out = outs[g // near]
                    out[g % near, band, :, pl.ds(at, LANES)] = piece.astype(out.dtype)
        return carry

    lax.fori_loop(0, frames, regroup, 0)


def channelise(row_block, volts, taps_wide, turn_c, turn_s, table, first, frames, far):
    taps = taps_wide.shape[0]
    length = volts.shape[2] if first > 0 else (frames + taps - 1) * NCH
    depth = NCH // RADIX
    bands = depth // LANES
    wide = 2 * frames * LANES
    near = RADIX // far
    return pl.pallas_call(
        functools.partial(channel_kernel, first),
        grid_spec=pltpu.PrefetchScalarGridSpec(
            num_scalar_prefetch=1,
            grid=(1,),
            in_specs=[
                pl.BlockSpec((2, ROWS, length), lambda i, row: (0, row[0], 0)),
                pl.BlockSpec(taps_wide.shape, lambda i, row: (0, 0, 0)),
                pl.BlockSpec(turn_c.shape, lambda i, row: (0, 0)),
                pl.BlockSpec(turn_s.shape, lambda i, row: (0, 0)),
                pl.BlockSpec(table.shape, lambda i, row: (0, 0)),
            ],
            out_specs=[pl.BlockSpec((near, bands, ROWS, wide), lambda i, row: (0, 0, 0, 0))] * far
            + [pl.BlockSpec((RADIX, frames, ROWS, 2 * depth), lambda i, row: (0, 0, 0, 0))],
            scratch_shapes=[
                pltpu.VMEM((2, RADIX, frames, ROWS, LANES), jnp.float32),
                pltpu.VMEM((RADIX, frames * ROWS, 2 * depth), jnp.float32),
            ],
        ),
        out_shape=[jax.ShapeDtypeStruct((near, bands, ROWS, wide), jnp.bfloat16)] * far
        + [jax.ShapeDtypeStruct((RADIX, frames, ROWS, 2 * depth), jnp.bfloat16)],
        compiler_params=pltpu.CompilerParams(vmem_limit_bytes=VMEM),
        cost_estimate=busy(frames / FRAMES),
    )(row_block, volts, taps_wide, turn_c, turn_s, table)


def slot_kernel(far, row_branch, hi_c, hi_s, lo_c, lo_s, *rest):
    chunks, outs, (table, total) = rest[: -2 - far], rest[-2 - far : -2], rest[-2:]
    depth = chunks[0].shape[3] // 2
    for a in range(hi_c.shape[1]):
        high_c, high_s = hi_c[:, a : a + 1], hi_s[:, a : a + 1]
        table[:, a * LANES : (a + 1) * LANES] = (high_c * lo_c[...] - high_s * lo_s[...]).astype(table.dtype)
        table[:, depth + a * LANES : depth + (a + 1) * LANES] = (
            high_s * lo_c[...] + high_c * lo_s[...]
        ).astype(table.dtype)
    total[...] = jnp.zeros_like(total)

    def branch(b, carry):
        rows = jnp.concatenate([c[b].reshape(c.shape[1] * c.shape[2], c.shape[3]) for c in chunks], axis=0)
        got = lax.dot_general(table[...], rows, NT, preferred_element_type=jnp.float32)
        total[...] = jnp.where(row_branch[...] == b, got, total[...])
        return carry

    lax.fori_loop(0, RADIX, branch, 0)
    plane, per = outs[0].shape[:2]
    for s, out in enumerate(outs):
        for d in range(plane):
            top = (s * plane + d) * per
            out[d] = total[top : top + per].astype(out.dtype)


def slot_tables(row_channel, row_filled, row_turned):
    depth = NCH // RADIX
    coarse = jnp.arange(depth // LANES, dtype=jnp.int32) * LANES
    fine = jnp.arange(LANES, dtype=jnp.int32)
    whole = row_channel - row_channel % RADIX
    hi_c, hi_s = phase(whole[:, None] * coarse[None, :] + row_turned[:, None] * (NCH // 4), NCH)
    lo_c, lo_s = phase(whole[:, None] * fine[None, :], NCH)
    scaling = row_filled.astype(jnp.float32)[:, None] * (1.0 / math.sqrt(NCH))
    return (row_channel % RADIX)[:, None], hi_c * scaling, hi_s * scaling, lo_c, lo_s


def slot_spectra(tables, chunks, per, far):
    rows = tables[0].shape[0]
    samples = sum(c.shape[1] * c.shape[2] for c in chunks)
    plane = rows // per // far
    return pl.pallas_call(
        functools.partial(slot_kernel, far),
        out_shape=[jax.ShapeDtypeStruct((plane, per, samples), jnp.bfloat16)] * far,
        scratch_shapes=[
            pltpu.VMEM((rows, chunks[0].shape[3]), jnp.bfloat16),
            pltpu.VMEM((rows, samples), jnp.float32),
        ],
        compiler_params=pltpu.CompilerParams(vmem_limit_bytes=VMEM),
        cost_estimate=busy(1),
    )(*tables, *chunks)


def correlate(here, pieces, far, halves):
    senders, sub, _ = pieces[0][0].shape
    lanes = pieces[0][0].shape[2] // (2 * pieces[0][4])
    half = FRAMES * lanes
    splits = max(1, senders * halves * sub // 256)
    each = senders // splits
    block = each * halves * sub
    count = far * splits
    signals = count * block

    def kernel(here_ref, *refs):
        parts, (out, held, turned, made, in_sems, out_sems) = refs[: len(pieces)], refs[len(pieces) :]
        coming = [[] for _ in range(count)]
        for index, (_, partner, which, first, frames) in enumerate(pieces):
            for q in range(splits):
                at = partner * splits + q
                for part in range(2):
                    src = parts[index].at[pl.ds(q * each, each), :, pl.ds(part * frames * lanes, frames * lanes)]
                    dst = held.at[at, :, which, :, pl.ds(part * half + first * lanes, frames * lanes)]
                    sem = in_sems.at[(index * splits + q) * 2 + part]
                    coming[at].append(pltpu.make_async_copy(src, dst, sem))
        for copies in coming:
            for copy in copies:
                copy.start()

        def rows_of(i):
            return pl.ds(pl.multiple_of(((here_ref[0] ^ (i // splits)) * splits + i % splits) * block, block), block)

        inverse = 1.0 / half
        going = [[], []]
        slot = 0
        for i in range(count):
            for copy in coming[i]:
                copy.wait()
            left = held[i].reshape(block, 2 * half)
            turned[:, :half] = left[:, half:]
            turned[:, half:] = -left[:, :half]
            at_i = rows_of(i)
            for j in range(i + 1):
                right = held[j].reshape(block, 2 * half)
                at_j = rows_of(j)
                for copy in going[slot]:
                    copy.wait()
                going[slot] = []
                for part, rows in enumerate((left, turned[...])):
                    got = lax.dot_general(rows, right, NT, preferred_element_type=jnp.float32) * inverse
                    made[slot, part, 0] = got
                    going[slot].append(
                        pltpu.make_async_copy(
                            made.at[slot, part, 0], out.at[part, at_i, at_j], out_sems.at[slot, part, 0]
                        )
                    )
                    if i != j:
                        made[slot, part, 1] = got.T if part == 0 else -got.T
                        going[slot].append(
                            pltpu.make_async_copy(
                                made.at[slot, part, 1], out.at[part, at_j, at_i], out_sems.at[slot, part, 1]
                            )
                        )
                for copy in going[slot]:
                    copy.start()
                slot = 1 - slot
        for copies in going:
            for copy in copies:
                copy.wait()

    return pl.pallas_call(
        kernel,
        in_specs=[pl.BlockSpec(memory_space=pltpu.SMEM)] + [pl.BlockSpec(memory_space=pl.ANY)] * len(pieces),
        out_specs=pl.BlockSpec(memory_space=pl.ANY),
        out_shape=jax.ShapeDtypeStruct((2, signals, signals), jnp.float32),
        scratch_shapes=[
            pltpu.VMEM((count, each, halves, sub, 2 * half), jnp.bfloat16),
            pltpu.VMEM((block, 2 * half), jnp.bfloat16),
            pltpu.VMEM((2, 2, 2, block, block), jnp.float32),
            pltpu.SemaphoreType.DMA((2 * splits * len(pieces),)),
            pltpu.SemaphoreType.DMA((2, 2, 2)),
        ],
        compiler_params=pltpu.CompilerParams(vmem_limit_bytes=VMEM),
        cost_estimate=NO_COST,
    )(here, *[piece[0] for piece in pieces])


def weight_kernel(channel, delays, gains, out):
    beams = delays.shape[0]
    turns = delays[...] * (channel[pl.program_id(0)].astype(jnp.float32) * (1.0 / NCH))
    part = turns - jnp.floor(turns + 0.5)
    square = part * part
    cos_t = jnp.full_like(part, TWO_PI**16 / math.factorial(16))
    sin_t = jnp.full_like(part, -(TWO_PI**15) / math.factorial(15))
    for power in range(14, -1, -2):
        sign = -1.0 if power % 4 == 2 else 1.0
        cos_t = cos_t * square + sign * TWO_PI**power / math.factorial(power)
        if power > 0:
            sign = -1.0 if (power - 1) % 4 == 3 else 1.0
            sin_t = sin_t * square + sign * TWO_PI ** (power - 1) / math.factorial(power - 1)
    scaled = gains[...] * (1.0 / math.sqrt(gains.shape[1]))
    out[0, :beams] = (scaled * cos_t).astype(out.dtype)
    out[0, beams:] = (-scaled * sin_t * part).astype(out.dtype)


def beam_weights(channel, delays, gains):
    beams, listed = delays.shape
    slots = channel.shape[0]
    return pl.pallas_call(
        weight_kernel,
        grid=(slots,),
        in_specs=[
            pl.BlockSpec(memory_space=pltpu.SMEM),
            pl.BlockSpec(delays.shape, lambda i: (0, 0)),
            pl.BlockSpec(gains.shape, lambda i: (0, 0)),
        ],
        out_specs=pl.BlockSpec((1, 2 * beams, listed), lambda i: (i, 0, 0)),
        out_shape=jax.ShapeDtypeStruct((slots, 2 * beams, listed), jnp.bfloat16),
        cost_estimate=NO_COST,
    )(channel, delays, gains)


def combine(spectra, chooser, weights, sub):
    slots, beams2, listed = weights.shape
    beams = beams2 // 2
    rows = 2 * slots
    senders = spectra[0].shape[0]
    partners = len(spectra)
    halves = spectra[0].shape[2] // (FRAMES * sub)
    count = LANES // sub
    inner = senders // count
    groups = partners * halves * inner
    tiles = 2 * listed // LANES

    def kernel(*refs):
        got, (choose, weight, out, ordered, picked) = refs[: len(spectra)], refs[len(spectra) :]
        lane_ids = lax.broadcasted_iota(jnp.int32, (rows, LANES), 1)
        for s, spectrum in enumerate(got):
            for h in range(halves):
                for q in range(inner):
                    for t in range(FRAMES // count):
                        lane = h * FRAMES * sub + t * LANES
                        pieces = [
                            spectrum[q * count + i, :, lane : lane + LANES].astype(jnp.float32)
                            for i in range(count)
                        ]
                        for f, piece in enumerate(swap_blocks(pieces, lane_ids)):
                            top = (t * count + f) * rows
                            ordered[(s * halves + h) * inner + q, top : top + rows, :] = piece
        acc = None
        for q in range(groups):
            term = jnp.dot(
                ordered[q].astype(jnp.bfloat16),
                choose[q * LANES : (q + 1) * LANES, :],
                preferred_element_type=jnp.float32,
            )
            acc = term if acc is None else acc + term
        for lane in range(tiles):
            picked[lane] = acc[:, lane * LANES : (lane + 1) * LANES]
        for i in range(slots):
            chosen = [
                jnp.concatenate(
                    [
                        picked[p * tiles // 2 + lane, pl.ds(part * slots + i, FRAMES, rows), :]
                        for lane in range(tiles // 2)
                    ],
                    axis=1,
                )
                for p in range(2)
                for part in range(2)
            ]
            stacked = jnp.concatenate(chosen, axis=0).astype(jnp.bfloat16)
            mixed = lax.dot_general(stacked, weight[i], NT, preferred_element_type=jnp.float32)
            for p in range(2):
                at = 2 * FRAMES * p
                of_re, of_im = mixed[at : at + FRAMES], mixed[at + FRAMES : at + 2 * FRAMES]
                out[0, i, 0, :, p * beams : (p + 1) * beams] = of_re[:, :beams] - of_im[:, beams:]
                out[0, i, 1, :, p * beams : (p + 1) * beams] = of_im[:, :beams] + of_re[:, beams:]

    return pl.pallas_call(
        kernel,
        out_shape=jax.ShapeDtypeStruct((1, slots, 2, FRAMES, 2 * beams), jnp.float32),
        scratch_shapes=[
            pltpu.VMEM((groups, FRAMES * rows, LANES), jnp.float32),
            pltpu.VMEM((tiles, FRAMES * rows, LANES), jnp.float32),
        ],
        compiler_params=pltpu.CompilerParams(vmem_limit_bytes=VMEM),
        cost_estimate=NO_COST,
    )(*spectra, chooser, weights)


def after(value, other):
    return lax.optimization_barrier((value, other))[0]


def body(volts, prototype, beam_channels, station_index, delays, gains, assign):
    sig_dev = volts.shape[1]
    far, near, sb_count = lax.axis_size("far"), lax.axis_size("near"), lax.axis_size("sb")
    far_here, near_here, sb_here = [lax.axis_index(name).astype(jnp.int32) for name in ("far", "near", "sb")]
    st_count = far * near
    plane = near * sb_count
    depth = NCH // RADIX
    bands = depth // LANES
    fine = NCH // sb_count // RADIX // st_count
    partner = far_here ^ jnp.arange(far, dtype=jnp.int32)
    stations = (partner[:, None] * near + jnp.arange(near, dtype=jnp.int32)[None, :]).reshape(-1)

    def spread(*ids):
        total = ids[0]
        for more in ids[1:]:
            total = total[..., None] + more
        return total.reshape(-1)

    out_ids = spread(
        jnp.arange(bands, dtype=jnp.int32)[:, None] * LANES + (stations * fine)[None, :],
        jnp.arange(fine, dtype=jnp.int32),
    )
    table = transform_table(out_ids)
    turn_c, turn_s = phase(
        jnp.arange(RADIX, dtype=jnp.int32)[:, None] * jnp.arange(depth, dtype=jnp.int32)[None, :], NCH
    )
    taps_wide = jnp.broadcast_to(prototype[:, None, :], (prototype.shape[0], 8, NCH))

    def cross(x):
        return lax.ppermute(x, "far", [(i, i ^ 1) for i in range(far)])

    latest = [None]

    def in_plane(x):
        if latest[0] is not None:
            x = after(x, latest[0])
        latest[0] = lax.all_to_all(x, ("near", "sb"), split_axis=0, concat_axis=0, tiled=True)
        return latest[0]

    share = sig_dev // sb_count
    sub = min(share, ROWS)
    halves = max(1, share // ROWS)
    inside = (sb_here * share) % ROWS
    unit = max(1, LANES * st_count * sb_count // NCH)
    early = FRAMES * 3 // 8 // unit * unit
    plan = [(0, 0, early), (0, early, FRAMES - early)] + [(h, 0, FRAMES) for h in range(1, halves)]
    crossed, owned, branches = [], [], []
    for c, (which, first, frames) in enumerate(plan):
        if c > 1:
            table = after(table, crossed[c - 2])
        row_block = (sb_here * share // ROWS + which)[None]
        *outs, kept = channelise(row_block, volts, taps_wide, turn_c, turn_s, table, first, frames, far)
        table = after(table, outs)
        branches.append(kept)
        if sub < ROWS:
            outs = [lax.dynamic_slice_in_dim(x, inside, sub, axis=2) for x in outs]
        inner = st_count // RADIX
        if inner > 1:
            outs = [
                x.reshape(near // inner, sb_count, sub, 2 * frames, RADIX, inner, fine).transpose(0, 5, 1, 2, 3, 4, 6)
                for x in outs
            ]
        outs = [x.reshape(plane, sub, -1) for x in outs]
        owned.append(outs[0])
        crossed.append(cross(outs[1]))

    assign, beam_channels, station_index = after((assign, beam_channels, station_index), branches)

    per_dev = SLOTS // st_count
    owners = assign[:, 0]
    taken = (owners[:, None] == jnp.arange(sb_count, dtype=jnp.int32)[None, :]).astype(jnp.int32)
    position = jnp.sum(taken * jnp.cumsum(taken, axis=0), axis=1) - 1
    place = owners * SLOTS + position
    slot_ids = spread(
        stations * per_dev,
        jnp.arange(sb_count, dtype=jnp.int32) * SLOTS,
        jnp.arange(per_dev, dtype=jnp.int32),
    )
    picker = (place[None, :] == slot_ids[:, None]).astype(jnp.int32)
    filled = jnp.sum(picker, axis=1)
    slot_channel = jnp.sum(picker * beam_channels[None, :], axis=1)

    def by_row(values):
        values = values.reshape(st_count * sb_count, 1, per_dev)
        return jnp.broadcast_to(values, (st_count * sb_count, 2, per_dev)).reshape(-1)

    turned = jnp.broadcast_to(jnp.arange(2, dtype=jnp.int32)[None, :, None], (st_count * sb_count, 2, per_dev))
    mine = lax.dynamic_slice_in_dim(slot_channel, (near_here * sb_count + sb_here) * per_dev, per_dev)
    row_branch, *tables = slot_tables(by_row(slot_channel), by_row(filled), turned.reshape(-1))

    in_place = []
    for c in range(len(plan) - 1):
        in_place.append([in_plane(owned[c]), in_plane(crossed[c])])
    row_branch = after(row_branch, (crossed[-2], in_place[-1][0]))
    spectra = slot_spectra([row_branch, *tables], branches, 2 * per_dev, far)
    if sub < ROWS:
        spectra = [
            lax.dynamic_slice_in_dim(x.reshape(plane, 2 * per_dev, FRAMES, ROWS), inside, sub, axis=3).reshape(
                plane, 2 * per_dev, -1
            )
            for x in spectra
        ]
    slot_crossed = cross(spectra[1])
    last = in_plane(owned[-1])
    slot_received = [in_plane(spectra[0])]
    weights = beam_weights(after(mine, (crossed[-1], slot_received[0])), delays, gains)
    in_place.append([last, in_plane(crossed[-1])])
    slot_received.append(in_plane(slot_crossed))

    pieces = []
    for c, (which, first, frames) in enumerate(plan):
        for s in range(far):
            got = in_place[c][s]
            if halves == 1:
                got = got.reshape(-1, min(256, plane * sub), got.shape[2])
            pieces.append((got, s, which, first, frames))

    signal_ids = spread(
        partner[:, None] * (near * sig_dev) + jnp.arange(halves, dtype=jnp.int32)[None, :] * sub,
        jnp.arange(plane, dtype=jnp.int32) * share,
        jnp.arange(sub, dtype=jnp.int32),
    )
    wanted = (station_index[None, :] * 2 + jnp.arange(2, dtype=jnp.int32)[:, None]).reshape(-1)
    chooser = (signal_ids[:, None] == wanted[None, :]).astype(jnp.bfloat16)

    visibility = correlate(after(far_here[None], weights), pieces, far, halves)
    signals = visibility.shape[1]
    beam_out = combine(slot_received, chooser, weights, sub)
    return (visibility.reshape(2, 1, 1, signals, signals), beam_out)


def solution(mesh):
    st_count, sb_count = mesh.shape["st"], mesh.shape["sb"]
    far = 2
    planes = Mesh(mesh.devices.reshape(far, st_count // far, sb_count), ("far", "near", "sb"))
    st = ("far", "near")
    in_specs = (P(None, st, None), P(), P(), P(), P(), P(), P())
    out_specs = (P(None, "sb", st, None, None), P("sb", st, None, None, None))
    return jax.shard_map(body, mesh=planes, in_specs=in_specs, out_specs=out_specs, check_vma=False)
```

```python
import functools
import math

import jax
import jax.numpy as jnp
from jax import lax
from jax.experimental import pallas as pl
from jax.experimental.pallas import tpu as pltpu
from jax.sharding import Mesh
from jax.sharding import PartitionSpec as P

NCH = 4096
FRAMES = 16
SLOTS = 160
RADIX = 8
LANES = 128
ROWS = 16
VMEM = 56 * 1024 * 1024

NO_COST = pl.CostEstimate(flops=1, bytes_accessed=1, transcendentals=0)

TWO_PI = 2.0 * math.pi
NT = (((1,), (1,)), ((), ()))


def busy(share):
    return pl.CostEstimate(flops=int(share * 1e10), bytes_accessed=1, transcendentals=0)


def phase(turns, length):
    angles = (turns % length).astype(jnp.float32) * (TWO_PI / length)
    return jnp.cos(angles), jnp.sin(angles)


def table_kernel(hi_c, hi_s, lo_c, lo_s, out):
    fine, width = lo_c.shape
    depth = hi_c.shape[0] * fine

    def block(a, carry):
        top = pl.multiple_of(a * fine, fine)
        high_c, high_s = hi_c[pl.ds(a, 1), :], hi_s[pl.ds(a, 1), :]
        cos_t = (high_c * lo_c[...] - high_s * lo_s[...]).astype(out.dtype)
        sin_t = (high_s * lo_c[...] + high_c * lo_s[...]).astype(out.dtype)
        out[pl.ds(top, fine), :width] = cos_t
        out[pl.ds(top, fine), width:] = -sin_t
        out[pl.ds(depth + top, fine), :width] = sin_t
        out[pl.ds(depth + top, fine), width:] = cos_t
        return carry

    lax.fori_loop(0, hi_c.shape[0], block, 0)


def transform_table(out_ids):
    depth = NCH // RADIX
    out_ids = out_ids[None, :]
    lo_c, lo_s = phase(jnp.arange(ROWS, dtype=jnp.int32)[:, None] * out_ids, depth)
    hi_c, hi_s = phase(jnp.arange(0, depth, ROWS, dtype=jnp.int32)[:, None] * out_ids, depth)
    scale = 1.0 / math.sqrt(NCH)
    return pl.pallas_call(
        table_kernel,
        out_shape=jax.ShapeDtypeStruct((2 * depth, 2 * depth), jnp.bfloat16),
        cost_estimate=NO_COST,
    )(hi_c * scale, hi_s * scale, lo_c, lo_s)


def radix8(re, im):
    half = math.sqrt(0.5)

    def four(xr, xi):
        ar, ai, br, bi = xr[0] + xr[2], xi[0] + xi[2], xr[0] - xr[2], xi[0] - xi[2]
        cr, ci, dr, di = xr[1] + xr[3], xi[1] + xi[3], xr[1] - xr[3], xi[1] - xi[3]
        return [ar + cr, br + di, ar - cr, br - di], [ai + ci, bi - dr, ai - ci, bi + dr]

    er, ei = four(re[0::2], im[0::2])
    odd_r, odd_i = four(re[1::2], im[1::2])
    tr = [odd_r[0], (odd_r[1] + odd_i[1]) * half, odd_i[2], (odd_i[3] - odd_r[3]) * half]
    ti = [odd_i[0], (odd_i[1] - odd_r[1]) * half, -odd_r[2], (odd_r[3] + odd_i[3]) * -half]
    return (
        [e + t for e, t in zip(er, tr)] + [e - t for e, t in zip(er, tr)],
        [e + t for e, t in zip(ei, ti)] + [e - t for e, t in zip(ei, ti)],
    )


def swap_blocks(parts, lane_ids):
    count = len(parts)
    width = LANES // count
    parts = list(parts)
    step = 1
    while step < count:
        keep = (lane_ids // width) % (2 * step) < step
        for b in range(count):
            if b & step == 0:
                low, high = parts[b], parts[b + step]
                parts[b] = jnp.where(keep, low, pltpu.roll(high, step * width, 1))
                parts[b + step] = jnp.where(keep, pltpu.roll(low, LANES - step * width, 1), high)
        step *= 2
    return parts


def gather_blocks(parts, lane_ids):
    count = len(parts)
    width = LANES // count
    turned = [parts[0]] + [pltpu.roll(parts[b], b * width, 1) for b in range(1, count)]
    turned = [turned[-b % count] for b in range(count)]
    step = 1
    while step < count:
        moved = (lane_ids // width) & step != 0
        turned = [jnp.where(moved, turned[(g - step) % count], turned[g]) for g in range(count)]
        step *= 2
    return [turned[0]] + [pltpu.roll(turned[g], LANES - g * width, 1) for g in range(1, count)]


def channel_kernel(first, row_block, volts, taps_wide, turn_c, turn_s, table, *rest):
    outs, (branches, filtered, product) = rest[:-3], rest[-3:]
    near = RADIX // len(outs)
    taps = taps_wide.shape[0]
    length = taps_wide.shape[2]
    frames = filtered.shape[2]
    depth = length // RADIX
    bands = depth // LANES

    def column(j, carry):
        lane = pl.multiple_of(j * LANES, LANES)

        def strip(n1, inner):
            base = pl.multiple_of(n1 * depth + j * LANES, LANES)
            for part in range(2):
                sums = [None] * frames
                for seg in range(frames + taps - 1):
                    start = pl.multiple_of((first + seg) * length + base, LANES)
                    value = volts[part, :, pl.ds(start, LANES)].astype(jnp.float32)
                    for f in range(max(0, seg - taps + 1), min(frames, seg + 1)):
                        coef = taps_wide[seg - f, :, pl.ds(base, LANES)]
                        term = value * jnp.concatenate([coef, coef], axis=0)
                        sums[f] = term if sums[f] is None else sums[f] + term
                    if seg >= taps - 1:
                        filtered[part, n1, seg - taps + 1] = sums[seg - taps + 1]
            return inner

        lax.fori_loop(0, RADIX, strip, 0)

        def butterfly(f, inner):
            re, im = radix8(
                [filtered[0, n1, f] for n1 in range(RADIX)],
                [filtered[1, n1, f] for n1 in range(RADIX)],
            )
            for b in range(RADIX):
                turned_r, turned_i = re[b], im[b]
                if b > 0:
                    cos_t, sin_t = turn_c[b : b + 1, pl.ds(lane, LANES)], turn_s[b : b + 1, pl.ds(lane, LANES)]
                    turned_r, turned_i = re[b] * cos_t + im[b] * sin_t, im[b] * cos_t - re[b] * sin_t
                branches[b, f, :, pl.ds(lane, LANES)] = turned_r.astype(branches.dtype)
                branches[b, f, :, pl.ds(pl.multiple_of(depth + lane, LANES), LANES)] = turned_i.astype(branches.dtype)
            return inner

        lax.fori_loop(0, frames, butterfly, 0)
        return carry

    lax.fori_loop(0, bands, column, 0)

    def multiply(b, carry):
        rows = branches[b].reshape(frames * ROWS, 2 * depth)
        product[b] = jnp.dot(rows, table[...], preferred_element_type=jnp.float32)
        return carry

    lax.fori_loop(0, RADIX, multiply, 0)
    lane_ids = lax.broadcasted_iota(jnp.int32, (ROWS, LANES), 1)

    def regroup(f, carry):
        top = pl.multiple_of(f * ROWS, ROWS)
        for part in range(2):
            for band in range(bands):
                lane = part * depth + band * LANES
                pieces = [product[b, pl.ds(top, ROWS), lane : lane + LANES] for b in range(RADIX)]
                for g, piece in enumerate(gather_blocks(pieces, lane_ids)):
                    at = pl.multiple_of((part * frames + f) * LANES, LANES)
                    out = outs[g // near]
                    out[g % near, band, :, pl.ds(at, LANES)] = piece.astype(out.dtype)
        return carry

    lax.fori_loop(0, frames, regroup, 0)


def channelise(row_block, volts, taps_wide, turn_c, turn_s, table, first, frames, far):
    taps = taps_wide.shape[0]
    length = volts.shape[2] if first > 0 else (frames + taps - 1) * NCH
    depth = NCH // RADIX
    bands = depth // LANES
    wide = 2 * frames * LANES
    near = RADIX // far
    return pl.pallas_call(
        functools.partial(channel_kernel, first),
        grid_spec=pltpu.PrefetchScalarGridSpec(
            num_scalar_prefetch=1,
            grid=(1,),
            in_specs=[
                pl.BlockSpec((2, ROWS, length), lambda i, row: (0, row[0], 0)),
                pl.BlockSpec(taps_wide.shape, lambda i, row: (0, 0, 0)),
                pl.BlockSpec(turn_c.shape, lambda i, row: (0, 0)),
                pl.BlockSpec(turn_s.shape, lambda i, row: (0, 0)),
                pl.BlockSpec(table.shape, lambda i, row: (0, 0)),
            ],
            out_specs=[pl.BlockSpec((near, bands, ROWS, wide), lambda i, row: (0, 0, 0, 0))] * far
            + [pl.BlockSpec((RADIX, frames, ROWS, 2 * depth), lambda i, row: (0, 0, 0, 0))],
            scratch_shapes=[
                pltpu.VMEM((2, RADIX, frames, ROWS, LANES), jnp.float32),
                pltpu.VMEM((RADIX, frames * ROWS, 2 * depth), jnp.float32),
            ],
        ),
        out_shape=[jax.ShapeDtypeStruct((near, bands, ROWS, wide), jnp.bfloat16)] * far
        + [jax.ShapeDtypeStruct((RADIX, frames, ROWS, 2 * depth), jnp.bfloat16)],
        compiler_params=pltpu.CompilerParams(vmem_limit_bytes=VMEM),
        cost_estimate=busy(frames / FRAMES),
    )(row_block, volts, taps_wide, turn_c, turn_s, table)


def slot_kernel(far, row_branch, hi_c, hi_s, lo_c, lo_s, *rest):
    chunks, outs, (table, total) = rest[: -2 - far], rest[-2 - far : -2], rest[-2:]
    depth = chunks[0].shape[3] // 2
    for a in range(hi_c.shape[1]):
        high_c, high_s = hi_c[:, a : a + 1], hi_s[:, a : a + 1]
        table[:, a * LANES : (a + 1) * LANES] = (high_c * lo_c[...] - high_s * lo_s[...]).astype(table.dtype)
        table[:, depth + a * LANES : depth + (a + 1) * LANES] = (
            high_s * lo_c[...] + high_c * lo_s[...]
        ).astype(table.dtype)
    total[...] = jnp.zeros_like(total)

    def branch(b, carry):
        rows = jnp.concatenate([c[b].reshape(c.shape[1] * c.shape[2], c.shape[3]) for c in chunks], axis=0)
        got = lax.dot_general(table[...], rows, NT, preferred_element_type=jnp.float32)
        total[...] = jnp.where(row_branch[...] == b, got, total[...])
        return carry

    lax.fori_loop(0, RADIX, branch, 0)
    plane, per = outs[0].shape[:2]
    for s, out in enumerate(outs):
        for d in range(plane):
            top = (s * plane + d) * per
            out[d] = total[top : top + per].astype(out.dtype)


def slot_tables(row_channel, row_filled, row_turned):
    depth = NCH // RADIX
    coarse = jnp.arange(depth // LANES, dtype=jnp.int32) * LANES
    fine = jnp.arange(LANES, dtype=jnp.int32)
    whole = row_channel - row_channel % RADIX
    hi_c, hi_s = phase(whole[:, None] * coarse[None, :] + row_turned[:, None] * (NCH // 4), NCH)
    lo_c, lo_s = phase(whole[:, None] * fine[None, :], NCH)
    scaling = row_filled.astype(jnp.float32)[:, None] * (1.0 / math.sqrt(NCH))
    return (row_channel % RADIX)[:, None], hi_c * scaling, hi_s * scaling, lo_c, lo_s


def slot_spectra(tables, chunks, per, far):
    rows = tables[0].shape[0]
    samples = sum(c.shape[1] * c.shape[2] for c in chunks)
    plane = rows // per // far
    return pl.pallas_call(
        functools.partial(slot_kernel, far),
        out_shape=[jax.ShapeDtypeStruct((plane, per, samples), jnp.bfloat16)] * far,
        scratch_shapes=[
            pltpu.VMEM((rows, chunks[0].shape[3]), jnp.bfloat16),
            pltpu.VMEM((rows, samples), jnp.float32),
        ],
        compiler_params=pltpu.CompilerParams(vmem_limit_bytes=VMEM),
        cost_estimate=busy(1),
    )(*tables, *chunks)


def correlate(here, pieces, far, halves, lanes):
    senders, sub, _ = pieces[0][0].shape
    half = FRAMES * lanes
    splits = max(1, senders * halves * sub // 256)
    each = senders // splits
    block = each * halves * sub
    count = far * splits
    signals = count * block

    def kernel(here_ref, *refs):
        parts, (out, held, turned, made, in_sems, out_sems) = refs[: len(pieces)], refs[len(pieces) :]
        coming = [[] for _ in range(count)]
        for index, (_, lane, partner, which, first, frames) in enumerate(pieces):
            for q in range(splits):
                at = partner * splits + (q ^ partner)
                for part in range(2):
                    src = parts[index].at[
                        pl.ds(q * each, each), :, pl.ds(lane + part * frames * lanes, frames * lanes)
                    ]
                    dst = held.at[at, :, which, :, pl.ds(part * half + first * lanes, frames * lanes)]
                    sem = in_sems.at[(index * splits + q) * 2 + part]
                    coming[at].append(pltpu.make_async_copy(src, dst, sem))
        for copies in coming:
            for copy in copies:
                copy.start()

        def rows_of(i):
            return pl.ds(pl.multiple_of(((here_ref[0] ^ (i // splits)) * splits + i % splits) * block, block), block)

        inverse = 1.0 / half
        going = [[], []]
        slot = 0
        for i in range(count):
            for copy in coming[i]:
                copy.wait()
            left = held[i].reshape(block, 2 * half)
            turned[:, :half] = left[:, half:]
            turned[:, half:] = -left[:, :half]
            at_i = rows_of(i)
            for j in range(i + 1):
                right = held[j].reshape(block, 2 * half)
                at_j = rows_of(j)
                for copy in going[slot]:
                    copy.wait()
                going[slot] = []
                for part, rows in enumerate((left, turned[...])):
                    got = lax.dot_general(rows, right, NT, preferred_element_type=jnp.float32) * inverse
                    made[slot, part, 0] = got
                    going[slot].append(
                        pltpu.make_async_copy(
                            made.at[slot, part, 0], out.at[part, at_i, at_j], out_sems.at[slot, part, 0]
                        )
                    )
                    if i != j:
                        made[slot, part, 1] = got.T if part == 0 else -got.T
                        going[slot].append(
                            pltpu.make_async_copy(
                                made.at[slot, part, 1], out.at[part, at_j, at_i], out_sems.at[slot, part, 1]
                            )
                        )
                for copy in going[slot]:
                    copy.start()
                slot = 1 - slot
        for copies in going:
            for copy in copies:
                copy.wait()

    return pl.pallas_call(
        kernel,
        in_specs=[pl.BlockSpec(memory_space=pltpu.SMEM)] + [pl.BlockSpec(memory_space=pl.ANY)] * len(pieces),
        out_specs=pl.BlockSpec(memory_space=pl.ANY),
        out_shape=jax.ShapeDtypeStruct((2, signals, signals), jnp.float32),
        scratch_shapes=[
            pltpu.VMEM((count, each, halves, sub, 2 * half), jnp.bfloat16),
            pltpu.VMEM((block, 2 * half), jnp.bfloat16),
            pltpu.VMEM((2, 2, 2, block, block), jnp.float32),
            pltpu.SemaphoreType.DMA((2 * splits * len(pieces),)),
            pltpu.SemaphoreType.DMA((2, 2, 2)),
        ],
        compiler_params=pltpu.CompilerParams(vmem_limit_bytes=VMEM),
        cost_estimate=NO_COST,
    )(here, *[piece[0] for piece in pieces])


def weight_kernel(channel, delays, gains, out):
    beams = delays.shape[0]
    turns = delays[...] * (channel[pl.program_id(0)].astype(jnp.float32) * (1.0 / NCH))
    part = turns - jnp.floor(turns + 0.5)
    square = part * part
    cos_t = jnp.full_like(part, TWO_PI**16 / math.factorial(16))
    sin_t = jnp.full_like(part, -(TWO_PI**15) / math.factorial(15))
    for power in range(14, -1, -2):
        sign = -1.0 if power % 4 == 2 else 1.0
        cos_t = cos_t * square + sign * TWO_PI**power / math.factorial(power)
        if power > 0:
            sign = -1.0 if (power - 1) % 4 == 3 else 1.0
            sin_t = sin_t * square + sign * TWO_PI ** (power - 1) / math.factorial(power - 1)
    scaled = gains[...] * (1.0 / math.sqrt(gains.shape[1]))
    out[0, :beams] = (scaled * cos_t).astype(out.dtype)
    out[0, beams:] = (-scaled * sin_t * part).astype(out.dtype)


def beam_weights(channel, delays, gains):
    beams, listed = delays.shape
    slots = channel.shape[0]
    return pl.pallas_call(
        weight_kernel,
        grid=(slots,),
        in_specs=[
            pl.BlockSpec(memory_space=pltpu.SMEM),
            pl.BlockSpec(delays.shape, lambda i: (0, 0)),
            pl.BlockSpec(gains.shape, lambda i: (0, 0)),
        ],
        out_specs=pl.BlockSpec((1, 2 * beams, listed), lambda i: (i, 0, 0)),
        out_shape=jax.ShapeDtypeStruct((slots, 2 * beams, listed), jnp.bfloat16),
        cost_estimate=NO_COST,
    )(channel, delays, gains)


def combine(spectra, chooser, weights, sub):
    slots, beams2, listed = weights.shape
    beams = beams2 // 2
    rows = 2 * slots
    senders = spectra.shape[0]
    partners = spectra.shape[1] // rows
    halves = spectra.shape[2] // (FRAMES * sub)
    count = LANES // sub
    inner = senders // count
    groups = partners * halves * inner
    tiles = 2 * listed // LANES

    def kernel(spectrum, choose, weight, out, ordered, picked):
        lane_ids = lax.broadcasted_iota(jnp.int32, (rows, LANES), 1)
        for s in range(partners):
            for h in range(halves):
                for q in range(inner):
                    for t in range(FRAMES // count):
                        lane = h * FRAMES * sub + t * LANES
                        pieces = [
                            spectrum[q * count + i, s * rows : (s + 1) * rows, lane : lane + LANES].astype(jnp.float32)
                            for i in range(count)
                        ]
                        for f, piece in enumerate(swap_blocks(pieces, lane_ids)):
                            top = (t * count + f) * rows
                            ordered[(s * halves + h) * inner + q, top : top + rows, :] = piece
        acc = None
        for q in range(groups):
            term = jnp.dot(
                ordered[q].astype(jnp.bfloat16),
                choose[q * LANES : (q + 1) * LANES, :],
                preferred_element_type=jnp.float32,
            )
            acc = term if acc is None else acc + term
        for lane in range(tiles):
            picked[lane] = acc[:, lane * LANES : (lane + 1) * LANES]
        for i in range(slots):
            chosen = [
                jnp.concatenate(
                    [
                        picked[p * tiles // 2 + lane, pl.ds(part * slots + i, FRAMES, rows), :]
                        for lane in range(tiles // 2)
                    ],
                    axis=1,
                )
                for p in range(2)
                for part in range(2)
            ]
            stacked = jnp.concatenate(chosen, axis=0).astype(jnp.bfloat16)
            mixed = lax.dot_general(stacked, weight[i], NT, preferred_element_type=jnp.float32)
            for p in range(2):
                at = 2 * FRAMES * p
                of_re, of_im = mixed[at : at + FRAMES], mixed[at + FRAMES : at + 2 * FRAMES]
                out[0, i, 0, :, p * beams : (p + 1) * beams] = of_re[:, :beams] - of_im[:, beams:]
                out[0, i, 1, :, p * beams : (p + 1) * beams] = of_im[:, :beams] + of_re[:, beams:]

    return pl.pallas_call(
        kernel,
        out_shape=jax.ShapeDtypeStruct((1, slots, 2, FRAMES, 2 * beams), jnp.float32),
        scratch_shapes=[
            pltpu.VMEM((groups, FRAMES * rows, LANES), jnp.float32),
            pltpu.VMEM((tiles, FRAMES * rows, LANES), jnp.float32),
        ],
        compiler_params=pltpu.CompilerParams(vmem_limit_bytes=VMEM),
        cost_estimate=NO_COST,
    )(spectra, chooser, weights)


def body(volts, prototype, beam_channels, station_index, delays, gains, assign):
    sig_dev = volts.shape[1]
    far, near, sb_count = lax.axis_size("far"), lax.axis_size("near"), lax.axis_size("sb")
    far_here, near_here, sb_here = [lax.axis_index(name).astype(jnp.int32) for name in ("far", "near", "sb")]
    st_count = far * near
    plane = near * sb_count
    depth = NCH // RADIX
    bands = depth // LANES
    fine = NCH // sb_count // RADIX // st_count
    partner = far_here ^ jnp.arange(far, dtype=jnp.int32)
    stations = (partner[:, None] * near + jnp.arange(near, dtype=jnp.int32)[None, :]).reshape(-1)

    def spread(*ids):
        total = ids[0]
        for more in ids[1:]:
            total = total[..., None] + more
        return total.reshape(-1)

    out_ids = spread(
        jnp.arange(bands, dtype=jnp.int32)[:, None] * LANES + (stations * fine)[None, :],
        jnp.arange(fine, dtype=jnp.int32),
    )
    table = transform_table(out_ids)
    turn_c, turn_s = phase(
        jnp.arange(RADIX, dtype=jnp.int32)[:, None] * jnp.arange(depth, dtype=jnp.int32)[None, :], NCH
    )
    taps_wide = jnp.broadcast_to(prototype[:, None, :], (prototype.shape[0], 8, NCH))

    def cross(x):
        pairs = [(i, i ^ (near + near // 2)) for i in range(st_count)]
        return lax.ppermute(x, ("far", "near"), pairs)

    def in_plane(xs, axis):
        joined = xs[0] if len(xs) == 1 else jnp.concatenate(xs, axis=axis)
        return lax.all_to_all(joined, ("near", "sb"), split_axis=0, concat_axis=0, tiled=True)

    share = sig_dev // sb_count
    sub = min(share, ROWS)
    halves = max(1, share // ROWS)
    inside = (sb_here * share) % ROWS
    unit = max(1, LANES * st_count * sb_count // NCH)
    early = FRAMES * 3 // 8 // unit * unit
    plan = [(0, 0, early), (0, early, FRAMES - early)] + [(h, 0, FRAMES) for h in range(1, halves)]
    group = NCH // (st_count * sb_count)

    def channels_of(c, table):
        which, first, frames = plan[c]
        row_block = (sb_here * share // ROWS + which)[None]
        *outs, kept = channelise(row_block, volts, taps_wide, turn_c, turn_s, table, first, frames, far)
        if sub < ROWS:
            outs = [lax.dynamic_slice_in_dim(x, inside, sub, axis=2) for x in outs]
        inner = st_count // RADIX
        if inner > 1:
            outs = [
                x.reshape(near // inner, sb_count, sub, 2 * frames, RADIX, inner, fine).transpose(0, 5, 1, 2, 3, 4, 6)
                for x in outs
            ]
        return [x.reshape(plane, sub, -1) for x in outs], kept

    barrier = lax.optimization_barrier
    lists = (assign, beam_channels, station_index)
    outs, kept = channels_of(0, table)
    branches, arrived, waiting, pieces = [kept], [], [], []
    for c in range(len(plan)):
        outs, waiting, table, lists, arrived[-1:] = barrier((outs, waiting, table, lists, arrived[-1:]))
        lane = 0
        for s, k in [(1, c - 1)][: len(waiting)] + [(0, c)]:
            pieces.append((c, lane, s, *plan[k]))
            lane += 2 * plan[k][2] * group
        arrived.append(in_plane(waiting + [outs[0]], 2))
        waiting = [cross(outs[1])]
        if c + 1 < len(plan):
            outs, kept = channels_of(c + 1, table)
            branches.append(kept)
    pieces.append((len(plan), 0, 1, *plan[-1]))
    assign, beam_channels, station_index = lists

    per_dev = SLOTS // st_count
    owners = assign[:, 0]
    taken = (owners[:, None] == jnp.arange(sb_count, dtype=jnp.int32)[None, :]).astype(jnp.int32)
    position = jnp.sum(taken * jnp.cumsum(taken, axis=0), axis=1) - 1
    place = owners * SLOTS + position
    slot_ids = spread(
        stations * per_dev,
        jnp.arange(sb_count, dtype=jnp.int32) * SLOTS,
        jnp.arange(per_dev, dtype=jnp.int32),
    )
    picker = (place[None, :] == slot_ids[:, None]).astype(jnp.int32)
    filled = jnp.sum(picker, axis=1)
    slot_channel = jnp.sum(picker * beam_channels[None, :], axis=1)

    def by_row(values):
        values = values.reshape(st_count * sb_count, 1, per_dev)
        return jnp.broadcast_to(values, (st_count * sb_count, 2, per_dev)).reshape(-1)

    turned = jnp.broadcast_to(jnp.arange(2, dtype=jnp.int32)[None, :, None], (st_count * sb_count, 2, per_dev))
    mine = lax.dynamic_slice_in_dim(slot_channel, (near_here * sb_count + sb_here) * per_dev, per_dev)
    tables = slot_tables(by_row(slot_channel), by_row(filled), turned.reshape(-1))
    spectra = slot_spectra(tables, branches, 2 * per_dev, far)
    if sub < ROWS:
        spectra = [
            lax.dynamic_slice_in_dim(x.reshape(plane, 2 * per_dev, FRAMES, ROWS), inside, sub, axis=3).reshape(
                plane, 2 * per_dev, -1
            )
            for x in spectra
        ]
    spectra, waiting, mine, arrived[-1:] = barrier((spectra, waiting, mine, arrived[-1:]))
    arrived.append(in_plane(waiting, 2))
    slot_crossed = cross(spectra[1])
    weights = beam_weights(mine, delays, gains)
    spectra, slot_crossed, weights, arrived[-1:] = barrier((spectra, slot_crossed, weights, arrived[-1:]))
    slot_received = in_plane([spectra[0], slot_crossed], 1)
    if halves == 1:
        arrived = [x.reshape(-1, min(256, plane * sub), x.shape[2]) for x in arrived]
    visibility = correlate(far_here[None], [(arrived[p[0]], *p[1:]) for p in pieces], far, halves, group)

    by_way = jnp.arange(near, dtype=jnp.int32)[None, :] ^ (jnp.arange(far, dtype=jnp.int32)[:, None] * (near // 2))
    signal_ids = (
        (partner[:, None] * near + by_way)[:, None, :, None, None] * sig_dev
        + jnp.arange(halves, dtype=jnp.int32)[:, None, None, None] * sub
        + jnp.arange(sb_count, dtype=jnp.int32)[:, None] * share
        + jnp.arange(sub, dtype=jnp.int32)
    ).reshape(-1)
    wanted = (station_index[None, :] * 2 + jnp.arange(2, dtype=jnp.int32)[:, None]).reshape(-1)
    chooser = (signal_ids[:, None] == wanted[None, :]).astype(jnp.bfloat16)

    signals = visibility.shape[1]
    beam_out = combine(slot_received, chooser, weights, sub)
    return (visibility.reshape(2, 1, 1, signals, signals), beam_out)


def solution(mesh):
    st_count, sb_count = mesh.shape["st"], mesh.shape["sb"]
    far = 2
    planes = Mesh(mesh.devices.reshape(far, st_count // far, sb_count), ("far", "near", "sb"))
    st = ("far", "near")
    in_specs = (P(None, st, None), P(), P(), P(), P(), P(), P())
    out_specs = (P(None, "sb", st, None, None), P("sb", st, None, None, None))
    return jax.shard_map(body, mesh=planes, in_specs=in_specs, out_specs=out_specs, check_vma=False)
```

```python
import functools
import math

import jax
import jax.numpy as jnp
import numpy as np
from jax import lax
from jax.experimental import pallas as pl
from jax.experimental.pallas import tpu as pltpu
from jax.sharding import PartitionSpec as P

NCH = 4096
FRAMES = 16
SLOTS = 160
RADIX = 8
LANES = 128
ROWS = 16
EARLY = 4
VMEM = 56 * 1024 * 1024

NO_COST = pl.CostEstimate(flops=1, bytes_accessed=1, transcendentals=0)

TWO_PI = 2.0 * math.pi
NT = (((1,), (1,)), ((), ()))


def busy(share):
    return pl.CostEstimate(flops=int(share * 1e10), bytes_accessed=1, transcendentals=0)


def phase(turns, length):
    angles = (turns % length).astype(jnp.float32) * (TWO_PI / length)
    return jnp.cos(angles), jnp.sin(angles)


def transform_tables():
    depth = NCH // RADIX
    ids = np.arange(depth)
    angles = 2 * np.pi / depth * (ids[:, None] * ids[None, :] % depth)
    turns = 2 * np.pi / NCH * (np.arange(RADIX)[:, None] * ids[None, :])
    scale = 1.0 / math.sqrt(NCH)
    both = (np.cos(angles) * scale, np.sin(angles) * scale, np.cos(turns), np.sin(turns))
    return [jnp.asarray(x.astype(np.float32)) for x in both]


def radix8(re, im):
    half = math.sqrt(0.5)

    def four(xr, xi):
        ar, ai, br, bi = xr[0] + xr[2], xi[0] + xi[2], xr[0] - xr[2], xi[0] - xi[2]
        cr, ci, dr, di = xr[1] + xr[3], xi[1] + xi[3], xr[1] - xr[3], xi[1] - xi[3]
        return [ar + cr, br + di, ar - cr, br - di], [ai + ci, bi - dr, ai - ci, bi + dr]

    er, ei = four(re[0::2], im[0::2])
    odd_r, odd_i = four(re[1::2], im[1::2])
    tr = [odd_r[0], (odd_r[1] + odd_i[1]) * half, odd_i[2], (odd_i[3] - odd_r[3]) * half]
    ti = [odd_i[0], (odd_i[1] - odd_r[1]) * half, -odd_r[2], (odd_r[3] + odd_i[3]) * -half]
    return (
        [e + t for e, t in zip(er, tr)] + [e - t for e, t in zip(er, tr)],
        [e + t for e, t in zip(ei, ti)] + [e - t for e, t in zip(ei, ti)],
    )


def swap_blocks(parts, lane_ids):
    count = len(parts)
    width = LANES // count
    parts = list(parts)
    step = 1
    while step < count:
        keep = (lane_ids // width) % (2 * step) < step
        for b in range(count):
            if b & step == 0:
                low, high = parts[b], parts[b + step]
                parts[b] = jnp.where(keep, low, pltpu.roll(high, step * width, 1))
                parts[b + step] = jnp.where(keep, pltpu.roll(low, LANES - step * width, 1), high)
        step *= 2
    return parts


def gather_blocks(parts, lane_ids):
    count = len(parts)
    width = LANES // count
    turned = [parts[0]] + [pltpu.roll(parts[b], b * width, 1) for b in range(1, count)]
    turned = [turned[-b % count] for b in range(count)]
    step = 1
    while step < count:
        moved = (lane_ids // width) & step != 0
        turned = [jnp.where(moved, turned[(g - step) % count], turned[g]) for g in range(count)]
        step *= 2
    return [turned[0]] + [pltpu.roll(turned[g], LANES - g * width, 1) for g in range(1, count)]


def channel_kernel(first, row_block, volts, prototype, cosines, sines, turn_c, turn_s, out, branches, *scratch):
    taps_wide, table, filtered, product = scratch
    taps = taps_wide.shape[0]
    length = taps_wide.shape[2]
    frames = filtered.shape[2]
    depth = length // RADIX
    bands = depth // LANES
    for t in range(taps):
        taps_wide[t] = jnp.broadcast_to(prototype[t : t + 1, :], taps_wide.shape[1:])
    cos_t, sin_t = cosines[...].astype(table.dtype), sines[...].astype(table.dtype)
    table[:depth, :depth] = cos_t
    table[:depth, depth:] = -sin_t
    table[depth:, :depth] = sin_t
    table[depth:, depth:] = cos_t

    def column(j, carry):
        lane = pl.multiple_of(j * LANES, LANES)

        def strip(n1, inner):
            base = pl.multiple_of(n1 * depth + j * LANES, LANES)
            for part in range(2):
                sums = [None] * frames
                for seg in range(frames + taps - 1):
                    start = pl.multiple_of((first + seg) * length + base, LANES)
                    value = volts[part, :, pl.ds(start, LANES)].astype(jnp.float32)
                    for f in range(max(0, seg - taps + 1), min(frames, seg + 1)):
                        coef = taps_wide[seg - f, :, pl.ds(base, LANES)]
                        term = value * jnp.concatenate([coef, coef], axis=0)
                        sums[f] = term if sums[f] is None else sums[f] + term
                    if seg >= taps - 1:
                        filtered[part, n1, seg - taps + 1] = sums[seg - taps + 1]
            return inner

        lax.fori_loop(0, RADIX, strip, 0)

        def butterfly(f, inner):
            re, im = radix8(
                [filtered[0, n1, f] for n1 in range(RADIX)],
                [filtered[1, n1, f] for n1 in range(RADIX)],
            )
            for b in range(RADIX):
                turned_r, turned_i = re[b], im[b]
                if b > 0:
                    cos_t, sin_t = turn_c[b : b + 1, pl.ds(lane, LANES)], turn_s[b : b + 1, pl.ds(lane, LANES)]
                    turned_r, turned_i = re[b] * cos_t + im[b] * sin_t, im[b] * cos_t - re[b] * sin_t
                branches[b, f, :, pl.ds(lane, LANES)] = turned_r.astype(branches.dtype)
                branches[b, f, :, pl.ds(pl.multiple_of(depth + lane, LANES), LANES)] = turned_i.astype(branches.dtype)
            return inner

        lax.fori_loop(0, frames, butterfly, 0)
        return carry

    lax.fori_loop(0, bands, column, 0)

    def multiply(b, carry):
        rows = branches[b].reshape(frames * ROWS, 2 * depth)
        product[b] = jnp.dot(rows, table[...], preferred_element_type=jnp.float32)
        return carry

    lax.fori_loop(0, RADIX, multiply, 0)
    lane_ids = lax.broadcasted_iota(jnp.int32, (ROWS, LANES), 1)

    def regroup(f, carry):
        top = pl.multiple_of(f * ROWS, ROWS)
        for part in range(2):
            for band in range(bands):
                lane = part * depth + band * LANES
                pieces = [product[b, pl.ds(top, ROWS), lane : lane + LANES] for b in range(RADIX)]
                for g, piece in enumerate(gather_blocks(pieces, lane_ids)):
                    at = pl.multiple_of((part * frames + f) * LANES, LANES)
                    out[g, band, :, pl.ds(at, LANES)] = piece.astype(out.dtype)
        return carry

    lax.fori_loop(0, frames, regroup, 0)


def channelise(row_block, volts, prototype, tables, first, frames):
    taps = prototype.shape[0]
    length = volts.shape[2] if first > 0 else (frames + taps - 1) * NCH
    depth = NCH // RADIX
    bands = depth // LANES
    wide = 2 * frames * LANES
    return pl.pallas_call(
        functools.partial(channel_kernel, first),
        grid_spec=pltpu.PrefetchScalarGridSpec(
            num_scalar_prefetch=1,
            grid=(1,),
            in_specs=[
                pl.BlockSpec((2, ROWS, length), lambda i, row: (0, row[0], 0)),
            ]
            + [pl.BlockSpec(x.shape, lambda i, row: (0, 0)) for x in (prototype, *tables)],
            out_specs=[
                pl.BlockSpec((RADIX, bands, ROWS, wide), lambda i, row: (0, 0, 0, 0)),
                pl.BlockSpec((RADIX, frames, ROWS, 2 * depth), lambda i, row: (0, 0, 0, 0)),
            ],
            scratch_shapes=[
                pltpu.VMEM((taps, 8, NCH), jnp.float32),
                pltpu.VMEM((2 * depth, 2 * depth), jnp.bfloat16),
                pltpu.VMEM((2, RADIX, frames, ROWS, LANES), jnp.float32),
                pltpu.VMEM((RADIX, frames * ROWS, 2 * depth), jnp.float32),
            ],
        ),
        out_shape=[
            jax.ShapeDtypeStruct((RADIX, bands, ROWS, wide), jnp.bfloat16),
            jax.ShapeDtypeStruct((RADIX, frames, ROWS, 2 * depth), jnp.bfloat16),
        ],
        compiler_params=pltpu.CompilerParams(vmem_limit_bytes=VMEM),
        cost_estimate=busy(frames / FRAMES),
    )(row_block, volts, prototype, *tables)


def slot_kernel(row_branch, hi_c, hi_s, lo_c, lo_s, *rest):
    chunks, (out, table, total) = rest[:-3], rest[-3:]
    depth = chunks[0].shape[3] // 2
    for a in range(hi_c.shape[1]):
        high_c, high_s = hi_c[:, a : a + 1], hi_s[:, a : a + 1]
        table[:, a * LANES : (a + 1) * LANES] = (high_c * lo_c[...] - high_s * lo_s[...]).astype(table.dtype)
        table[:, depth + a * LANES : depth + (a + 1) * LANES] = (
            high_s * lo_c[...] + high_c * lo_s[...]
        ).astype(table.dtype)
    total[...] = jnp.zeros_like(total)

    def branch(b, carry):
        rows = jnp.concatenate([c[b].reshape(c.shape[1] * c.shape[2], c.shape[3]) for c in chunks], axis=0)
        got = lax.dot_general(table[...], rows, NT, preferred_element_type=jnp.float32)
        total[...] = jnp.where(row_branch[...] == b, got, total[...])
        return carry

    lax.fori_loop(0, RADIX, branch, 0)
    per = out.shape[1]
    for d in range(out.shape[0]):
        out[d] = total[d * per : (d + 1) * per].astype(out.dtype)


def slot_tables(row_channel, row_filled, row_turned):
    depth = NCH // RADIX
    coarse = jnp.arange(depth // LANES, dtype=jnp.int32) * LANES
    fine = jnp.arange(LANES, dtype=jnp.int32)
    whole = row_channel - row_channel % RADIX
    hi_c, hi_s = phase(whole[:, None] * coarse[None, :] + row_turned[:, None] * (NCH // 4), NCH)
    lo_c, lo_s = phase(whole[:, None] * fine[None, :], NCH)
    scaling = row_filled.astype(jnp.float32)[:, None] * (1.0 / math.sqrt(NCH))
    return (row_channel % RADIX)[:, None], hi_c * scaling, hi_s * scaling, lo_c, lo_s


def slot_spectra(tables, chunks, per):
    rows = tables[0].shape[0]
    samples = sum(c.shape[1] * c.shape[2] for c in chunks)
    return pl.pallas_call(
        slot_kernel,
        out_shape=jax.ShapeDtypeStruct((rows // per, per, samples), jnp.bfloat16),
        scratch_shapes=[
            pltpu.VMEM((rows, chunks[0].shape[3]), jnp.bfloat16),
            pltpu.VMEM((rows, samples), jnp.float32),
        ],
        compiler_params=pltpu.CompilerParams(vmem_limit_bytes=VMEM),
        cost_estimate=busy(1),
    )(*tables, *chunks)


def correlate(pieces, halves, lanes):
    senders, sub, _ = pieces[0][0].shape
    half = FRAMES * lanes
    signals = senders * halves * sub
    count = max(1, signals // 256)
    each = senders // count
    block = each * halves * sub

    def kernel(*refs):
        parts, (out, held, turned, made, in_sems, out_sems) = refs[: len(pieces)], refs[len(pieces) :]
        coming = [[] for _ in range(count)]
        for index, (_, which, first, frames) in enumerate(pieces):
            for q in range(count):
                for part in range(2):
                    src = parts[index].at[pl.ds(q * each, each), :, pl.ds(part * frames * lanes, frames * lanes)]
                    dst = held.at[q, :, which, :, pl.ds(part * half + first * lanes, frames * lanes)]
                    sem = in_sems.at[(index * count + q) * 2 + part]
                    coming[q].append(pltpu.make_async_copy(src, dst, sem))
        for copies in coming:
            for copy in copies:
                copy.start()

        def rows_of(i):
            return pl.ds(i * block, block)

        inverse = 1.0 / half
        going = [[], []]
        slot = 0
        for i in range(count):
            for copy in coming[i]:
                copy.wait()
            left = held[i].reshape(block, 2 * half)
            turned[:, :half] = left[:, half:]
            turned[:, half:] = -left[:, :half]
            at_i = rows_of(i)
            for j in range(i + 1):
                right = held[j].reshape(block, 2 * half)
                at_j = rows_of(j)
                for copy in going[slot]:
                    copy.wait()
                going[slot] = []
                for part, rows in enumerate((left, turned[...])):
                    got = lax.dot_general(rows, right, NT, preferred_element_type=jnp.float32) * inverse
                    made[slot, part, 0] = got
                    going[slot].append(
                        pltpu.make_async_copy(
                            made.at[slot, part, 0], out.at[part, at_i, at_j], out_sems.at[slot, part, 0]
                        )
                    )
                    if i != j:
                        made[slot, part, 1] = got.T if part == 0 else -got.T
                        going[slot].append(
                            pltpu.make_async_copy(
                                made.at[slot, part, 1], out.at[part, at_j, at_i], out_sems.at[slot, part, 1]
                            )
                        )
                for copy in going[slot]:
                    copy.start()
                slot = 1 - slot
        for copies in going:
            for copy in copies:
                copy.wait()

    return pl.pallas_call(
        kernel,
        in_specs=[pl.BlockSpec(memory_space=pl.ANY)] * len(pieces),
        out_specs=pl.BlockSpec(memory_space=pl.ANY),
        out_shape=jax.ShapeDtypeStruct((2, signals, signals), jnp.float32),
        scratch_shapes=[
            pltpu.VMEM((count, each, halves, sub, 2 * half), jnp.bfloat16),
            pltpu.VMEM((block, 2 * half), jnp.bfloat16),
            pltpu.VMEM((2, 2, 2, block, block), jnp.float32),
            pltpu.SemaphoreType.DMA((2 * count * len(pieces),)),
            pltpu.SemaphoreType.DMA((2, 2, 2)),
        ],
        compiler_params=pltpu.CompilerParams(vmem_limit_bytes=VMEM),
        cost_estimate=NO_COST,
    )(*[piece[0] for piece in pieces])


def weight_kernel(channel, delays, gains, out):
    beams = delays.shape[0]
    turns = delays[...] * (channel[pl.program_id(0)].astype(jnp.float32) * (1.0 / NCH))
    part = turns - jnp.floor(turns + 0.5)
    square = part * part
    cos_t = jnp.full_like(part, TWO_PI**16 / math.factorial(16))
    sin_t = jnp.full_like(part, -(TWO_PI**15) / math.factorial(15))
    for power in range(14, -1, -2):
        sign = -1.0 if power % 4 == 2 else 1.0
        cos_t = cos_t * square + sign * TWO_PI**power / math.factorial(power)
        if power > 0:
            sign = -1.0 if (power - 1) % 4 == 3 else 1.0
            sin_t = sin_t * square + sign * TWO_PI ** (power - 1) / math.factorial(power - 1)
    scaled = gains[...] * (1.0 / math.sqrt(gains.shape[1]))
    out[0, :beams] = (scaled * cos_t).astype(out.dtype)
    out[0, beams:] = (-scaled * sin_t * part).astype(out.dtype)


def beam_weights(channel, delays, gains):
    beams, listed = delays.shape
    slots = channel.shape[0]
    return pl.pallas_call(
        weight_kernel,
        grid=(slots,),
        in_specs=[
            pl.BlockSpec(memory_space=pltpu.SMEM),
            pl.BlockSpec(delays.shape, lambda i: (0, 0)),
            pl.BlockSpec(gains.shape, lambda i: (0, 0)),
        ],
        out_specs=pl.BlockSpec((1, 2 * beams, listed), lambda i: (i, 0, 0)),
        out_shape=jax.ShapeDtypeStruct((slots, 2 * beams, listed), jnp.bfloat16),
        cost_estimate=NO_COST,
    )(channel, delays, gains)


def combine(spectra, chooser, weights, sub):
    slots, beams2, listed = weights.shape
    beams = beams2 // 2
    rows = 2 * slots
    senders = spectra.shape[0]
    halves = spectra.shape[2] // (FRAMES * sub)
    count = LANES // sub
    inner = senders // count
    groups = halves * inner
    tiles = 2 * listed // LANES

    def kernel(spectrum, choose, weight, out, ordered, picked):
        lane_ids = lax.broadcasted_iota(jnp.int32, (rows, LANES), 1)
        for h in range(halves):
            for q in range(inner):
                for t in range(FRAMES // count):
                    lane = h * FRAMES * sub + t * LANES
                    pieces = [
                        spectrum[q * count + i, :, lane : lane + LANES].astype(jnp.float32) for i in range(count)
                    ]
                    for f, piece in enumerate(swap_blocks(pieces, lane_ids)):
                        top = (t * count + f) * rows
                        ordered[h * inner + q, top : top + rows, :] = piece
        acc = None
        for q in range(groups):
            term = jnp.dot(
                ordered[q].astype(jnp.bfloat16),
                choose[q * LANES : (q + 1) * LANES, :],
                preferred_element_type=jnp.float32,
            )
            acc = term if acc is None else acc + term
        for lane in range(tiles):
            picked[lane] = acc[:, lane * LANES : (lane + 1) * LANES]
        for i in range(slots):
            chosen = [
                jnp.concatenate(
                    [
                        picked[p * tiles // 2 + lane, pl.ds(part * slots + i, FRAMES, rows), :]
                        for lane in range(tiles // 2)
                    ],
                    axis=1,
                )
                for p in range(2)
                for part in range(2)
            ]
            stacked = jnp.concatenate(chosen, axis=0).astype(jnp.bfloat16)
            mixed = lax.dot_general(stacked, weight[i], NT, preferred_element_type=jnp.float32)
            for p in range(2):
                at = 2 * FRAMES * p
                of_re, of_im = mixed[at : at + FRAMES], mixed[at + FRAMES : at + 2 * FRAMES]
                out[0, i, 0, :, p * beams : (p + 1) * beams] = of_re[:, :beams] - of_im[:, beams:]
                out[0, i, 1, :, p * beams : (p + 1) * beams] = of_im[:, :beams] + of_re[:, beams:]

    return pl.pallas_call(
        kernel,
        out_shape=jax.ShapeDtypeStruct((1, slots, 2, FRAMES, 2 * beams), jnp.float32),
        scratch_shapes=[
            pltpu.VMEM((groups, FRAMES * rows, LANES), jnp.float32),
            pltpu.VMEM((tiles, FRAMES * rows, LANES), jnp.float32),
        ],
        compiler_params=pltpu.CompilerParams(vmem_limit_bytes=VMEM),
        cost_estimate=NO_COST,
    )(spectra, chooser, weights)


def body(volts, prototype, beam_channels, station_index, delays, gains, assign):
    sig_dev = volts.shape[1]
    st_count, sb_count = lax.axis_size("st"), lax.axis_size("sb")
    st_here, sb_here = lax.axis_index("st").astype(jnp.int32), lax.axis_index("sb").astype(jnp.int32)
    devices = st_count * sb_count
    group = NCH // devices
    fine = group // RADIX
    constants = transform_tables()
    barrier = lax.optimization_barrier

    def exchange(x):
        return lax.all_to_all(x, ("st", "sb"), split_axis=0, concat_axis=0, tiled=True)

    share = sig_dev // sb_count
    sub = min(share, ROWS)
    halves = max(1, share // ROWS)
    inside = (sb_here * share) % ROWS
    unit = max(1, LANES // group)
    early = max(unit, EARLY // unit * unit)
    plan = [(0, 0, early), (0, early, FRAMES - early)] + [(h, 0, FRAMES) for h in range(1, halves)]

    def channels_of(c, here):
        which, first, frames = plan[c]
        row_block = (here * share // ROWS + which)[None]
        out, kept = channelise(row_block, volts, prototype, constants, first, frames)
        if sub < ROWS:
            out = lax.dynamic_slice_in_dim(out, inside, sub, axis=2)
        inner = st_count // RADIX
        if inner > 1:
            out = out.reshape(RADIX, sb_count, sub, 2 * frames, RADIX, inner, fine).transpose(0, 5, 1, 2, 3, 4, 6)
        return out.reshape(devices, sub, -1), kept

    lists = (assign, beam_channels, station_index)
    here = sb_here
    out, kept = channels_of(0, here)
    branches, arrived = [kept], []
    for c in range(1, len(plan)):
        out, here, lists, arrived[-1:] = barrier((out, here, lists, arrived[-1:]))
        arrived.append(exchange(out))
        out, kept = channels_of(c, here)
        branches.append(kept)

    assign, beam_channels, station_index = barrier((lists, kept))[0]
    per_dev = SLOTS // st_count
    owners = assign[:, 0]
    taken = (owners[:, None] == jnp.arange(sb_count, dtype=jnp.int32)[None, :]).astype(jnp.int32)
    position = jnp.sum(taken * jnp.cumsum(taken, axis=0), axis=1) - 1
    place = owners * SLOTS + position
    slot_ids = (
        jnp.arange(st_count, dtype=jnp.int32)[:, None, None] * per_dev
        + jnp.arange(sb_count, dtype=jnp.int32)[:, None] * SLOTS
        + jnp.arange(per_dev, dtype=jnp.int32)
    ).reshape(-1)
    picker = (place[None, :] == slot_ids[:, None]).astype(jnp.int32)
    filled = jnp.sum(picker, axis=1)
    slot_channel = jnp.sum(picker * beam_channels[None, :], axis=1)

    def by_row(values):
        return jnp.broadcast_to(values.reshape(devices, 1, per_dev), (devices, 2, per_dev)).reshape(-1)

    turned = jnp.broadcast_to(jnp.arange(2, dtype=jnp.int32)[None, :, None], (devices, 2, per_dev)).reshape(-1)
    mine = lax.dynamic_slice_in_dim(slot_channel, (st_here * sb_count + sb_here) * per_dev, per_dev)
    tables = slot_tables(by_row(slot_channel), by_row(filled), turned)
    spectra = slot_spectra(tables, branches, 2 * per_dev)
    if sub < ROWS:
        spectra = spectra.reshape(devices, 2 * per_dev, FRAMES, ROWS)
        spectra = lax.dynamic_slice_in_dim(spectra, inside, sub, axis=3).reshape(devices, 2 * per_dev, -1)

    out, spectra, mine, arrived[-1:] = barrier((out, spectra, mine, arrived[-1:]))
    arrived.append(exchange(out))
    weights = beam_weights(mine, delays, gains)
    signal_ids = (
        jnp.arange(halves, dtype=jnp.int32)[:, None, None] * sub
        + jnp.arange(devices, dtype=jnp.int32)[:, None] * share
        + jnp.arange(sub, dtype=jnp.int32)
    ).reshape(-1)
    wanted = (station_index[None, :] * 2 + jnp.arange(2, dtype=jnp.int32)[:, None]).reshape(-1)
    chooser = (signal_ids[:, None] == wanted[None, :]).astype(jnp.bfloat16)

    spectra, weights, chooser, arrived[-1:] = barrier((spectra, weights, chooser, arrived[-1:]))
    slot_received = exchange(spectra)
    if halves == 1:
        arrived = [x.reshape(-1, min(256, devices * sub), x.shape[2]) for x in arrived]
    visibility = correlate([(x, *part) for x, part in zip(arrived, plan)], halves, group)
    signals = visibility.shape[1]
    beam_out = combine(slot_received, chooser, weights, sub)
    return (visibility.reshape(2, 1, 1, signals, signals), beam_out)


def solution(mesh):
    in_specs = (P(None, "st", None), P(), P(), P(), P(), P(), P())
    out_specs = (P(None, "sb", "st", None, None), P("sb", "st", None, None, None))
    return jax.shard_map(body, mesh=mesh, in_specs=in_specs, out_specs=out_specs, check_vma=False)
```

```python
import functools
import math

import jax
import jax.numpy as jnp
import numpy as np
from jax import lax
from jax.experimental import pallas as pl
from jax.experimental.pallas import tpu as pltpu
from jax.sharding import PartitionSpec as P

NCH = 4096
FRAMES = 16
SLOTS = 160
RADIX = 8
LANES = 128
ROWS = 16
EARLY = 4
VMEM = 56 * 1024 * 1024

NO_COST = pl.CostEstimate(flops=1, bytes_accessed=1, transcendentals=0)

TWO_PI = 2.0 * math.pi
NT = (((1,), (1,)), ((), ()))


def busy(share):
    return pl.CostEstimate(flops=int(share * 1e10), bytes_accessed=1, transcendentals=0)


def phase(turns, length):
    angles = (turns % length).astype(jnp.float32) * (TWO_PI / length)
    return jnp.cos(angles), jnp.sin(angles)


def transform_tables():
    depth = NCH // RADIX
    ids = np.arange(depth)
    angles = 2 * np.pi / depth * (ids[:, None] * ids[None, :] % depth)
    turns = 2 * np.pi / NCH * (np.arange(RADIX)[:, None] * ids[None, :])
    scale = 1.0 / math.sqrt(NCH)
    both = (np.cos(angles) * scale, np.sin(angles) * scale, np.cos(turns), np.sin(turns))
    return [jnp.asarray(x.astype(np.float32)) for x in both]


def radix8(re, im):
    half = math.sqrt(0.5)

    def four(xr, xi):
        ar, ai, br, bi = xr[0] + xr[2], xi[0] + xi[2], xr[0] - xr[2], xi[0] - xi[2]
        cr, ci, dr, di = xr[1] + xr[3], xi[1] + xi[3], xr[1] - xr[3], xi[1] - xi[3]
        return [ar + cr, br + di, ar - cr, br - di], [ai + ci, bi - dr, ai - ci, bi + dr]

    er, ei = four(re[0::2], im[0::2])
    odd_r, odd_i = four(re[1::2], im[1::2])
    tr = [odd_r[0], (odd_r[1] + odd_i[1]) * half, odd_i[2], (odd_i[3] - odd_r[3]) * half]
    ti = [odd_i[0], (odd_i[1] - odd_r[1]) * half, -odd_r[2], (odd_r[3] + odd_i[3]) * -half]
    return (
        [e + t for e, t in zip(er, tr)] + [e - t for e, t in zip(er, tr)],
        [e + t for e, t in zip(ei, ti)] + [e - t for e, t in zip(ei, ti)],
    )


def swap_blocks(parts, lane_ids):
    count = len(parts)
    width = LANES // count
    parts = list(parts)
    step = 1
    while step < count:
        keep = (lane_ids // width) % (2 * step) < step
        for b in range(count):
            if b & step == 0:
                low, high = parts[b], parts[b + step]
                parts[b] = jnp.where(keep, low, pltpu.roll(high, step * width, 1))
                parts[b + step] = jnp.where(keep, pltpu.roll(low, LANES - step * width, 1), high)
        step *= 2
    return parts


def gather_blocks(parts, lane_ids):
    count = len(parts)
    width = LANES // count
    turned = [parts[0]] + [pltpu.roll(parts[b], b * width, 1) for b in range(1, count)]
    turned = [turned[-b % count] for b in range(count)]
    step = 1
    while step < count:
        moved = (lane_ids // width) & step != 0
        turned = [jnp.where(moved, turned[(g - step) % count], turned[g]) for g in range(count)]
        step *= 2
    return [turned[0]] + [pltpu.roll(turned[g], LANES - g * width, 1) for g in range(1, count)]


def channel_kernel(first, row_block, volts, prototype, cosines, sines, turn_c, turn_s, out, branches, *scratch):
    taps_wide, table, filtered, product = scratch
    taps = taps_wide.shape[0]
    length = taps_wide.shape[2]
    frames = filtered.shape[2]
    depth = length // RADIX
    bands = depth // LANES
    for t in range(taps):
        taps_wide[t] = jnp.broadcast_to(prototype[t : t + 1, :], taps_wide.shape[1:])
    cos_t, sin_t = cosines[...].astype(table.dtype), sines[...].astype(table.dtype)
    table[:depth, :depth] = cos_t
    table[:depth, depth:] = -sin_t
    table[depth:, :depth] = sin_t
    table[depth:, depth:] = cos_t

    def column(j, carry):
        lane = pl.multiple_of(j * LANES, LANES)

        def strip(n1, inner):
            base = pl.multiple_of(n1 * depth + j * LANES, LANES)
            for part in range(2):
                sums = [None] * frames
                for seg in range(frames + taps - 1):
                    start = pl.multiple_of((first + seg) * length + base, LANES)
                    value = volts[part, :, pl.ds(start, LANES)].astype(jnp.float32)
                    for f in range(max(0, seg - taps + 1), min(frames, seg + 1)):
                        coef = taps_wide[seg - f, :, pl.ds(base, LANES)]
                        term = value * jnp.concatenate([coef, coef], axis=0)
                        sums[f] = term if sums[f] is None else sums[f] + term
                    if seg >= taps - 1:
                        filtered[part, n1, seg - taps + 1] = sums[seg - taps + 1]
            return inner

        lax.fori_loop(0, RADIX, strip, 0)

        def butterfly(f, inner):
            re, im = radix8(
                [filtered[0, n1, f] for n1 in range(RADIX)],
                [filtered[1, n1, f] for n1 in range(RADIX)],
            )
            for b in range(RADIX):
                turned_r, turned_i = re[b], im[b]
                if b > 0:
                    cos_t, sin_t = turn_c[b : b + 1, pl.ds(lane, LANES)], turn_s[b : b + 1, pl.ds(lane, LANES)]
                    turned_r, turned_i = re[b] * cos_t + im[b] * sin_t, im[b] * cos_t - re[b] * sin_t
                branches[b, f, :, pl.ds(lane, LANES)] = turned_r.astype(branches.dtype)
                branches[b, f, :, pl.ds(pl.multiple_of(depth + lane, LANES), LANES)] = turned_i.astype(branches.dtype)
            return inner

        lax.fori_loop(0, frames, butterfly, 0)
        return carry

    lax.fori_loop(0, bands, column, 0)

    rows = frames * ROWS
    joined = RADIX
    while joined * rows > 1024:
        joined //= 2

    def multiply(step, carry):
        some = pl.ds(step // bands * joined, joined)
        lanes = pl.ds(pl.multiple_of(step % bands * 2 * LANES, 2 * LANES), 2 * LANES)
        left = branches[some].reshape(joined * rows, 2 * depth)
        got = jnp.dot(left, table[:, lanes], preferred_element_type=jnp.float32)
        product[some, :, lanes] = got.reshape(joined, rows, 2 * LANES)
        return carry

    lax.fori_loop(0, RADIX // joined * bands, multiply, 0)
    lane_ids = lax.broadcasted_iota(jnp.int32, (ROWS, LANES), 1)

    def regroup(f, carry):
        top = pl.multiple_of(f * ROWS, ROWS)
        for part in range(2):
            for band in range(bands):
                lane = part * depth + band * LANES
                pieces = [product[b, pl.ds(top, ROWS), lane : lane + LANES] for b in range(RADIX)]
                for g, piece in enumerate(gather_blocks(pieces, lane_ids)):
                    at = pl.multiple_of((part * frames + f) * LANES, LANES)
                    out[g, band, :, pl.ds(at, LANES)] = piece.astype(out.dtype)
        return carry

    lax.fori_loop(0, frames, regroup, 0)


def channelise(row_block, volts, prototype, tables, first, frames):
    taps = prototype.shape[0]
    length = volts.shape[2] if first > 0 else (frames + taps - 1) * NCH
    depth = NCH // RADIX
    bands = depth // LANES
    wide = 2 * frames * LANES
    return pl.pallas_call(
        functools.partial(channel_kernel, first),
        grid_spec=pltpu.PrefetchScalarGridSpec(
            num_scalar_prefetch=1,
            grid=(1,),
            in_specs=[
                pl.BlockSpec((2, ROWS, length), lambda i, row: (0, row[0], 0)),
            ]
            + [pl.BlockSpec(x.shape, lambda i, row: (0, 0)) for x in (prototype, *tables)],
            out_specs=[
                pl.BlockSpec((RADIX, bands, ROWS, wide), lambda i, row: (0, 0, 0, 0)),
                pl.BlockSpec((RADIX, frames, ROWS, 2 * depth), lambda i, row: (0, 0, 0, 0)),
            ],
            scratch_shapes=[
                pltpu.VMEM((taps, 8, NCH), jnp.float32),
                pltpu.VMEM((2 * depth, 2 * depth), jnp.bfloat16),
                pltpu.VMEM((2, RADIX, frames, ROWS, LANES), jnp.float32),
                pltpu.VMEM((RADIX, frames * ROWS, 2 * depth), jnp.float32),
            ],
        ),
        out_shape=[
            jax.ShapeDtypeStruct((RADIX, bands, ROWS, wide), jnp.bfloat16),
            jax.ShapeDtypeStruct((RADIX, frames, ROWS, 2 * depth), jnp.bfloat16),
        ],
        compiler_params=pltpu.CompilerParams(vmem_limit_bytes=VMEM),
        cost_estimate=busy(frames / FRAMES),
    )(row_block, volts, prototype, *tables)


def slot_kernel(row_branch, hi_c, hi_s, lo_c, lo_s, *rest):
    chunks, (out, table, total) = rest[:-3], rest[-3:]
    depth = chunks[0].shape[3] // 2
    for a in range(hi_c.shape[1]):
        high_c, high_s = hi_c[:, a : a + 1], hi_s[:, a : a + 1]
        table[:, a * LANES : (a + 1) * LANES] = (high_c * lo_c[...] - high_s * lo_s[...]).astype(table.dtype)
        table[:, depth + a * LANES : depth + (a + 1) * LANES] = (
            high_s * lo_c[...] + high_c * lo_s[...]
        ).astype(table.dtype)
    total[...] = jnp.zeros_like(total)

    def branch(b, carry):
        rows = jnp.concatenate([c[b].reshape(c.shape[1] * c.shape[2], c.shape[3]) for c in chunks], axis=0)
        got = lax.dot_general(table[...], rows, NT, preferred_element_type=jnp.float32)
        total[...] = jnp.where(row_branch[...] == b, got, total[...])
        return carry

    lax.fori_loop(0, RADIX, branch, 0)
    per = out.shape[1]
    for d in range(out.shape[0]):
        out[d] = total[d * per : (d + 1) * per].astype(out.dtype)


def slot_tables(row_channel, row_filled, row_turned):
    depth = NCH // RADIX
    coarse = jnp.arange(depth // LANES, dtype=jnp.int32) * LANES
    fine = jnp.arange(LANES, dtype=jnp.int32)
    whole = row_channel - row_channel % RADIX
    hi_c, hi_s = phase(whole[:, None] * coarse[None, :] + row_turned[:, None] * (NCH // 4), NCH)
    lo_c, lo_s = phase(whole[:, None] * fine[None, :], NCH)
    scaling = row_filled.astype(jnp.float32)[:, None] * (1.0 / math.sqrt(NCH))
    return (row_channel % RADIX)[:, None], hi_c * scaling, hi_s * scaling, lo_c, lo_s


def slot_spectra(tables, chunks, per):
    rows = tables[0].shape[0]
    samples = sum(c.shape[1] * c.shape[2] for c in chunks)
    return pl.pallas_call(
        slot_kernel,
        out_shape=jax.ShapeDtypeStruct((rows // per, per, samples), jnp.bfloat16),
        scratch_shapes=[
            pltpu.VMEM((rows, chunks[0].shape[3]), jnp.bfloat16),
            pltpu.VMEM((rows, samples), jnp.float32),
        ],
        compiler_params=pltpu.CompilerParams(vmem_limit_bytes=VMEM),
        cost_estimate=busy(1),
    )(*tables, *chunks)


def correlate(pieces, halves, lanes):
    senders, sub, _ = pieces[0][0].shape
    half = FRAMES * lanes
    signals = senders * halves * sub
    count = max(1, signals // 256)
    each = senders // count
    block = each * halves * sub

    def kernel(*refs):
        parts, (out, held, turned, made, in_sems, out_sems) = refs[: len(pieces)], refs[len(pieces) :]
        coming = [[] for _ in range(count)]
        for index, (_, which, first, frames) in enumerate(pieces):
            for q in range(count):
                for part in range(2):
                    src = parts[index].at[pl.ds(q * each, each), :, pl.ds(part * frames * lanes, frames * lanes)]
                    dst = held.at[q, :, which, :, pl.ds(part * half + first * lanes, frames * lanes)]
                    sem = in_sems.at[(index * count + q) * 2 + part]
                    coming[q].append(pltpu.make_async_copy(src, dst, sem))
        for copies in coming:
            for copy in copies:
                copy.start()

        def rows_of(i):
            return pl.ds(i * block, block)

        inverse = 1.0 / half
        going = [[], []]
        slot = 0
        for i in range(count):
            for copy in coming[i]:
                copy.wait()
            left = held[i].reshape(block, 2 * half)
            turned[:, :half] = left[:, half:]
            turned[:, half:] = -left[:, :half]
            at_i = rows_of(i)
            for j in range(i + 1):
                right = held[j].reshape(block, 2 * half)
                at_j = rows_of(j)
                for copy in going[slot]:
                    copy.wait()
                going[slot] = []
                for part, rows in enumerate((left, turned[...])):
                    got = lax.dot_general(rows, right, NT, preferred_element_type=jnp.float32) * inverse
                    made[slot, part, 0] = got
                    going[slot].append(
                        pltpu.make_async_copy(
                            made.at[slot, part, 0], out.at[part, at_i, at_j], out_sems.at[slot, part, 0]
                        )
                    )
                    if i != j:
                        made[slot, part, 1] = got.T if part == 0 else -got.T
                        going[slot].append(
                            pltpu.make_async_copy(
                                made.at[slot, part, 1], out.at[part, at_j, at_i], out_sems.at[slot, part, 1]
                            )
                        )
                for copy in going[slot]:
                    copy.start()
                slot = 1 - slot
        for copies in going:
            for copy in copies:
                copy.wait()

    return pl.pallas_call(
        kernel,
        in_specs=[pl.BlockSpec(memory_space=pl.ANY)] * len(pieces),
        out_specs=pl.BlockSpec(memory_space=pl.ANY),
        out_shape=jax.ShapeDtypeStruct((2, signals, signals), jnp.float32),
        scratch_shapes=[
            pltpu.VMEM((count, each, halves, sub, 2 * half), jnp.bfloat16),
            pltpu.VMEM((block, 2 * half), jnp.bfloat16),
            pltpu.VMEM((2, 2, 2, block, block), jnp.float32),
            pltpu.SemaphoreType.DMA((2 * count * len(pieces),)),
            pltpu.SemaphoreType.DMA((2, 2, 2)),
        ],
        compiler_params=pltpu.CompilerParams(vmem_limit_bytes=VMEM),
        cost_estimate=NO_COST,
    )(*[piece[0] for piece in pieces])


def weight_kernel(channel, delays, gains, out):
    beams = delays.shape[0]
    turns = delays[...] * (channel[pl.program_id(0)].astype(jnp.float32) * (1.0 / NCH))
    part = turns - jnp.floor(turns + 0.5)
    square = part * part
    cos_t = jnp.full_like(part, TWO_PI**16 / math.factorial(16))
    sin_t = jnp.full_like(part, -(TWO_PI**15) / math.factorial(15))
    for power in range(14, -1, -2):
        sign = -1.0 if power % 4 == 2 else 1.0
        cos_t = cos_t * square + sign * TWO_PI**power / math.factorial(power)
        if power > 0:
            sign = -1.0 if (power - 1) % 4 == 3 else 1.0
            sin_t = sin_t * square + sign * TWO_PI ** (power - 1) / math.factorial(power - 1)
    scaled = gains[...] * (1.0 / math.sqrt(gains.shape[1]))
    out[0, :beams] = (scaled * cos_t).astype(out.dtype)
    out[0, beams:] = (-scaled * sin_t * part).astype(out.dtype)


def beam_weights(channel, delays, gains):
    beams, listed = delays.shape
    slots = channel.shape[0]
    return pl.pallas_call(
        weight_kernel,
        grid=(slots,),
        in_specs=[
            pl.BlockSpec(memory_space=pltpu.SMEM),
            pl.BlockSpec(delays.shape, lambda i: (0, 0)),
            pl.BlockSpec(gains.shape, lambda i: (0, 0)),
        ],
        out_specs=pl.BlockSpec((1, 2 * beams, listed), lambda i: (i, 0, 0)),
        out_shape=jax.ShapeDtypeStruct((slots, 2 * beams, listed), jnp.bfloat16),
        cost_estimate=NO_COST,
    )(channel, delays, gains)


def combine(spectra, chooser, weights, sub):
    slots, beams2, listed = weights.shape
    beams = beams2 // 2
    rows = 2 * slots
    senders = spectra.shape[0]
    halves = spectra.shape[2] // (FRAMES * sub)
    count = LANES // sub
    inner = senders // count
    groups = halves * inner
    tiles = 2 * listed // LANES

    def kernel(spectrum, choose, weight_hbm, out, ordered, picked, weight, sem):
        coming = pltpu.make_async_copy(weight_hbm, weight, sem)
        coming.start()
        lane_ids = lax.broadcasted_iota(jnp.int32, (rows, LANES), 1)
        for h in range(halves):
            for q in range(inner):
                for t in range(FRAMES // count):
                    lane = h * FRAMES * sub + t * LANES
                    pieces = [
                        spectrum[q * count + i, :, lane : lane + LANES].astype(jnp.float32) for i in range(count)
                    ]
                    for f, piece in enumerate(swap_blocks(pieces, lane_ids)):
                        top = (t * count + f) * rows
                        group = (h * inner + q) * LANES
                        ordered[top : top + rows, group : group + LANES] = piece
        acc = jnp.dot(ordered[...].astype(jnp.bfloat16), choose[...], preferred_element_type=jnp.float32)
        for lane in range(tiles):
            picked[lane] = acc[:, lane * LANES : (lane + 1) * LANES]
        coming.wait()
        for i in range(slots):
            chosen = [
                jnp.concatenate(
                    [
                        picked[p * tiles // 2 + lane, pl.ds(part * slots + i, FRAMES, rows), :]
                        for lane in range(tiles // 2)
                    ],
                    axis=1,
                )
                for p in range(2)
                for part in range(2)
            ]
            stacked = jnp.concatenate(chosen, axis=0).astype(jnp.bfloat16)
            mixed = lax.dot_general(stacked, weight[i], NT, preferred_element_type=jnp.float32)
            for p in range(2):
                at = 2 * FRAMES * p
                of_re, of_im = mixed[at : at + FRAMES], mixed[at + FRAMES : at + 2 * FRAMES]
                out[0, i, 0, :, p * beams : (p + 1) * beams] = of_re[:, :beams] - of_im[:, beams:]
                out[0, i, 1, :, p * beams : (p + 1) * beams] = of_im[:, :beams] + of_re[:, beams:]

    return pl.pallas_call(
        kernel,
        in_specs=[pl.BlockSpec(memory_space=pltpu.VMEM)] * 2 + [pl.BlockSpec(memory_space=pl.ANY)],
        out_shape=jax.ShapeDtypeStruct((1, slots, 2, FRAMES, 2 * beams), jnp.float32),
        scratch_shapes=[
            pltpu.VMEM((FRAMES * rows, groups * LANES), jnp.float32),
            pltpu.VMEM((tiles, FRAMES * rows, LANES), jnp.float32),
            pltpu.VMEM(weights.shape, weights.dtype),
            pltpu.SemaphoreType.DMA,
        ],
        compiler_params=pltpu.CompilerParams(vmem_limit_bytes=VMEM),
        cost_estimate=NO_COST,
    )(spectra, chooser, weights)


def body(volts, prototype, beam_channels, station_index, delays, gains, assign):
    sig_dev = volts.shape[1]
    st_count, sb_count = lax.axis_size("st"), lax.axis_size("sb")
    st_here, sb_here = lax.axis_index("st").astype(jnp.int32), lax.axis_index("sb").astype(jnp.int32)
    devices = st_count * sb_count
    group = NCH // devices
    fine = group // RADIX
    constants = transform_tables()
    barrier = lax.optimization_barrier

    def exchange(x):
        return lax.all_to_all(x, ("st", "sb"), split_axis=0, concat_axis=0, tiled=True)

    share = sig_dev // sb_count
    sub = min(share, ROWS)
    halves = max(1, share // ROWS)
    inside = (sb_here * share) % ROWS
    unit = max(1, LANES // group)
    early = max(unit, EARLY // unit * unit)
    plan = [(0, 0, early), (0, early, FRAMES - early)] + [(h, 0, FRAMES) for h in range(1, halves)]

    def channels_of(c, here):
        which, first, frames = plan[c]
        row_block = (here * share // ROWS + which)[None]
        out, kept = channelise(row_block, volts, prototype, constants, first, frames)
        if sub < ROWS:
            out = lax.dynamic_slice_in_dim(out, inside, sub, axis=2)
        inner = st_count // RADIX
        if inner > 1:
            out = out.reshape(RADIX, sb_count, sub, 2 * frames, RADIX, inner, fine).transpose(0, 5, 1, 2, 3, 4, 6)
        return out.reshape(devices, sub, -1), kept

    lists = (assign, beam_channels, station_index)
    here = sb_here
    out, kept = channels_of(0, here)
    branches, arrived = [kept], []
    for c in range(1, len(plan)):
        out, here, lists, arrived[-1:] = barrier((out, here, lists, arrived[-1:]))
        arrived.append(exchange(out))
        out, kept = channels_of(c, here)
        branches.append(kept)

    assign, beam_channels, station_index = barrier((lists, kept))[0]
    per_dev = SLOTS // st_count
    owners = assign[:, 0]
    taken = (owners[:, None] == jnp.arange(sb_count, dtype=jnp.int32)[None, :]).astype(jnp.int32)
    position = jnp.sum(taken * jnp.cumsum(taken, axis=0), axis=1) - 1
    place = owners * SLOTS + position
    slot_ids = (
        jnp.arange(st_count, dtype=jnp.int32)[:, None, None] * per_dev
        + jnp.arange(sb_count, dtype=jnp.int32)[:, None] * SLOTS
        + jnp.arange(per_dev, dtype=jnp.int32)
    ).reshape(-1)
    picker = (place[None, :] == slot_ids[:, None]).astype(jnp.int32)
    filled = jnp.sum(picker, axis=1)
    slot_channel = jnp.sum(picker * beam_channels[None, :], axis=1)

    def by_row(values):
        return jnp.broadcast_to(values.reshape(devices, 1, per_dev), (devices, 2, per_dev)).reshape(-1)

    turned = jnp.broadcast_to(jnp.arange(2, dtype=jnp.int32)[None, :, None], (devices, 2, per_dev)).reshape(-1)
    mine = lax.dynamic_slice_in_dim(slot_channel, (st_here * sb_count + sb_here) * per_dev, per_dev)
    tables = slot_tables(by_row(slot_channel), by_row(filled), turned)
    spectra = slot_spectra(tables, branches, 2 * per_dev)
    if sub < ROWS:
        spectra = spectra.reshape(devices, 2 * per_dev, FRAMES, ROWS)
        spectra = lax.dynamic_slice_in_dim(spectra, inside, sub, axis=3).reshape(devices, 2 * per_dev, -1)

    out, spectra, mine, arrived[-1:] = barrier((out, spectra, mine, arrived[-1:]))
    arrived.append(exchange(out))
    weights = beam_weights(mine, delays, gains)
    signal_ids = (
        jnp.arange(halves, dtype=jnp.int32)[:, None, None] * sub
        + jnp.arange(devices, dtype=jnp.int32)[:, None] * share
        + jnp.arange(sub, dtype=jnp.int32)
    ).reshape(-1)
    wanted = (station_index[None, :] * 2 + jnp.arange(2, dtype=jnp.int32)[:, None]).reshape(-1)
    chooser = (signal_ids[:, None] == wanted[None, :]).astype(jnp.bfloat16)

    spectra, weights, chooser, arrived[-1:] = barrier((spectra, weights, chooser, arrived[-1:]))
    slot_received = exchange(spectra)
    if halves == 1:
        arrived = [x.reshape(-1, min(256, devices * sub), x.shape[2]) for x in arrived]
    visibility = correlate([(x, *part) for x, part in zip(arrived, plan)], halves, group)
    signals = visibility.shape[1]
    beam_out = combine(slot_received, chooser, weights, sub)
    return (visibility.reshape(2, 1, 1, signals, signals), beam_out)


def solution(mesh):
    in_specs = (P(None, "st", None), P(), P(), P(), P(), P(), P())
    out_specs = (P(None, "sb", "st", None, None), P("sb", "st", None, None, None))
    return jax.shard_map(body, mesh=mesh, in_specs=in_specs, out_specs=out_specs, check_vma=False)
```

```python
import functools
import math

import jax
import jax.numpy as jnp
import numpy as np
from jax import lax
from jax.experimental import pallas as pl
from jax.experimental.pallas import tpu as pltpu
from jax.sharding import Mesh
from jax.sharding import PartitionSpec as P

NCH = 4096
FRAMES = 16
SLOTS = 160
RADIX = 8
LANES = 128
ROWS = 16
EARLY = 4
LATE = 6
VMEM = 56 * 1024 * 1024

NO_COST = pl.CostEstimate(flops=1, bytes_accessed=1, transcendentals=0)

TWO_PI = 2.0 * math.pi
NT = (((1,), (1,)), ((), ()))


def busy(share):
    return pl.CostEstimate(flops=int(share * 1e10), bytes_accessed=1, transcendentals=0)


def phase(turns, length):
    angles = (turns % length).astype(jnp.float32) * (TWO_PI / length)
    return jnp.cos(angles), jnp.sin(angles)


def transform_tables():
    depth = NCH // RADIX
    ids = np.arange(depth)
    angles = 2 * np.pi / depth * (ids[:, None] * ids[None, :] % depth)
    turns = 2 * np.pi / NCH * (np.arange(RADIX)[:, None] * ids[None, :])
    scale = 1.0 / math.sqrt(NCH)
    both = (np.cos(angles) * scale, np.sin(angles) * scale, np.cos(turns), np.sin(turns))
    return [jnp.asarray(x.astype(np.float32)) for x in both]


def radix8(re, im):
    half = math.sqrt(0.5)

    def four(xr, xi):
        ar, ai, br, bi = xr[0] + xr[2], xi[0] + xi[2], xr[0] - xr[2], xi[0] - xi[2]
        cr, ci, dr, di = xr[1] + xr[3], xi[1] + xi[3], xr[1] - xr[3], xi[1] - xi[3]
        return [ar + cr, br + di, ar - cr, br - di], [ai + ci, bi - dr, ai - ci, bi + dr]

    er, ei = four(re[0::2], im[0::2])
    odd_r, odd_i = four(re[1::2], im[1::2])
    tr = [odd_r[0], (odd_r[1] + odd_i[1]) * half, odd_i[2], (odd_i[3] - odd_r[3]) * half]
    ti = [odd_i[0], (odd_i[1] - odd_r[1]) * half, -odd_r[2], (odd_r[3] + odd_i[3]) * -half]
    return (
        [e + t for e, t in zip(er, tr)] + [e - t for e, t in zip(er, tr)],
        [e + t for e, t in zip(ei, ti)] + [e - t for e, t in zip(ei, ti)],
    )


def swap_blocks(parts, lane_ids):
    count = len(parts)
    width = LANES // count
    parts = list(parts)
    step = 1
    while step < count:
        keep = (lane_ids // width) % (2 * step) < step
        for b in range(count):
            if b & step == 0:
                low, high = parts[b], parts[b + step]
                parts[b] = jnp.where(keep, low, pltpu.roll(high, step * width, 1))
                parts[b + step] = jnp.where(keep, pltpu.roll(low, LANES - step * width, 1), high)
        step *= 2
    return parts


def gather_blocks(parts, lane_ids):
    count = len(parts)
    width = LANES // count
    turned = [parts[0]] + [pltpu.roll(parts[b], b * width, 1) for b in range(1, count)]
    turned = [turned[-b % count] for b in range(count)]
    step = 1
    while step < count:
        moved = (lane_ids // width) & step != 0
        turned = [jnp.where(moved, turned[(g - step) % count], turned[g]) for g in range(count)]
        step *= 2
    return [turned[0]] + [pltpu.roll(turned[g], LANES - g * width, 1) for g in range(1, count)]


def by_partner(x, here, far):
    width = LANES // far
    lane_ids = lax.broadcasted_iota(jnp.int32, x.shape, 1)
    step = 1
    while step < far:
        upper = (lane_ids // width) & step != 0
        other = jnp.where(upper, pltpu.roll(x, step * width, 1), pltpu.roll(x, LANES - step * width, 1))
        x = jnp.where(here & step != 0, other, x)
        step *= 2
    return x


def channel_kernel(first, place, volts, prototype, cosines, sines, turn_c, turn_s, *rest):
    outs, (branches, taps_wide, table, filtered, product) = rest[:-5], rest[-5:]
    near = RADIX // len(outs)
    taps = taps_wide.shape[0]
    length = taps_wide.shape[2]
    frames = filtered.shape[2]
    depth = length // RADIX
    bands = depth // LANES
    for t in range(taps):
        taps_wide[t] = jnp.broadcast_to(prototype[t : t + 1, :], taps_wide.shape[1:])
    cos_t, sin_t = [
        jnp.concatenate(
            [by_partner(x[:, lane : lane + LANES], place[1], len(outs)) for lane in range(0, depth, LANES)], axis=1
        ).astype(table.dtype)
        for x in (cosines, sines)
    ]
    table[:depth, :depth] = cos_t
    table[:depth, depth:] = -sin_t
    table[depth:, :depth] = sin_t
    table[depth:, depth:] = cos_t

    def column(j, carry):
        lane = pl.multiple_of(j * LANES, LANES)

        def strip(n1, inner):
            base = pl.multiple_of(n1 * depth + j * LANES, LANES)
            for part in range(2):
                sums = [None] * frames
                for seg in range(frames + taps - 1):
                    start = pl.multiple_of((first + seg) * length + base, LANES)
                    value = volts[part, :, pl.ds(start, LANES)].astype(jnp.float32)
                    for f in range(max(0, seg - taps + 1), min(frames, seg + 1)):
                        coef = taps_wide[seg - f, :, pl.ds(base, LANES)]
                        term = value * jnp.concatenate([coef, coef], axis=0)
                        sums[f] = term if sums[f] is None else sums[f] + term
                    if seg >= taps - 1:
                        filtered[part, n1, seg - taps + 1] = sums[seg - taps + 1]
            return inner

        lax.fori_loop(0, RADIX, strip, 0)

        def butterfly(f, inner):
            re, im = radix8(
                [filtered[0, n1, f] for n1 in range(RADIX)],
                [filtered[1, n1, f] for n1 in range(RADIX)],
            )
            for b in range(RADIX):
                turned_r, turned_i = re[b], im[b]
                if b > 0:
                    cos_t, sin_t = turn_c[b : b + 1, pl.ds(lane, LANES)], turn_s[b : b + 1, pl.ds(lane, LANES)]
                    turned_r, turned_i = re[b] * cos_t + im[b] * sin_t, im[b] * cos_t - re[b] * sin_t
                branches[b, f, :, pl.ds(lane, LANES)] = turned_r.astype(branches.dtype)
                branches[b, f, :, pl.ds(pl.multiple_of(depth + lane, LANES), LANES)] = turned_i.astype(branches.dtype)
            return inner

        lax.fori_loop(0, frames, butterfly, 0)
        return carry

    lax.fori_loop(0, bands, column, 0)

    rows = frames * ROWS
    joined = RADIX
    while joined * rows > 1024:
        joined //= 2

    def multiply(step, carry):
        some = pl.ds(step // bands * joined, joined)
        lanes = pl.ds(pl.multiple_of(step % bands * 2 * LANES, 2 * LANES), 2 * LANES)
        left = branches[some].reshape(joined * rows, 2 * depth)
        got = jnp.dot(left, table[:, lanes], preferred_element_type=jnp.float32)
        product[some, :, lanes] = got.reshape(joined, rows, 2 * LANES)
        return carry

    lax.fori_loop(0, RADIX // joined * bands, multiply, 0)
    lane_ids = lax.broadcasted_iota(jnp.int32, (ROWS, LANES), 1)

    def regroup(f, carry):
        top = pl.multiple_of(f * ROWS, ROWS)
        for part in range(2):
            for band in range(bands):
                lane = part * depth + band * LANES
                pieces = [product[b, pl.ds(top, ROWS), lane : lane + LANES] for b in range(RADIX)]
                for g, piece in enumerate(gather_blocks(pieces, lane_ids)):
                    at = pl.multiple_of((part * frames + f) * LANES, LANES)
                    out = outs[g // near]
                    out[g % near, band, :, pl.ds(at, LANES)] = piece.astype(out.dtype)
        return carry

    lax.fori_loop(0, frames, regroup, 0)


def channelise(place, volts, prototype, tables, first, frames, far):
    near = RADIX // far
    taps = prototype.shape[0]
    length = volts.shape[2] if first > 0 else (frames + taps - 1) * NCH
    depth = NCH // RADIX
    bands = depth // LANES
    wide = 2 * frames * LANES
    return pl.pallas_call(
        functools.partial(channel_kernel, first),
        grid_spec=pltpu.PrefetchScalarGridSpec(
            num_scalar_prefetch=1,
            grid=(1,),
            in_specs=[
                pl.BlockSpec((2, ROWS, length), lambda i, row: (0, row[0], 0)),
            ]
            + [pl.BlockSpec(x.shape, lambda i, row: (0, 0)) for x in (prototype, *tables)],
            out_specs=[
                *[pl.BlockSpec((near, bands, ROWS, wide), lambda i, row: (0, 0, 0, 0))] * far,
                pl.BlockSpec((RADIX, frames, ROWS, 2 * depth), lambda i, row: (0, 0, 0, 0)),
            ],
            scratch_shapes=[
                pltpu.VMEM((taps, 8, NCH), jnp.float32),
                pltpu.VMEM((2 * depth, 2 * depth), jnp.bfloat16),
                pltpu.VMEM((2, RADIX, frames, ROWS, LANES), jnp.float32),
                pltpu.VMEM((RADIX, frames * ROWS, 2 * depth), jnp.float32),
            ],
        ),
        out_shape=[
            *[jax.ShapeDtypeStruct((near, bands, ROWS, wide), jnp.bfloat16)] * far,
            jax.ShapeDtypeStruct((RADIX, frames, ROWS, 2 * depth), jnp.bfloat16),
        ],
        compiler_params=pltpu.CompilerParams(vmem_limit_bytes=VMEM),
        cost_estimate=busy(frames / FRAMES),
    )(place, volts, prototype, *tables)


def slot_kernel(far, row_branch, hi_c, hi_s, lo_c, lo_s, *rest):
    chunks, outs, (table, total) = rest[: -2 - far], rest[-2 - far : -2], rest[-2:]
    depth = chunks[0].shape[3] // 2
    for a in range(hi_c.shape[1]):
        high_c, high_s = hi_c[:, a : a + 1], hi_s[:, a : a + 1]
        table[:, a * LANES : (a + 1) * LANES] = (high_c * lo_c[...] - high_s * lo_s[...]).astype(table.dtype)
        table[:, depth + a * LANES : depth + (a + 1) * LANES] = (
            high_s * lo_c[...] + high_c * lo_s[...]
        ).astype(table.dtype)
    total[...] = jnp.zeros_like(total)

    def branch(b, carry):
        rows = jnp.concatenate([c[b].reshape(c.shape[1] * c.shape[2], c.shape[3]) for c in chunks], axis=0)
        got = lax.dot_general(table[...], rows, NT, preferred_element_type=jnp.float32)
        total[...] = jnp.where(row_branch[...] == b, got, total[...])
        return carry

    lax.fori_loop(0, RADIX, branch, 0)
    plane, per = outs[0].shape[:2]
    for s, out in enumerate(outs):
        for d in range(plane):
            top = (s * plane + d) * per
            out[d] = total[top : top + per].astype(out.dtype)


def slot_tables(row_channel, row_filled, row_turned):
    depth = NCH // RADIX
    coarse = jnp.arange(depth // LANES, dtype=jnp.int32) * LANES
    fine = jnp.arange(LANES, dtype=jnp.int32)
    whole = row_channel - row_channel % RADIX
    hi_c, hi_s = phase(whole[:, None] * coarse[None, :] + row_turned[:, None] * (NCH // 4), NCH)
    lo_c, lo_s = phase(whole[:, None] * fine[None, :], NCH)
    scaling = row_filled.astype(jnp.float32)[:, None] * (1.0 / math.sqrt(NCH))
    return (row_channel % RADIX)[:, None], hi_c * scaling, hi_s * scaling, lo_c, lo_s


def slot_spectra(tables, chunks, per, far):
    rows = tables[0].shape[0]
    samples = sum(c.shape[1] * c.shape[2] for c in chunks)
    return pl.pallas_call(
        functools.partial(slot_kernel, far),
        out_shape=[jax.ShapeDtypeStruct((rows // per // far, per, samples), jnp.bfloat16)] * far,
        scratch_shapes=[
            pltpu.VMEM((rows, chunks[0].shape[3]), jnp.bfloat16),
            pltpu.VMEM((rows, samples), jnp.float32),
        ],
        compiler_params=pltpu.CompilerParams(vmem_limit_bytes=VMEM),
        cost_estimate=busy(1),
    )(*tables, *chunks)


def correlate(here, pieces, far, halves, lanes):
    senders = pieces[0][0].shape[0]
    sub = pieces[0][0].shape[1] if halves == 1 else ROWS
    half = FRAMES * lanes
    block = senders * halves * sub
    signals = far * block

    def kernel(here_ref, *refs):
        parts, (out, held, turned, made, in_sems, out_sems) = refs[: len(pieces)], refs[len(pieces) :]
        coming = [[] for _ in range(far)]
        for index, (_, partner, row, which, first, frames) in enumerate(pieces):
            for part in range(2):
                src = parts[index].at[:, pl.ds(row, sub), pl.ds(part * frames * lanes, frames * lanes)]
                dst = held.at[partner, :, which, :, pl.ds(part * half + first * lanes, frames * lanes)]
                coming[partner].append(pltpu.make_async_copy(src, dst, in_sems.at[2 * index + part]))
        for copies in coming:
            for copy in copies:
                copy.start()

        def rows_of(i):
            return pl.ds(pl.multiple_of((here_ref[0] ^ i) * block, block), block)

        inverse = 1.0 / half
        going = [[], []]
        slot = 0
        for i in range(far):
            for copy in coming[i]:
                copy.wait()
            left = held[i].reshape(block, 2 * half)
            turned[:, :half] = left[:, half:]
            turned[:, half:] = -left[:, :half]
            at_i = rows_of(i)
            for j in range(i + 1):
                right = held[j].reshape(block, 2 * half)
                at_j = rows_of(j)
                for copy in going[slot]:
                    copy.wait()
                going[slot] = []
                for part, rows in enumerate((left, turned[...])):
                    got = lax.dot_general(rows, right, NT, preferred_element_type=jnp.float32) * inverse
                    made[slot, part, 0] = got
                    going[slot].append(
                        pltpu.make_async_copy(
                            made.at[slot, part, 0], out.at[part, at_i, at_j], out_sems.at[slot, part, 0]
                        )
                    )
                    if i != j:
                        made[slot, part, 1] = got.T if part == 0 else -got.T
                        going[slot].append(
                            pltpu.make_async_copy(
                                made.at[slot, part, 1], out.at[part, at_j, at_i], out_sems.at[slot, part, 1]
                            )
                        )
                for copy in going[slot]:
                    copy.start()
                slot = 1 - slot
        for copies in going:
            for copy in copies:
                copy.wait()

    return pl.pallas_call(
        kernel,
        in_specs=[pl.BlockSpec(memory_space=pltpu.SMEM)] + [pl.BlockSpec(memory_space=pl.ANY)] * len(pieces),
        out_specs=pl.BlockSpec(memory_space=pl.ANY),
        out_shape=jax.ShapeDtypeStruct((2, signals, signals), jnp.float32),
        scratch_shapes=[
            pltpu.VMEM((far, senders, halves, sub, 2 * half), jnp.bfloat16),
            pltpu.VMEM((block, 2 * half), jnp.bfloat16),
            pltpu.VMEM((2, 2, 2, block, block), jnp.float32),
            pltpu.SemaphoreType.DMA((2 * len(pieces),)),
            pltpu.SemaphoreType.DMA((2, 2, 2)),
        ],
        compiler_params=pltpu.CompilerParams(vmem_limit_bytes=VMEM // 2),
        cost_estimate=NO_COST,
    )(here, *[piece[0] for piece in pieces])


def weight_kernel(channel, delays, gains, out):
    beams = delays.shape[0]
    turns = delays[...] * (channel[pl.program_id(0)].astype(jnp.float32) * (1.0 / NCH))
    part = turns - jnp.floor(turns + 0.5)
    square = part * part
    cos_t = jnp.full_like(part, TWO_PI**16 / math.factorial(16))
    sin_t = jnp.full_like(part, -(TWO_PI**15) / math.factorial(15))
    for power in range(14, -1, -2):
        sign = -1.0 if power % 4 == 2 else 1.0
        cos_t = cos_t * square + sign * TWO_PI**power / math.factorial(power)
        if power > 0:
            sign = -1.0 if (power - 1) % 4 == 3 else 1.0
            sin_t = sin_t * square + sign * TWO_PI ** (power - 1) / math.factorial(power - 1)
    scaled = gains[...] * (1.0 / math.sqrt(gains.shape[1]))
    out[0, :beams] = (scaled * cos_t).astype(out.dtype)
    out[0, beams:] = (-scaled * sin_t * part).astype(out.dtype)


def beam_weights(channel, delays, gains):
    beams, listed = delays.shape
    slots = channel.shape[0]
    return pl.pallas_call(
        weight_kernel,
        grid=(slots,),
        in_specs=[
            pl.BlockSpec(memory_space=pltpu.SMEM),
            pl.BlockSpec(delays.shape, lambda i: (0, 0)),
            pl.BlockSpec(gains.shape, lambda i: (0, 0)),
        ],
        out_specs=pl.BlockSpec((1, 2 * beams, listed), lambda i: (i, 0, 0)),
        out_shape=jax.ShapeDtypeStruct((slots, 2 * beams, listed), jnp.bfloat16),
        cost_estimate=NO_COST,
    )(channel, delays, gains)


def combine(spectra, chooser, weights, sub):
    slots, beams2, listed = weights.shape
    beams = beams2 // 2
    rows = 2 * slots
    senders = spectra.shape[0]
    halves = spectra.shape[2] // (FRAMES * sub)
    count = LANES // sub
    inner = senders // count
    partners = spectra.shape[1] // rows
    groups = partners * halves * inner
    tiles = 2 * listed // LANES

    def kernel(spectrum, choose, weight_hbm, out, ordered, picked, weight, sem):
        coming = pltpu.make_async_copy(weight_hbm, weight, sem)
        coming.start()
        lane_ids = lax.broadcasted_iota(jnp.int32, (rows, LANES), 1)
        for s in range(partners):
            for h in range(halves):
                for q in range(inner):
                    for t in range(FRAMES // count):
                        lane = h * FRAMES * sub + t * LANES
                        pieces = [
                            spectrum[q * count + i, s * rows : (s + 1) * rows, lane : lane + LANES].astype(jnp.float32)
                            for i in range(count)
                        ]
                        for f, piece in enumerate(swap_blocks(pieces, lane_ids)):
                            top = (t * count + f) * rows
                            group = ((s * halves + h) * inner + q) * LANES
                            ordered[top : top + rows, group : group + LANES] = piece
        acc = jnp.dot(ordered[...].astype(jnp.bfloat16), choose[...], preferred_element_type=jnp.float32)
        for lane in range(tiles):
            picked[lane] = acc[:, lane * LANES : (lane + 1) * LANES]
        coming.wait()
        for i in range(slots):
            chosen = [
                jnp.concatenate(
                    [
                        picked[p * tiles // 2 + lane, pl.ds(part * slots + i, FRAMES, rows), :]
                        for lane in range(tiles // 2)
                    ],
                    axis=1,
                )
                for p in range(2)
                for part in range(2)
            ]
            stacked = jnp.concatenate(chosen, axis=0).astype(jnp.bfloat16)
            mixed = lax.dot_general(stacked, weight[i], NT, preferred_element_type=jnp.float32)
            for p in range(2):
                at = 2 * FRAMES * p
                of_re, of_im = mixed[at : at + FRAMES], mixed[at + FRAMES : at + 2 * FRAMES]
                out[0, i, 0, :, p * beams : (p + 1) * beams] = of_re[:, :beams] - of_im[:, beams:]
                out[0, i, 1, :, p * beams : (p + 1) * beams] = of_im[:, :beams] + of_re[:, beams:]

    return pl.pallas_call(
        kernel,
        in_specs=[pl.BlockSpec(memory_space=pltpu.VMEM)] * 2 + [pl.BlockSpec(memory_space=pl.ANY)],
        out_shape=jax.ShapeDtypeStruct((1, slots, 2, FRAMES, 2 * beams), jnp.float32),
        scratch_shapes=[
            pltpu.VMEM((FRAMES * rows, groups * LANES), jnp.float32),
            pltpu.VMEM((tiles, FRAMES * rows, LANES), jnp.float32),
            pltpu.VMEM(weights.shape, weights.dtype),
            pltpu.SemaphoreType.DMA,
        ],
        compiler_params=pltpu.CompilerParams(vmem_limit_bytes=VMEM // 2),
        cost_estimate=NO_COST,
    )(spectra, chooser, weights)


def body(volts, prototype, beam_channels, station_index, delays, gains, assign):
    sig_dev = volts.shape[1]
    far, near, sb_count = lax.axis_size("far"), lax.axis_size("near"), lax.axis_size("sb")
    far_here, near_here, sb_here = [lax.axis_index(name).astype(jnp.int32) for name in ("far", "near", "sb")]
    st_count = far * near
    devices = st_count * sb_count
    plane = near * sb_count
    group = NCH // devices
    fine = group // RADIX
    partner = far_here ^ jnp.arange(far, dtype=jnp.int32)
    constants = transform_tables()
    barrier = lax.optimization_barrier

    def to_planes(xs):
        return [xs[0]] + [lax.ppermute(xs[s], "far", [(i, i ^ s) for i in range(far)]) for s in range(far - 1, 0, -1)][::-1]

    def in_plane(xs):
        joined = jnp.concatenate(xs, axis=1)
        return lax.all_to_all(joined, ("near", "sb"), split_axis=0, concat_axis=0, tiled=True)

    share = sig_dev // sb_count
    sub = min(share, ROWS)
    halves = max(1, share // ROWS)
    inside = (sb_here * share) % ROWS
    unit = max(1, LANES // group)
    early, late = [max(unit, x // unit * unit) for x in (EARLY, LATE)]
    plan = [(0, 0, early), (0, early, FRAMES - early)]
    for h in range(1, halves):
        plan += [(h, 0, FRAMES - late), (h, FRAMES - late, late)]

    def channels_of(c, here):
        which, first, frames = plan[c]
        place = jnp.stack([here * share // ROWS + which, far_here])
        *outs, kept = channelise(place, volts, prototype, constants, first, frames, far)
        if sub < ROWS:
            outs = [lax.dynamic_slice_in_dim(x, inside, sub, axis=2) for x in outs]
        inner = st_count // RADIX
        if inner > 1:
            outs = [
                x.reshape(near // inner, sb_count, sub, 2 * frames, RADIX, inner, fine).transpose(0, 5, 1, 2, 3, 4, 6)
                for x in outs
            ]
        return [x.reshape(plane, sub, -1) for x in outs], kept

    lists = (assign, beam_channels, station_index)
    here = sb_here
    outs, kept = channels_of(0, here)
    branches, arrived, crossed = [kept], [], None
    for c in range(1, len(plan)):
        outs, crossed, here, lists, arrived[-1:] = barrier((outs, crossed, here, lists, arrived[-1:]))
        if crossed is not None:
            arrived.append(in_plane(crossed))
        crossed = to_planes(outs)
        outs, kept = channels_of(c, here)
        branches.append(kept)

    outs, crossed, lists, branches, arrived[-1:] = barrier((outs, crossed, lists, branches, arrived[-1:]))
    arrived.append(in_plane(crossed))
    crossed = to_planes(outs)
    assign, beam_channels, station_index = lists
    per_dev = SLOTS // st_count
    owners = assign[:, 0]
    taken = (owners[:, None] == jnp.arange(sb_count, dtype=jnp.int32)[None, :]).astype(jnp.int32)
    position = jnp.sum(taken * jnp.cumsum(taken, axis=0), axis=1) - 1
    place = owners * SLOTS + position
    slot_ids = (
        (partner[:, None] * near + jnp.arange(near, dtype=jnp.int32)).reshape(-1)[:, None, None] * per_dev
        + jnp.arange(sb_count, dtype=jnp.int32)[:, None] * SLOTS
        + jnp.arange(per_dev, dtype=jnp.int32)
    ).reshape(-1)
    picker = (place[None, :] == slot_ids[:, None]).astype(jnp.int32)
    filled = jnp.sum(picker, axis=1)
    slot_channel = jnp.sum(picker * beam_channels[None, :], axis=1)

    def by_row(values):
        return jnp.broadcast_to(values.reshape(devices, 1, per_dev), (devices, 2, per_dev)).reshape(-1)

    turned = jnp.broadcast_to(jnp.arange(2, dtype=jnp.int32)[None, :, None], (devices, 2, per_dev)).reshape(-1)
    mine = lax.dynamic_slice_in_dim(slot_channel, (near_here * sb_count + sb_here) * per_dev, per_dev)
    tables = slot_tables(by_row(slot_channel), by_row(filled), turned)
    spectra = slot_spectra(tables, branches, 2 * per_dev, far)
    if sub < ROWS:
        spectra = [
            lax.dynamic_slice_in_dim(x.reshape(plane, 2 * per_dev, FRAMES, ROWS), inside, sub, axis=3).reshape(
                plane, 2 * per_dev, -1
            )
            for x in spectra
        ]

    crossed, spectra, mine, arrived[-1:] = barrier((crossed, spectra, mine, arrived[-1:]))
    arrived.append(in_plane(crossed))
    slot_crossed = to_planes(spectra)
    weights = beam_weights(mine, delays, gains)
    signal_ids = (
        (partner[:, None] * (near * sig_dev) + jnp.arange(halves, dtype=jnp.int32) * sub)[:, :, None, None]
        + jnp.arange(plane, dtype=jnp.int32)[:, None] * share
        + jnp.arange(sub, dtype=jnp.int32)
    ).reshape(-1)
    wanted = (station_index[None, :] * 2 + jnp.arange(2, dtype=jnp.int32)[:, None]).reshape(-1)
    chooser = (signal_ids[:, None] == wanted[None, :]).astype(jnp.bfloat16)

    slot_crossed, weights, chooser, arrived[-1:] = barrier((slot_crossed, weights, chooser, arrived[-1:]))
    slot_received = in_plane(slot_crossed)
    pieces = []
    for x, part in zip(arrived, plan):
        for s in range(far):
            if halves == 1:
                pieces.append((x[:, s * sub : (s + 1) * sub].reshape(1, plane * sub, -1), s, 0, *part))
            else:
                pieces.append((x, s, s * sub, *part))
    visibility = correlate(far_here[None], pieces, far, halves, group)
    signals = visibility.shape[1]
    beam_out = combine(slot_received, chooser, weights, sub)
    return (visibility.reshape(2, 1, 1, signals, signals), beam_out)


def solution(mesh):
    st_count, sb_count = mesh.shape["st"], mesh.shape["sb"]
    far = math.gcd(4, st_count)
    planes = Mesh(mesh.devices.reshape(far, st_count // far, sb_count), ("far", "near", "sb"))
    st = ("far", "near")
    in_specs = (P(None, st, None), P(), P(), P(), P(), P(), P())
    out_specs = (P(None, "sb", st, None, None), P("sb", st, None, None, None))
    return jax.shard_map(body, mesh=planes, in_specs=in_specs, out_specs=out_specs, check_vma=False)
```

```python
import functools
import math

import jax
import jax.numpy as jnp
import numpy as np
from jax import lax
from jax.experimental import pallas as pl
from jax.experimental.pallas import tpu as pltpu
from jax.sharding import Mesh
from jax.sharding import PartitionSpec as P

NCH = 4096
FRAMES = 16
SLOTS = 160
RADIX = 8
LANES = 128
ROWS = 16
EARLY = 4
VMEM = 56 * 1024 * 1024

NO_COST = pl.CostEstimate(flops=1, bytes_accessed=1, transcendentals=0)

TWO_PI = 2.0 * math.pi
NT = (((1,), (1,)), ((), ()))


def busy(share):
    return pl.CostEstimate(flops=int(share * 1e10), bytes_accessed=1, transcendentals=0)


def phase(turns, length):
    angles = (turns % length).astype(jnp.float32) * (TWO_PI / length)
    return jnp.cos(angles), jnp.sin(angles)


def transform_tables():
    depth = NCH // RADIX
    ids = np.arange(depth)
    angles = 2 * np.pi / depth * (ids[:, None] * ids[None, :] % depth)
    turns = 2 * np.pi / NCH * (np.arange(RADIX)[:, None] * ids[None, :])
    scale = 1.0 / math.sqrt(NCH)
    both = (np.cos(angles) * scale, np.sin(angles) * scale, np.cos(turns), np.sin(turns))
    return [jnp.asarray(x.astype(np.float32)) for x in both]


def radix8(re, im):
    half = math.sqrt(0.5)

    def four(xr, xi):
        ar, ai, br, bi = xr[0] + xr[2], xi[0] + xi[2], xr[0] - xr[2], xi[0] - xi[2]
        cr, ci, dr, di = xr[1] + xr[3], xi[1] + xi[3], xr[1] - xr[3], xi[1] - xi[3]
        return [ar + cr, br + di, ar - cr, br - di], [ai + ci, bi - dr, ai - ci, bi + dr]

    er, ei = four(re[0::2], im[0::2])
    odd_r, odd_i = four(re[1::2], im[1::2])
    tr = [odd_r[0], (odd_r[1] + odd_i[1]) * half, odd_i[2], (odd_i[3] - odd_r[3]) * half]
    ti = [odd_i[0], (odd_i[1] - odd_r[1]) * half, -odd_r[2], (odd_r[3] + odd_i[3]) * -half]
    return (
        [e + t for e, t in zip(er, tr)] + [e - t for e, t in zip(er, tr)],
        [e + t for e, t in zip(ei, ti)] + [e - t for e, t in zip(ei, ti)],
    )


def swap_blocks(parts, lane_ids):
    count = len(parts)
    width = LANES // count
    parts = list(parts)
    step = 1
    while step < count:
        keep = (lane_ids // width) % (2 * step) < step
        for b in range(count):
            if b & step == 0:
                low, high = parts[b], parts[b + step]
                parts[b] = jnp.where(keep, low, pltpu.roll(high, step * width, 1))
                parts[b + step] = jnp.where(keep, pltpu.roll(low, LANES - step * width, 1), high)
        step *= 2
    return parts


def gather_blocks(parts, lane_ids):
    count = len(parts)
    width = LANES // count
    turned = [parts[0]] + [pltpu.roll(parts[b], b * width, 1) for b in range(1, count)]
    turned = [turned[-b % count] for b in range(count)]
    step = 1
    while step < count:
        moved = (lane_ids // width) & step != 0
        turned = [jnp.where(moved, turned[(g - step) % count], turned[g]) for g in range(count)]
        step *= 2
    return [turned[0]] + [pltpu.roll(turned[g], LANES - g * width, 1) for g in range(1, count)]


def channel_kernel(first, row_block, volts, prototype, cosines, sines, turn_c, turn_s, out, branches, *scratch):
    taps_wide, table, filtered, product = scratch
    near = out.shape[1]
    taps = taps_wide.shape[0]
    length = taps_wide.shape[2]
    frames = filtered.shape[2]
    depth = length // RADIX
    bands = depth // LANES
    for t in range(taps):
        taps_wide[t] = jnp.broadcast_to(prototype[t : t + 1, :], taps_wide.shape[1:])
    cos_t, sin_t = cosines[...].astype(table.dtype), sines[...].astype(table.dtype)
    table[:depth, :depth] = cos_t
    table[:depth, depth:] = -sin_t
    table[depth:, :depth] = sin_t
    table[depth:, depth:] = cos_t

    def column(j, carry):
        lane = pl.multiple_of(j * LANES, LANES)

        def strip(n1, inner):
            base = pl.multiple_of(n1 * depth + j * LANES, LANES)
            for part in range(2):
                sums = [None] * frames
                for seg in range(frames + taps - 1):
                    start = pl.multiple_of((first + seg) * length + base, LANES)
                    value = volts[part, :, pl.ds(start, LANES)].astype(jnp.float32)
                    for f in range(max(0, seg - taps + 1), min(frames, seg + 1)):
                        coef = taps_wide[seg - f, :, pl.ds(base, LANES)]
                        term = value * jnp.concatenate([coef, coef], axis=0)
                        sums[f] = term if sums[f] is None else sums[f] + term
                    if seg >= taps - 1:
                        filtered[part, n1, seg - taps + 1] = sums[seg - taps + 1]
            return inner

        lax.fori_loop(0, RADIX, strip, 0)

        def butterfly(f, inner):
            re, im = radix8(
                [filtered[0, n1, f] for n1 in range(RADIX)],
                [filtered[1, n1, f] for n1 in range(RADIX)],
            )
            for b in range(RADIX):
                turned_r, turned_i = re[b], im[b]
                if b > 0:
                    cos_t, sin_t = turn_c[b : b + 1, pl.ds(lane, LANES)], turn_s[b : b + 1, pl.ds(lane, LANES)]
                    turned_r, turned_i = re[b] * cos_t + im[b] * sin_t, im[b] * cos_t - re[b] * sin_t
                branches[b, f, :, pl.ds(lane, LANES)] = turned_r.astype(branches.dtype)
                branches[b, f, :, pl.ds(pl.multiple_of(depth + lane, LANES), LANES)] = turned_i.astype(branches.dtype)
            return inner

        lax.fori_loop(0, frames, butterfly, 0)
        return carry

    lax.fori_loop(0, bands, column, 0)

    rows = frames * ROWS
    joined = RADIX
    while joined * rows > 1024:
        joined //= 2

    def multiply(step, carry):
        some = pl.ds(step // bands * joined, joined)
        lanes = pl.ds(pl.multiple_of(step % bands * 2 * LANES, 2 * LANES), 2 * LANES)
        left = branches[some].reshape(joined * rows, 2 * depth)
        got = jnp.dot(left, table[:, lanes], preferred_element_type=jnp.float32)
        product[some, :, lanes] = got.reshape(joined, rows, 2 * LANES)
        return carry

    lax.fori_loop(0, RADIX // joined * bands, multiply, 0)
    lane_ids = lax.broadcasted_iota(jnp.int32, (ROWS, LANES), 1)

    def regroup(f, carry):
        top = pl.multiple_of(f * ROWS, ROWS)
        for part in range(2):
            for band in range(bands):
                lane = part * depth + band * LANES
                pieces = [product[b, pl.ds(top, ROWS), lane : lane + LANES] for b in range(RADIX)]
                for g, piece in enumerate(gather_blocks(pieces, lane_ids)):
                    at = pl.multiple_of((part * frames + f) * LANES, LANES)
                    out[band, g % near, g // near, :, pl.ds(at, LANES)] = piece.astype(out.dtype)
        return carry

    lax.fori_loop(0, frames, regroup, 0)


def channelise(row_block, volts, prototype, tables, first, frames, far):
    near = RADIX // far
    taps = prototype.shape[0]
    length = volts.shape[2] if first > 0 else (frames + taps - 1) * NCH
    depth = NCH // RADIX
    bands = depth // LANES
    wide = 2 * frames * LANES
    return pl.pallas_call(
        functools.partial(channel_kernel, first),
        grid_spec=pltpu.PrefetchScalarGridSpec(
            num_scalar_prefetch=1,
            grid=(1,),
            in_specs=[
                pl.BlockSpec((2, ROWS, length), lambda i, row: (0, row[0], 0)),
            ]
            + [pl.BlockSpec(x.shape, lambda i, row: (0, 0)) for x in (prototype, *tables)],
            out_specs=[
                pl.BlockSpec((bands, near, far, ROWS, wide), lambda i, row: (0, 0, 0, 0, 0)),
                pl.BlockSpec((RADIX, frames, ROWS, 2 * depth), lambda i, row: (0, 0, 0, 0)),
            ],
            scratch_shapes=[
                pltpu.VMEM((taps, 8, NCH), jnp.float32),
                pltpu.VMEM((2 * depth, 2 * depth), jnp.bfloat16),
                pltpu.VMEM((2, RADIX, frames, ROWS, LANES), jnp.float32),
                pltpu.VMEM((RADIX, frames * ROWS, 2 * depth), jnp.float32),
            ],
        ),
        out_shape=[
            jax.ShapeDtypeStruct((bands, near, far, ROWS, wide), jnp.bfloat16),
            jax.ShapeDtypeStruct((RADIX, frames, ROWS, 2 * depth), jnp.bfloat16),
        ],
        compiler_params=pltpu.CompilerParams(vmem_limit_bytes=VMEM),
        cost_estimate=busy(frames / FRAMES),
    )(row_block, volts, prototype, *tables)


def slot_kernel(row_branch, hi_c, hi_s, lo_c, lo_s, *rest):
    chunks, (out, table, total) = rest[:-3], rest[-3:]
    depth = chunks[0].shape[3] // 2
    for a in range(hi_c.shape[1]):
        high_c, high_s = hi_c[:, a : a + 1], hi_s[:, a : a + 1]
        table[:, a * LANES : (a + 1) * LANES] = (high_c * lo_c[...] - high_s * lo_s[...]).astype(table.dtype)
        table[:, depth + a * LANES : depth + (a + 1) * LANES] = (
            high_s * lo_c[...] + high_c * lo_s[...]
        ).astype(table.dtype)
    total[...] = jnp.zeros_like(total)

    def branch(b, carry):
        rows = jnp.concatenate([c[b].reshape(c.shape[1] * c.shape[2], c.shape[3]) for c in chunks], axis=0)
        got = lax.dot_general(table[...], rows, NT, preferred_element_type=jnp.float32)
        total[...] = jnp.where(row_branch[...] == b, got, total[...])
        return carry

    lax.fori_loop(0, RADIX, branch, 0)
    per = out.shape[1]
    for d in range(out.shape[0]):
        out[d] = total[d * per : (d + 1) * per].astype(out.dtype)


def slot_tables(row_channel, row_filled, row_turned):
    depth = NCH // RADIX
    coarse = jnp.arange(depth // LANES, dtype=jnp.int32) * LANES
    fine = jnp.arange(LANES, dtype=jnp.int32)
    whole = row_channel - row_channel % RADIX
    hi_c, hi_s = phase(whole[:, None] * coarse[None, :] + row_turned[:, None] * (NCH // 4), NCH)
    lo_c, lo_s = phase(whole[:, None] * fine[None, :], NCH)
    scaling = row_filled.astype(jnp.float32)[:, None] * (1.0 / math.sqrt(NCH))
    return (row_channel % RADIX)[:, None], hi_c * scaling, hi_s * scaling, lo_c, lo_s


def slot_spectra(tables, chunks, per):
    rows = tables[0].shape[0]
    samples = sum(c.shape[1] * c.shape[2] for c in chunks)
    return pl.pallas_call(
        slot_kernel,
        out_shape=jax.ShapeDtypeStruct((rows // per, per, samples), jnp.bfloat16),
        scratch_shapes=[
            pltpu.VMEM((rows, chunks[0].shape[3]), jnp.bfloat16),
            pltpu.VMEM((rows, samples), jnp.float32),
        ],
        compiler_params=pltpu.CompilerParams(vmem_limit_bytes=VMEM),
        cost_estimate=busy(1),
    )(*tables, *chunks)


def correlate(pieces, halves, lanes):
    sb_count, near, far, sub, _ = pieces[0][0].shape
    half = FRAMES * lanes
    each = near * sb_count
    block = each * halves * sub
    signals = far * block

    def kernel(*refs):
        parts, (out, held, turned, made, in_sems, out_sems) = refs[: len(pieces)], refs[len(pieces) :]
        coming = [[] for _ in range(far)]
        for index, (_, which, first, frames) in enumerate(pieces):
            for q in range(far):
                for x in range(near):
                    for part in range(2):
                        src = parts[index].at[:, x, q, :, pl.ds(part * frames * lanes, frames * lanes)]
                        at = pl.ds(part * half + first * lanes, frames * lanes)
                        dst = held.at[q, pl.ds(x * sb_count, sb_count), which, :, at]
                        sem = in_sems.at[((index * far + q) * near + x) * 2 + part]
                        coming[q].append(pltpu.make_async_copy(src, dst, sem))
        for copies in coming:
            for copy in copies:
                copy.start()

        def rows_of(i):
            return pl.ds(i * block, block)

        inverse = 1.0 / half
        going = [[], []]
        slot = 0
        for i in range(far):
            for copy in coming[i]:
                copy.wait()
            left = held[i].reshape(block, 2 * half)
            turned[:, :half] = left[:, half:]
            turned[:, half:] = -left[:, :half]
            at_i = rows_of(i)
            for j in range(i + 1):
                right = held[j].reshape(block, 2 * half)
                at_j = rows_of(j)
                for copy in going[slot]:
                    copy.wait()
                going[slot] = []
                for part, rows in enumerate((left, turned[...])):
                    got = lax.dot_general(rows, right, NT, preferred_element_type=jnp.float32) * inverse
                    made[slot, part, 0] = got
                    going[slot].append(
                        pltpu.make_async_copy(
                            made.at[slot, part, 0], out.at[part, at_i, at_j], out_sems.at[slot, part, 0]
                        )
                    )
                    if i != j:
                        made[slot, part, 1] = got.T if part == 0 else -got.T
                        going[slot].append(
                            pltpu.make_async_copy(
                                made.at[slot, part, 1], out.at[part, at_j, at_i], out_sems.at[slot, part, 1]
                            )
                        )
                for copy in going[slot]:
                    copy.start()
                slot = 1 - slot
        for copies in going:
            for copy in copies:
                copy.wait()

    return pl.pallas_call(
        kernel,
        in_specs=[pl.BlockSpec(memory_space=pl.ANY)] * len(pieces),
        out_specs=pl.BlockSpec(memory_space=pl.ANY),
        out_shape=jax.ShapeDtypeStruct((2, signals, signals), jnp.float32),
        scratch_shapes=[
            pltpu.VMEM((far, each, halves, sub, 2 * half), jnp.bfloat16),
            pltpu.VMEM((block, 2 * half), jnp.bfloat16),
            pltpu.VMEM((2, 2, 2, block, block), jnp.float32),
            pltpu.SemaphoreType.DMA((2 * far * near * len(pieces),)),
            pltpu.SemaphoreType.DMA((2, 2, 2)),
        ],
        compiler_params=pltpu.CompilerParams(vmem_limit_bytes=VMEM // 2),
        cost_estimate=NO_COST,
    )(*[piece[0] for piece in pieces])


def weight_kernel(channel, delays, gains, out):
    beams = delays.shape[0]
    turns = delays[...] * (channel[pl.program_id(0)].astype(jnp.float32) * (1.0 / NCH))
    part = turns - jnp.floor(turns + 0.5)
    square = part * part
    cos_t = jnp.full_like(part, TWO_PI**16 / math.factorial(16))
    sin_t = jnp.full_like(part, -(TWO_PI**15) / math.factorial(15))
    for power in range(14, -1, -2):
        sign = -1.0 if power % 4 == 2 else 1.0
        cos_t = cos_t * square + sign * TWO_PI**power / math.factorial(power)
        if power > 0:
            sign = -1.0 if (power - 1) % 4 == 3 else 1.0
            sin_t = sin_t * square + sign * TWO_PI ** (power - 1) / math.factorial(power - 1)
    scaled = gains[...] * (1.0 / math.sqrt(gains.shape[1]))
    out[0, :beams] = (scaled * cos_t).astype(out.dtype)
    out[0, beams:] = (-scaled * sin_t * part).astype(out.dtype)


def beam_weights(channel, delays, gains):
    beams, listed = delays.shape
    slots = channel.shape[0]
    return pl.pallas_call(
        weight_kernel,
        grid=(slots,),
        in_specs=[
            pl.BlockSpec(memory_space=pltpu.SMEM),
            pl.BlockSpec(delays.shape, lambda i: (0, 0)),
            pl.BlockSpec(gains.shape, lambda i: (0, 0)),
        ],
        out_specs=pl.BlockSpec((1, 2 * beams, listed), lambda i: (i, 0, 0)),
        out_shape=jax.ShapeDtypeStruct((slots, 2 * beams, listed), jnp.bfloat16),
        cost_estimate=NO_COST,
    )(channel, delays, gains)


def combine(spectra, chooser, weights, sub):
    slots, beams2, listed = weights.shape
    beams = beams2 // 2
    rows = 2 * slots
    senders = spectra.shape[0]
    halves = spectra.shape[2] // (FRAMES * sub)
    count = LANES // sub
    inner = senders // count
    groups = halves * inner
    tiles = 2 * listed // LANES

    def kernel(spectrum, choose, weight_hbm, out, ordered, picked, weight, sem):
        coming = pltpu.make_async_copy(weight_hbm, weight, sem)
        coming.start()
        lane_ids = lax.broadcasted_iota(jnp.int32, (rows, LANES), 1)
        for h in range(halves):
            for q in range(inner):
                for t in range(FRAMES // count):
                    lane = h * FRAMES * sub + t * LANES
                    pieces = [
                        spectrum[q * count + i, :, lane : lane + LANES].astype(jnp.float32) for i in range(count)
                    ]
                    for f, piece in enumerate(swap_blocks(pieces, lane_ids)):
                        top = (t * count + f) * rows
                        group = (h * inner + q) * LANES
                        ordered[top : top + rows, group : group + LANES] = piece
        acc = jnp.dot(ordered[...].astype(jnp.bfloat16), choose[...], preferred_element_type=jnp.float32)
        for lane in range(tiles):
            picked[lane] = acc[:, lane * LANES : (lane + 1) * LANES]
        coming.wait()
        for i in range(slots):
            chosen = [
                jnp.concatenate(
                    [
                        picked[p * tiles // 2 + lane, pl.ds(part * slots + i, FRAMES, rows), :]
                        for lane in range(tiles // 2)
                    ],
                    axis=1,
                )
                for p in range(2)
                for part in range(2)
            ]
            stacked = jnp.concatenate(chosen, axis=0).astype(jnp.bfloat16)
            mixed = lax.dot_general(stacked, weight[i], NT, preferred_element_type=jnp.float32)
            for p in range(2):
                at = 2 * FRAMES * p
                of_re, of_im = mixed[at : at + FRAMES], mixed[at + FRAMES : at + 2 * FRAMES]
                out[0, i, 0, :, p * beams : (p + 1) * beams] = of_re[:, :beams] - of_im[:, beams:]
                out[0, i, 1, :, p * beams : (p + 1) * beams] = of_im[:, :beams] + of_re[:, beams:]

    return pl.pallas_call(
        kernel,
        in_specs=[pl.BlockSpec(memory_space=pltpu.VMEM)] * 2 + [pl.BlockSpec(memory_space=pl.ANY)],
        out_shape=jax.ShapeDtypeStruct((1, slots, 2, FRAMES, 2 * beams), jnp.float32),
        scratch_shapes=[
            pltpu.VMEM((FRAMES * rows, groups * LANES), jnp.float32),
            pltpu.VMEM((tiles, FRAMES * rows, LANES), jnp.float32),
            pltpu.VMEM(weights.shape, weights.dtype),
            pltpu.SemaphoreType.DMA,
        ],
        compiler_params=pltpu.CompilerParams(vmem_limit_bytes=VMEM // 2),
        cost_estimate=NO_COST,
    )(spectra, chooser, weights)


def body(volts, prototype, beam_channels, station_index, delays, gains, assign):
    sig_dev = volts.shape[1]
    far, near, sb_count = lax.axis_size("far"), lax.axis_size("near"), lax.axis_size("sb")
    far_here, near_here, sb_here = [lax.axis_index(name).astype(jnp.int32) for name in ("far", "near", "sb")]
    st_count = far * near
    devices = st_count * sb_count
    group = NCH // devices
    fine = group // RADIX
    constants = transform_tables()
    barrier = lax.optimization_barrier

    def exchange(x):
        return lax.all_to_all(x, ("sb", "near", "far"), split_axis=0, concat_axis=0, tiled=True)

    share = sig_dev // sb_count
    sub = min(share, ROWS)
    halves = max(1, share // ROWS)
    inside = (sb_here * share) % ROWS
    unit = max(1, LANES // group)
    early = max(unit, EARLY // unit * unit)
    plan = [(0, 0, early), (0, early, FRAMES - early)] + [(h, 0, FRAMES) for h in range(1, halves)]

    def channels_of(c, here):
        which, first, frames = plan[c]
        row_block = (here * share // ROWS + which)[None]
        out, kept = channelise(row_block, volts, prototype, constants, first, frames, far)
        if sub < ROWS:
            out = lax.dynamic_slice_in_dim(out, inside, sub, axis=3)
        inner = st_count // RADIX
        if inner > 1:
            out = out.reshape(sb_count, near // inner, far, sub, 2 * frames, RADIX, inner, fine)
            out = out.transpose(0, 1, 6, 2, 3, 4, 5, 7)
        return out.reshape(devices, sub, -1), kept

    lists = (assign, beam_channels, station_index)
    here = sb_here
    out, kept = channels_of(0, here)
    branches, arrived = [kept], []
    for c in range(1, len(plan)):
        out, here, lists, arrived[-1:] = barrier((out, here, lists, arrived[-1:]))
        arrived.append(exchange(out))
        out, kept = channels_of(c, here)
        branches.append(kept)

    assign, beam_channels, station_index = barrier((lists, kept))[0]
    per_dev = SLOTS // st_count
    owners = assign[:, 0]
    taken = (owners[:, None] == jnp.arange(sb_count, dtype=jnp.int32)[None, :]).astype(jnp.int32)
    position = jnp.sum(taken * jnp.cumsum(taken, axis=0), axis=1) - 1
    place = owners * SLOTS + position
    slot_ids = (
        jnp.arange(sb_count, dtype=jnp.int32)[:, None, None, None] * SLOTS
        + jnp.arange(near, dtype=jnp.int32)[:, None, None] * per_dev
        + jnp.arange(far, dtype=jnp.int32)[:, None] * (near * per_dev)
        + jnp.arange(per_dev, dtype=jnp.int32)
    ).reshape(-1)
    picker = (place[None, :] == slot_ids[:, None]).astype(jnp.int32)
    filled = jnp.sum(picker, axis=1)
    slot_channel = jnp.sum(picker * beam_channels[None, :], axis=1)

    def by_row(values):
        return jnp.broadcast_to(values.reshape(devices, 1, per_dev), (devices, 2, per_dev)).reshape(-1)

    turned = jnp.broadcast_to(jnp.arange(2, dtype=jnp.int32)[None, :, None], (devices, 2, per_dev)).reshape(-1)
    own = ((sb_here * near + near_here) * far + far_here) * per_dev
    mine = lax.dynamic_slice_in_dim(slot_channel, own, per_dev)
    tables = slot_tables(by_row(slot_channel), by_row(filled), turned)
    spectra = slot_spectra(tables, branches, 2 * per_dev)
    if sub < ROWS:
        spectra = spectra.reshape(devices, 2 * per_dev, FRAMES, ROWS)
        spectra = lax.dynamic_slice_in_dim(spectra, inside, sub, axis=3).reshape(devices, 2 * per_dev, -1)

    out, spectra, mine, arrived[-1:] = barrier((out, spectra, mine, arrived[-1:]))
    arrived.append(exchange(out))
    weights = beam_weights(mine, delays, gains)
    signal_ids = (
        jnp.arange(halves, dtype=jnp.int32)[:, None, None, None, None] * sub
        + jnp.arange(sb_count, dtype=jnp.int32)[:, None, None, None] * share
        + jnp.arange(near, dtype=jnp.int32)[:, None, None] * sig_dev
        + jnp.arange(far, dtype=jnp.int32)[:, None] * (near * sig_dev)
        + jnp.arange(sub, dtype=jnp.int32)
    ).reshape(-1)
    wanted = (station_index[None, :] * 2 + jnp.arange(2, dtype=jnp.int32)[:, None]).reshape(-1)
    chooser = (signal_ids[:, None] == wanted[None, :]).astype(jnp.bfloat16)

    spectra, weights, chooser, arrived[-1:] = barrier((spectra, weights, chooser, arrived[-1:]))
    slot_received = exchange(spectra)
    arrived = [x.reshape(sb_count, near, far, sub, -1) for x in arrived]
    if halves == 1:
        arrived = [x.transpose(2, 1, 0, 3, 4).reshape(1, 1, far, near * sb_count * sub, -1) for x in arrived]
    visibility = correlate([(x, *part) for x, part in zip(arrived, plan)], halves, group)
    signals = visibility.shape[1]
    beam_out = combine(slot_received, chooser, weights, sub)
    return (visibility.reshape(2, 1, 1, signals, signals), beam_out)


def solution(mesh):
    st_count, sb_count = mesh.shape["st"], mesh.shape["sb"]
    far = math.gcd(4, st_count)
    planes = Mesh(mesh.devices.reshape(far, st_count // far, sb_count), ("far", "near", "sb"))
    st = ("far", "near")
    in_specs = (P(None, st, None), P(), P(), P(), P(), P(), P())
    out_specs = (P(None, "sb", st, None, None), P("sb", st, None, None, None))
    return jax.shard_map(body, mesh=planes, in_specs=in_specs, out_specs=out_specs, check_vma=False)
```

```python
import functools
import math

import jax
import jax.numpy as jnp
import numpy as np
from jax import lax
from jax.experimental import pallas as pl
from jax.experimental.pallas import tpu as pltpu
from jax.sharding import Mesh
from jax.sharding import PartitionSpec as P

NCH = 4096
FRAMES = 16
SLOTS = 160
RADIX = 8
LANES = 128
ROWS = 16
EARLY = 4
VMEM = 56 * 1024 * 1024

NO_COST = pl.CostEstimate(flops=1, bytes_accessed=1, transcendentals=0)

TWO_PI = 2.0 * math.pi
NT = (((1,), (1,)), ((), ()))


def busy(share):
    return pl.CostEstimate(flops=int(share * 1e10), bytes_accessed=1, transcendentals=0)


def phase(turns, length):
    angles = (turns % length).astype(jnp.float32) * (TWO_PI / length)
    return jnp.cos(angles), jnp.sin(angles)


def transform_tables():
    depth = NCH // RADIX
    ids = np.arange(depth)
    angles = 2 * np.pi / depth * (ids[:, None] * ids[None, :] % depth)
    turns = 2 * np.pi / NCH * (np.arange(RADIX)[:, None] * ids[None, :])
    scale = 1.0 / math.sqrt(NCH)
    both = (np.cos(angles) * scale, np.sin(angles) * scale, np.cos(turns), np.sin(turns))
    return [jnp.asarray(x.astype(np.float32)) for x in both]


def radix8(re, im):
    half = math.sqrt(0.5)

    def four(xr, xi):
        ar, ai, br, bi = xr[0] + xr[2], xi[0] + xi[2], xr[0] - xr[2], xi[0] - xi[2]
        cr, ci, dr, di = xr[1] + xr[3], xi[1] + xi[3], xr[1] - xr[3], xi[1] - xi[3]
        return [ar + cr, br + di, ar - cr, br - di], [ai + ci, bi - dr, ai - ci, bi + dr]

    er, ei = four(re[0::2], im[0::2])
    odd_r, odd_i = four(re[1::2], im[1::2])
    tr = [odd_r[0], (odd_r[1] + odd_i[1]) * half, odd_i[2], (odd_i[3] - odd_r[3]) * half]
    ti = [odd_i[0], (odd_i[1] - odd_r[1]) * half, -odd_r[2], (odd_r[3] + odd_i[3]) * -half]
    return (
        [e + t for e, t in zip(er, tr)] + [e - t for e, t in zip(er, tr)],
        [e + t for e, t in zip(ei, ti)] + [e - t for e, t in zip(ei, ti)],
    )


def swap_blocks(parts, lane_ids):
    count = len(parts)
    width = LANES // count
    parts = list(parts)
    step = 1
    while step < count:
        keep = (lane_ids // width) % (2 * step) < step
        for b in range(count):
            if b & step == 0:
                low, high = parts[b], parts[b + step]
                parts[b] = jnp.where(keep, low, pltpu.roll(high, step * width, 1))
                parts[b + step] = jnp.where(keep, pltpu.roll(low, LANES - step * width, 1), high)
        step *= 2
    return parts


def gather_blocks(parts, lane_ids):
    count = len(parts)
    width = LANES // count
    turned = [parts[0]] + [pltpu.roll(parts[b], b * width, 1) for b in range(1, count)]
    turned = [turned[-b % count] for b in range(count)]
    step = 1
    while step < count:
        moved = (lane_ids // width) & step != 0
        turned = [jnp.where(moved, turned[(g - step) % count], turned[g]) for g in range(count)]
        step *= 2
    return [turned[0]] + [pltpu.roll(turned[g], LANES - g * width, 1) for g in range(1, count)]


def channel_kernel(first, row_block, volts_hbm, prototype, cosines, sines, turn_c, turn_s, out, branches, *scratch):
    volts, waves, taps_wide, table, filtered, product, sems = scratch
    near = out.shape[1]
    taps = taps_wide.shape[0]
    length = taps_wide.shape[2]
    frames = filtered.shape[3]
    depth = length // RADIX
    bands = depth // LANES
    top = pl.multiple_of(row_block[0] * ROWS, ROWS)
    reach = pl.ds(first * length, volts.shape[2])
    coming = [
        pltpu.make_async_copy(volts_hbm.at[part, pl.ds(top, ROWS), reach], volts.at[part], sems.at[part])
        for part in range(2)
    ]
    coming += [pltpu.make_async_copy(x, waves.at[i], sems.at[2 + i]) for i, x in enumerate((cosines, sines))]
    for copy in coming:
        copy.start()
    for t in range(taps):
        taps_wide[t] = jnp.broadcast_to(prototype[t : t + 1, :], taps_wide.shape[1:])

    for part in range(2):
        coming[part].wait()

        def strip(step, carry, part=part):
            j, n1 = step // RADIX, step % RADIX
            base = pl.multiple_of(n1 * depth + j * LANES, LANES)
            sums = [None] * frames
            for seg in range(frames + taps - 1):
                start = pl.multiple_of(seg * length + base, LANES)
                value = volts[part, :, pl.ds(start, LANES)].astype(jnp.float32)
                for f in range(max(0, seg - taps + 1), min(frames, seg + 1)):
                    coef = taps_wide[seg - f, :, pl.ds(base, LANES)]
                    term = value * jnp.concatenate([coef, coef], axis=0)
                    sums[f] = term if sums[f] is None else sums[f] + term
                if seg >= taps - 1:
                    filtered[j, part, n1, seg - taps + 1] = sums[seg - taps + 1]
            return carry

        lax.fori_loop(0, bands * RADIX, strip, 0)

    def column(j, carry):
        lane = pl.multiple_of(j * LANES, LANES)

        def butterfly(f, inner):
            re, im = radix8(
                [filtered[j, 0, n1, f] for n1 in range(RADIX)],
                [filtered[j, 1, n1, f] for n1 in range(RADIX)],
            )
            for b in range(RADIX):
                turned_r, turned_i = re[b], im[b]
                if b > 0:
                    cos_t, sin_t = turn_c[b : b + 1, pl.ds(lane, LANES)], turn_s[b : b + 1, pl.ds(lane, LANES)]
                    turned_r, turned_i = re[b] * cos_t + im[b] * sin_t, im[b] * cos_t - re[b] * sin_t
                branches[b, f, :, pl.ds(lane, LANES)] = turned_r.astype(branches.dtype)
                branches[b, f, :, pl.ds(pl.multiple_of(depth + lane, LANES), LANES)] = turned_i.astype(branches.dtype)
            return inner

        lax.fori_loop(0, frames, butterfly, 0)
        return carry

    lax.fori_loop(0, bands, column, 0)

    for copy in coming[2:]:
        copy.wait()
    cos_t, sin_t = waves[0].astype(table.dtype), waves[1].astype(table.dtype)
    table[:depth, :depth] = cos_t
    table[:depth, depth:] = -sin_t
    table[depth:, :depth] = sin_t
    table[depth:, depth:] = cos_t
    rows = frames * ROWS
    joined = RADIX
    while joined * rows > 1024:
        joined //= 2

    def multiply(step, carry):
        some = pl.ds(step // bands * joined, joined)
        lanes = pl.ds(pl.multiple_of(step % bands * 2 * LANES, 2 * LANES), 2 * LANES)
        left = branches[some].reshape(joined * rows, 2 * depth)
        got = jnp.dot(left, table[:, lanes], preferred_element_type=jnp.float32)
        product[some, :, lanes] = got.reshape(joined, rows, 2 * LANES)
        return carry

    lax.fori_loop(0, RADIX // joined * bands, multiply, 0)
    lane_ids = lax.broadcasted_iota(jnp.int32, (ROWS, LANES), 1)

    def regroup(f, carry):
        top = pl.multiple_of(f * ROWS, ROWS)
        for part in range(2):
            for band in range(bands):
                lane = part * depth + band * LANES
                pieces = [product[b, pl.ds(top, ROWS), lane : lane + LANES] for b in range(RADIX)]
                for g, piece in enumerate(gather_blocks(pieces, lane_ids)):
                    at = pl.multiple_of((part * frames + f) * LANES, LANES)
                    out[band, g % near, g // near, :, pl.ds(at, LANES)] = piece.astype(out.dtype)
        return carry

    lax.fori_loop(0, frames, regroup, 0)


def channelise(row_block, volts, prototype, tables, first, frames, far):
    near = RADIX // far
    taps = prototype.shape[0]
    length = (frames + taps - 1) * NCH
    depth = NCH // RADIX
    bands = depth // LANES
    wide = 2 * frames * LANES
    return pl.pallas_call(
        functools.partial(channel_kernel, first),
        grid_spec=pltpu.PrefetchScalarGridSpec(
            num_scalar_prefetch=1,
            grid=(1,),
            in_specs=[
                pl.BlockSpec(memory_space=pl.ANY),
                pl.BlockSpec(prototype.shape, lambda i, row: (0, 0)),
                pl.BlockSpec(memory_space=pl.ANY),
                pl.BlockSpec(memory_space=pl.ANY),
                pl.BlockSpec(tables[2].shape, lambda i, row: (0, 0)),
                pl.BlockSpec(tables[3].shape, lambda i, row: (0, 0)),
            ],
            out_specs=[
                pl.BlockSpec((bands, near, far, ROWS, wide), lambda i, row: (0, 0, 0, 0, 0)),
                pl.BlockSpec((RADIX, frames, ROWS, 2 * depth), lambda i, row: (0, 0, 0, 0)),
            ],
            scratch_shapes=[
                pltpu.VMEM((2, ROWS, length), jnp.bfloat16),
                pltpu.VMEM((2, depth, depth), jnp.float32),
                pltpu.VMEM((taps, 8, NCH), jnp.float32),
                pltpu.VMEM((2 * depth, 2 * depth), jnp.bfloat16),
                pltpu.VMEM((bands, 2, RADIX, frames, ROWS, LANES), jnp.float32),
                pltpu.VMEM((RADIX, frames * ROWS, 2 * depth), jnp.float32),
                pltpu.SemaphoreType.DMA((4,)),
            ],
        ),
        out_shape=[
            jax.ShapeDtypeStruct((bands, near, far, ROWS, wide), jnp.bfloat16),
            jax.ShapeDtypeStruct((RADIX, frames, ROWS, 2 * depth), jnp.bfloat16),
        ],
        compiler_params=pltpu.CompilerParams(vmem_limit_bytes=VMEM),
        cost_estimate=busy(frames / FRAMES),
    )(row_block, volts, prototype, *tables)


def slot_kernel(row_branch, hi_c, hi_s, lo_c, lo_s, *rest):
    chunks, (out, table, total) = rest[:-3], rest[-3:]
    depth = chunks[0].shape[3] // 2
    for a in range(hi_c.shape[1]):
        high_c, high_s = hi_c[:, a : a + 1], hi_s[:, a : a + 1]
        table[:, a * LANES : (a + 1) * LANES] = (high_c * lo_c[...] - high_s * lo_s[...]).astype(table.dtype)
        table[:, depth + a * LANES : depth + (a + 1) * LANES] = (
            high_s * lo_c[...] + high_c * lo_s[...]
        ).astype(table.dtype)
    total[...] = jnp.zeros_like(total)

    def branch(b, carry):
        rows = jnp.concatenate([c[b].reshape(c.shape[1] * c.shape[2], c.shape[3]) for c in chunks], axis=0)
        got = lax.dot_general(table[...], rows, NT, preferred_element_type=jnp.float32)
        total[...] = jnp.where(row_branch[...] == b, got, total[...])
        return carry

    lax.fori_loop(0, RADIX, branch, 0)
    per = out.shape[1]
    for d in range(out.shape[0]):
        out[d] = total[d * per : (d + 1) * per].astype(out.dtype)


def slot_tables(row_channel, row_filled, row_turned):
    depth = NCH // RADIX
    coarse = jnp.arange(depth // LANES, dtype=jnp.int32) * LANES
    fine = jnp.arange(LANES, dtype=jnp.int32)
    whole = row_channel - row_channel % RADIX
    hi_c, hi_s = phase(whole[:, None] * coarse[None, :] + row_turned[:, None] * (NCH // 4), NCH)
    lo_c, lo_s = phase(whole[:, None] * fine[None, :], NCH)
    scaling = row_filled.astype(jnp.float32)[:, None] * (1.0 / math.sqrt(NCH))
    return (row_channel % RADIX)[:, None], hi_c * scaling, hi_s * scaling, lo_c, lo_s


def slot_spectra(tables, chunks, per):
    rows = tables[0].shape[0]
    samples = sum(c.shape[1] * c.shape[2] for c in chunks)
    return pl.pallas_call(
        slot_kernel,
        out_shape=jax.ShapeDtypeStruct((rows // per, per, samples), jnp.bfloat16),
        scratch_shapes=[
            pltpu.VMEM((rows, chunks[0].shape[3]), jnp.bfloat16),
            pltpu.VMEM((rows, samples), jnp.float32),
        ],
        compiler_params=pltpu.CompilerParams(vmem_limit_bytes=VMEM),
        cost_estimate=busy(1),
    )(*tables, *chunks)


def correlate(pieces, halves, lanes):
    sb_count, near, far, sub, _ = pieces[0][0].shape
    half = FRAMES * lanes
    each = near * sb_count
    block = each * halves * sub
    signals = far * block

    def kernel(*refs):
        parts, (out, held, turned, made, in_sems, out_sems) = refs[: len(pieces)], refs[len(pieces) :]
        coming = [[] for _ in range(far)]
        for index, (_, which, first, frames) in enumerate(pieces):
            for q in range(far):
                for x in range(near):
                    for part in range(2):
                        src = parts[index].at[:, x, q, :, pl.ds(part * frames * lanes, frames * lanes)]
                        at = pl.ds(part * half + first * lanes, frames * lanes)
                        dst = held.at[q, pl.ds(x * sb_count, sb_count), which, :, at]
                        sem = in_sems.at[((index * far + q) * near + x) * 2 + part]
                        coming[q].append(pltpu.make_async_copy(src, dst, sem))
        for copies in coming:
            for copy in copies:
                copy.start()

        def rows_of(i):
            return pl.ds(i * block, block)

        inverse = 1.0 / half
        going = [[], []]
        slot = 0
        for i in range(far):
            for copy in coming[i]:
                copy.wait()
            left = held[i].reshape(block, 2 * half)
            turned[:, :half] = left[:, half:]
            turned[:, half:] = -left[:, :half]
            at_i = rows_of(i)
            for j in range(i + 1):
                right = held[j].reshape(block, 2 * half)
                at_j = rows_of(j)
                for copy in going[slot]:
                    copy.wait()
                going[slot] = []
                for part, rows in enumerate((left, turned[...])):
                    got = lax.dot_general(rows, right, NT, preferred_element_type=jnp.float32) * inverse
                    made[slot, part, 0] = got
                    going[slot].append(
                        pltpu.make_async_copy(
                            made.at[slot, part, 0], out.at[part, at_i, at_j], out_sems.at[slot, part, 0]
                        )
                    )
                    if i != j:
                        made[slot, part, 1] = got.T if part == 0 else -got.T
                        going[slot].append(
                            pltpu.make_async_copy(
                                made.at[slot, part, 1], out.at[part, at_j, at_i], out_sems.at[slot, part, 1]
                            )
                        )
                for copy in going[slot]:
                    copy.start()
                slot = 1 - slot
        for copies in going:
            for copy in copies:
                copy.wait()

    return pl.pallas_call(
        kernel,
        in_specs=[pl.BlockSpec(memory_space=pl.ANY)] * len(pieces),
        out_specs=pl.BlockSpec(memory_space=pl.ANY),
        out_shape=jax.ShapeDtypeStruct((2, signals, signals), jnp.float32),
        scratch_shapes=[
            pltpu.VMEM((far, each, halves, sub, 2 * half), jnp.bfloat16),
            pltpu.VMEM((block, 2 * half), jnp.bfloat16),
            pltpu.VMEM((2, 2, 2, block, block), jnp.float32),
            pltpu.SemaphoreType.DMA((2 * far * near * len(pieces),)),
            pltpu.SemaphoreType.DMA((2, 2, 2)),
        ],
        compiler_params=pltpu.CompilerParams(vmem_limit_bytes=VMEM // 2),
        cost_estimate=NO_COST,
    )(*[piece[0] for piece in pieces])


def weight_kernel(channel, delays, gains, out):
    beams = delays.shape[0]
    turns = delays[...] * (channel[pl.program_id(0)].astype(jnp.float32) * (1.0 / NCH))
    part = turns - jnp.floor(turns + 0.5)
    square = part * part
    cos_t = jnp.full_like(part, TWO_PI**16 / math.factorial(16))
    sin_t = jnp.full_like(part, -(TWO_PI**15) / math.factorial(15))
    for power in range(14, -1, -2):
        sign = -1.0 if power % 4 == 2 else 1.0
        cos_t = cos_t * square + sign * TWO_PI**power / math.factorial(power)
        if power > 0:
            sign = -1.0 if (power - 1) % 4 == 3 else 1.0
            sin_t = sin_t * square + sign * TWO_PI ** (power - 1) / math.factorial(power - 1)
    scaled = gains[...] * (1.0 / math.sqrt(gains.shape[1]))
    out[0, :beams] = (scaled * cos_t).astype(out.dtype)
    out[0, beams:] = (-scaled * sin_t * part).astype(out.dtype)


def beam_weights(channel, delays, gains):
    beams, listed = delays.shape
    slots = channel.shape[0]
    return pl.pallas_call(
        weight_kernel,
        grid=(slots,),
        in_specs=[
            pl.BlockSpec(memory_space=pltpu.SMEM),
            pl.BlockSpec(delays.shape, lambda i: (0, 0)),
            pl.BlockSpec(gains.shape, lambda i: (0, 0)),
        ],
        out_specs=pl.BlockSpec((1, 2 * beams, listed), lambda i: (i, 0, 0)),
        out_shape=jax.ShapeDtypeStruct((slots, 2 * beams, listed), jnp.bfloat16),
        cost_estimate=NO_COST,
    )(channel, delays, gains)


def combine(spectra, chooser, weights, sub):
    slots, beams2, listed = weights.shape
    beams = beams2 // 2
    rows = 2 * slots
    senders = spectra.shape[0]
    halves = spectra.shape[2] // (FRAMES * sub)
    count = LANES // sub
    inner = senders // count
    groups = halves * inner
    tiles = 2 * listed // LANES

    def kernel(spectrum, choose, weight_hbm, out, ordered, picked, weight, sem):
        coming = pltpu.make_async_copy(weight_hbm, weight, sem)
        coming.start()
        lane_ids = lax.broadcasted_iota(jnp.int32, (rows, LANES), 1)
        for h in range(halves):
            for q in range(inner):
                for t in range(FRAMES // count):
                    lane = h * FRAMES * sub + t * LANES
                    pieces = [
                        spectrum[q * count + i, :, lane : lane + LANES].astype(jnp.float32) for i in range(count)
                    ]
                    for f, piece in enumerate(swap_blocks(pieces, lane_ids)):
                        top = (t * count + f) * rows
                        group = (h * inner + q) * LANES
                        ordered[top : top + rows, group : group + LANES] = piece
        acc = jnp.dot(ordered[...].astype(jnp.bfloat16), choose[...], preferred_element_type=jnp.float32)
        for lane in range(tiles):
            picked[lane] = acc[:, lane * LANES : (lane + 1) * LANES]
        coming.wait()
        for i in range(slots):
            chosen = [
                jnp.concatenate(
                    [
                        picked[p * tiles // 2 + lane, pl.ds(part * slots + i, FRAMES, rows), :]
                        for lane in range(tiles // 2)
                    ],
                    axis=1,
                )
                for p in range(2)
                for part in range(2)
            ]
            stacked = jnp.concatenate(chosen, axis=0).astype(jnp.bfloat16)
            mixed = lax.dot_general(stacked, weight[i], NT, preferred_element_type=jnp.float32)
            for p in range(2):
                at = 2 * FRAMES * p
                of_re, of_im = mixed[at : at + FRAMES], mixed[at + FRAMES : at + 2 * FRAMES]
                out[0, i, 0, :, p * beams : (p + 1) * beams] = of_re[:, :beams] - of_im[:, beams:]
                out[0, i, 1, :, p * beams : (p + 1) * beams] = of_im[:, :beams] + of_re[:, beams:]

    return pl.pallas_call(
        kernel,
        in_specs=[pl.BlockSpec(memory_space=pltpu.VMEM)] * 2 + [pl.BlockSpec(memory_space=pl.ANY)],
        out_shape=jax.ShapeDtypeStruct((1, slots, 2, FRAMES, 2 * beams), jnp.float32),
        scratch_shapes=[
            pltpu.VMEM((FRAMES * rows, groups * LANES), jnp.float32),
            pltpu.VMEM((tiles, FRAMES * rows, LANES), jnp.float32),
            pltpu.VMEM(weights.shape, weights.dtype),
            pltpu.SemaphoreType.DMA,
        ],
        compiler_params=pltpu.CompilerParams(vmem_limit_bytes=VMEM),
        cost_estimate=NO_COST,
    )(spectra, chooser, weights)


def body(volts, prototype, beam_channels, station_index, delays, gains, assign):
    sig_dev = volts.shape[1]
    far, near, sb_count = lax.axis_size("far"), lax.axis_size("near"), lax.axis_size("sb")
    far_here, near_here, sb_here = [lax.axis_index(name).astype(jnp.int32) for name in ("far", "near", "sb")]
    st_count = far * near
    devices = st_count * sb_count
    group = NCH // devices
    fine = group // RADIX
    constants = transform_tables()
    barrier = lax.optimization_barrier

    def exchange(x):
        return lax.all_to_all(x, ("sb", "near", "far"), split_axis=0, concat_axis=0, tiled=True)

    share = sig_dev // sb_count
    sub = min(share, ROWS)
    halves = max(1, share // ROWS)
    inside = (sb_here * share) % ROWS
    unit = max(1, LANES // group)
    early = max(unit, EARLY // unit * unit)
    plan = [(0, 0, early), (0, early, FRAMES - early)] + [(h, 0, FRAMES) for h in range(1, halves)]

    def channels_of(c, here):
        which, first, frames = plan[c]
        row_block = (here * share // ROWS + which)[None]
        out, kept = channelise(row_block, volts, prototype, constants, first, frames, far)
        if sub < ROWS:
            out = lax.dynamic_slice_in_dim(out, inside, sub, axis=3)
        inner = st_count // RADIX
        if inner > 1:
            out = out.reshape(sb_count, near // inner, far, sub, 2 * frames, RADIX, inner, fine)
            out = out.transpose(0, 1, 6, 2, 3, 4, 5, 7)
        return out.reshape(devices, sub, -1), kept

    lists = (assign, beam_channels, station_index)
    here = sb_here
    out, kept = channels_of(0, here)
    branches, arrived = [kept], []
    for c in range(1, len(plan)):
        out, here, lists, arrived[-1:] = barrier((out, here, lists, arrived[-1:]))
        arrived.append(exchange(out))
        out, kept = channels_of(c, here)
        branches.append(kept)

    assign, beam_channels, station_index = barrier((lists, kept))[0]
    per_dev = SLOTS // st_count
    owners = assign[:, 0]
    taken = (owners[:, None] == jnp.arange(sb_count, dtype=jnp.int32)[None, :]).astype(jnp.int32)
    position = jnp.sum(taken * jnp.cumsum(taken, axis=0), axis=1) - 1
    place = owners * SLOTS + position
    slot_ids = (
        jnp.arange(sb_count, dtype=jnp.int32)[:, None, None, None] * SLOTS
        + jnp.arange(near, dtype=jnp.int32)[:, None, None] * per_dev
        + jnp.arange(far, dtype=jnp.int32)[:, None] * (near * per_dev)
        + jnp.arange(per_dev, dtype=jnp.int32)
    ).reshape(-1)
    picker = (place[None, :] == slot_ids[:, None]).astype(jnp.int32)
    filled = jnp.sum(picker, axis=1)
    slot_channel = jnp.sum(picker * beam_channels[None, :], axis=1)

    def by_row(values):
        return jnp.broadcast_to(values.reshape(devices, 1, per_dev), (devices, 2, per_dev)).reshape(-1)

    turned = jnp.broadcast_to(jnp.arange(2, dtype=jnp.int32)[None, :, None], (devices, 2, per_dev)).reshape(-1)
    own = ((sb_here * near + near_here) * far + far_here) * per_dev
    mine = lax.dynamic_slice_in_dim(slot_channel, own, per_dev)
    tables = slot_tables(by_row(slot_channel), by_row(filled), turned)
    spectra = slot_spectra(tables, branches, 2 * per_dev)
    if sub < ROWS:
        spectra = spectra.reshape(devices, 2 * per_dev, FRAMES, ROWS)
        spectra = lax.dynamic_slice_in_dim(spectra, inside, sub, axis=3).reshape(devices, 2 * per_dev, -1)

    out, spectra, mine, arrived[-1:] = barrier((out, spectra, mine, arrived[-1:]))
    arrived.append(exchange(out))
    weights = beam_weights(mine, delays, gains)
    signal_ids = (
        jnp.arange(halves, dtype=jnp.int32)[:, None, None, None, None] * sub
        + jnp.arange(sb_count, dtype=jnp.int32)[:, None, None, None] * share
        + jnp.arange(near, dtype=jnp.int32)[:, None, None] * sig_dev
        + jnp.arange(far, dtype=jnp.int32)[:, None] * (near * sig_dev)
        + jnp.arange(sub, dtype=jnp.int32)
    ).reshape(-1)
    wanted = (station_index[None, :] * 2 + jnp.arange(2, dtype=jnp.int32)[:, None]).reshape(-1)
    chooser = (signal_ids[:, None] == wanted[None, :]).astype(jnp.bfloat16)

    spectra, weights, chooser, arrived[-1:] = barrier((spectra, weights, chooser, arrived[-1:]))
    slot_received = exchange(spectra)
    arrived = [x.reshape(sb_count, near, far, sub, -1) for x in arrived]
    if halves == 1:
        arrived = [x.transpose(2, 1, 0, 3, 4).reshape(1, 1, far, near * sb_count * sub, -1) for x in arrived]
    visibility = correlate([(x, *part) for x, part in zip(arrived, plan)], halves, group)
    signals = visibility.shape[1]
    beam_out = combine(slot_received, chooser, weights, sub)
    return (visibility.reshape(2, 1, 1, signals, signals), beam_out)


def solution(mesh):
    st_count, sb_count = mesh.shape["st"], mesh.shape["sb"]
    far = math.gcd(4, st_count)
    planes = Mesh(mesh.devices.reshape(far, st_count // far, sb_count), ("far", "near", "sb"))
    st = ("far", "near")
    in_specs = (P(None, st, None), P(), P(), P(), P(), P(), P())
    out_specs = (P(None, "sb", st, None, None), P("sb", st, None, None, None))
    return jax.shard_map(body, mesh=planes, in_specs=in_specs, out_specs=out_specs, check_vma=False)
```

```python
import functools
import math

import jax
import jax.numpy as jnp
import numpy as np
from jax import lax
from jax.experimental import pallas as pl
from jax.experimental.pallas import tpu as pltpu
from jax.sharding import Mesh
from jax.sharding import PartitionSpec as P

NCH = 4096
FRAMES = 16
SLOTS = 160
RADIX = 8
LANES = 128
ROWS = 16
EARLY = 4
VMEM = 56 * 1024 * 1024

NO_COST = pl.CostEstimate(flops=1, bytes_accessed=1, transcendentals=0)

TWO_PI = 2.0 * math.pi
NT = (((1,), (1,)), ((), ()))


def busy(share):
    return pl.CostEstimate(flops=int(share * 1e10), bytes_accessed=1, transcendentals=0)


def phase(turns, length):
    angles = (turns % length).astype(jnp.float32) * (TWO_PI / length)
    return jnp.cos(angles), jnp.sin(angles)


def transform_tables():
    depth = NCH // RADIX
    ids = np.arange(depth)
    angles = 2 * np.pi / depth * (ids[:, None] * ids[None, :] % depth)
    turns = 2 * np.pi / NCH * (np.arange(RADIX)[:, None] * ids[None, :])
    scale = 1.0 / math.sqrt(NCH)
    both = (np.cos(angles) * scale, np.sin(angles) * scale, np.cos(turns), np.sin(turns))
    return [jnp.asarray(x.astype(np.float32)) for x in both]


def radix8(re, im):
    half = math.sqrt(0.5)

    def four(xr, xi):
        ar, ai, br, bi = xr[0] + xr[2], xi[0] + xi[2], xr[0] - xr[2], xi[0] - xi[2]
        cr, ci, dr, di = xr[1] + xr[3], xi[1] + xi[3], xr[1] - xr[3], xi[1] - xi[3]
        return [ar + cr, br + di, ar - cr, br - di], [ai + ci, bi - dr, ai - ci, bi + dr]

    er, ei = four(re[0::2], im[0::2])
    odd_r, odd_i = four(re[1::2], im[1::2])
    tr = [odd_r[0], (odd_r[1] + odd_i[1]) * half, odd_i[2], (odd_i[3] - odd_r[3]) * half]
    ti = [odd_i[0], (odd_i[1] - odd_r[1]) * half, -odd_r[2], (odd_r[3] + odd_i[3]) * -half]
    return (
        [e + t for e, t in zip(er, tr)] + [e - t for e, t in zip(er, tr)],
        [e + t for e, t in zip(ei, ti)] + [e - t for e, t in zip(ei, ti)],
    )


def swap_blocks(parts, lane_ids):
    count = len(parts)
    width = LANES // count
    parts = list(parts)
    step = 1
    while step < count:
        keep = (lane_ids // width) % (2 * step) < step
        for b in range(count):
            if b & step == 0:
                low, high = parts[b], parts[b + step]
                parts[b] = jnp.where(keep, low, pltpu.roll(high, step * width, 1))
                parts[b + step] = jnp.where(keep, pltpu.roll(low, LANES - step * width, 1), high)
        step *= 2
    return parts


def gather_blocks(parts, lane_ids):
    count = len(parts)
    width = LANES // count
    turned = [parts[0]] + [pltpu.roll(parts[b], b * width, 1) for b in range(1, count)]
    turned = [turned[-b % count] for b in range(count)]
    step = 1
    while step < count:
        moved = (lane_ids // width) & step != 0
        turned = [jnp.where(moved, turned[(g - step) % count], turned[g]) for g in range(count)]
        step *= 2
    return [turned[0]] + [pltpu.roll(turned[g], LANES - g * width, 1) for g in range(1, count)]


def channel_kernel(first, row_block, volts_hbm, prototype, cosines, sines, turn_c, turn_s, out, branches, *scratch):
    volts, waves, taps_wide, table, filtered, product, sems = scratch
    near = out.shape[1]
    taps = taps_wide.shape[0]
    length = taps_wide.shape[2]
    frames = filtered.shape[3]
    depth = length // RADIX
    bands = depth // LANES
    top = pl.multiple_of(row_block[0] * ROWS, ROWS)
    reach = pl.ds(first * length, volts.shape[2])
    coming = [
        pltpu.make_async_copy(volts_hbm.at[part, pl.ds(top, ROWS), reach], volts.at[part], sems.at[part])
        for part in range(2)
    ]
    coming += [pltpu.make_async_copy(x, waves.at[i], sems.at[2 + i]) for i, x in enumerate((cosines, sines))]
    for copy in coming:
        copy.start()
    for t in range(taps):
        taps_wide[t] = jnp.broadcast_to(prototype[t : t + 1, :], taps_wide.shape[1:])

    def strip(part, step):
        j, n1 = step // RADIX, step % RADIX
        base = pl.multiple_of(n1 * depth + j * LANES, LANES)
        sums = [None] * frames
        for seg in range(frames + taps - 1):
            start = pl.multiple_of(seg * length + base, LANES)
            value = volts[part, :, pl.ds(start, LANES)].astype(jnp.float32)
            for f in range(max(0, seg - taps + 1), min(frames, seg + 1)):
                coef = taps_wide[seg - f, :, pl.ds(base, LANES)]
                term = value * jnp.concatenate([coef, coef], axis=0)
                sums[f] = term if sums[f] is None else sums[f] + term
            if seg >= taps - 1:
                filtered[j, part, n1, seg - taps + 1] = sums[seg - taps + 1]

    together = 4 if frames <= 4 else 1

    for part in range(2):
        coming[part].wait()

        def strips(step, carry, part=part):
            for k in range(together):
                strip(part, step * together + k)
            return carry

        lax.fori_loop(0, bands * RADIX // together, strips, 0)

    def column(j, carry):
        lane = pl.multiple_of(j * LANES, LANES)

        def butterfly(f):
            re, im = radix8(
                [filtered[j, 0, n1, f] for n1 in range(RADIX)],
                [filtered[j, 1, n1, f] for n1 in range(RADIX)],
            )
            for b in range(RADIX):
                turned_r, turned_i = re[b], im[b]
                if b > 0:
                    cos_t, sin_t = turn_c[b : b + 1, pl.ds(lane, LANES)], turn_s[b : b + 1, pl.ds(lane, LANES)]
                    turned_r, turned_i = re[b] * cos_t + im[b] * sin_t, im[b] * cos_t - re[b] * sin_t
                branches[b, f, :, pl.ds(lane, LANES)] = turned_r.astype(branches.dtype)
                branches[b, f, :, pl.ds(pl.multiple_of(depth + lane, LANES), LANES)] = turned_i.astype(branches.dtype)

        def pair(step, inner):
            butterfly(2 * step)
            butterfly(2 * step + 1)
            return inner

        lax.fori_loop(0, frames // 2, pair, 0)
        return carry

    lax.fori_loop(0, bands, column, 0)

    for copy in coming[2:]:
        copy.wait()
    cos_t, sin_t = waves[0].astype(table.dtype), waves[1].astype(table.dtype)
    table[:depth, :depth] = cos_t
    table[:depth, depth:] = -sin_t
    table[depth:, :depth] = sin_t
    table[depth:, depth:] = cos_t
    rows = frames * ROWS
    joined = RADIX
    while joined * rows > 1024:
        joined //= 2

    def multiply(step, carry):
        some = pl.ds(step // bands * joined, joined)
        lanes = pl.ds(pl.multiple_of(step % bands * 2 * LANES, 2 * LANES), 2 * LANES)
        left = branches[some].reshape(joined * rows, 2 * depth)
        got = jnp.dot(left, table[:, lanes], preferred_element_type=jnp.float32)
        product[some, :, lanes] = got.reshape(joined, rows, 2 * LANES)
        return carry

    lax.fori_loop(0, RADIX // joined * bands, multiply, 0)
    lane_ids = lax.broadcasted_iota(jnp.int32, (ROWS, LANES), 1)

    def regroup(f, carry):
        top = pl.multiple_of(f * ROWS, ROWS)
        for part in range(2):
            for band in range(bands):
                lane = part * depth + band * LANES
                pieces = [product[b, pl.ds(top, ROWS), lane : lane + LANES] for b in range(RADIX)]
                for g, piece in enumerate(gather_blocks(pieces, lane_ids)):
                    at = pl.multiple_of((part * frames + f) * LANES, LANES)
                    out[band, g % near, g // near, :, pl.ds(at, LANES)] = piece.astype(out.dtype)
        return carry

    lax.fori_loop(0, frames, regroup, 0)


def channelise(row_block, volts, prototype, tables, first, frames, far):
    near = RADIX // far
    taps = prototype.shape[0]
    length = (frames + taps - 1) * NCH
    depth = NCH // RADIX
    bands = depth // LANES
    wide = 2 * frames * LANES
    return pl.pallas_call(
        functools.partial(channel_kernel, first),
        grid_spec=pltpu.PrefetchScalarGridSpec(
            num_scalar_prefetch=1,
            grid=(1,),
            in_specs=[
                pl.BlockSpec(memory_space=pl.ANY),
                pl.BlockSpec(prototype.shape, lambda i, row: (0, 0)),
                pl.BlockSpec(memory_space=pl.ANY),
                pl.BlockSpec(memory_space=pl.ANY),
                pl.BlockSpec(tables[2].shape, lambda i, row: (0, 0)),
                pl.BlockSpec(tables[3].shape, lambda i, row: (0, 0)),
            ],
            out_specs=[
                pl.BlockSpec((bands, near, far, ROWS, wide), lambda i, row: (0, 0, 0, 0, 0)),
                pl.BlockSpec((RADIX, frames, ROWS, 2 * depth), lambda i, row: (0, 0, 0, 0)),
            ],
            scratch_shapes=[
                pltpu.VMEM((2, ROWS, length), jnp.bfloat16),
                pltpu.VMEM((2, depth, depth), jnp.float32),
                pltpu.VMEM((taps, 8, NCH), jnp.float32),
                pltpu.VMEM((2 * depth, 2 * depth), jnp.bfloat16),
                pltpu.VMEM((bands, 2, RADIX, frames, ROWS, LANES), jnp.float32),
                pltpu.VMEM((RADIX, frames * ROWS, 2 * depth), jnp.float32),
                pltpu.SemaphoreType.DMA((4,)),
            ],
        ),
        out_shape=[
            jax.ShapeDtypeStruct((bands, near, far, ROWS, wide), jnp.bfloat16),
            jax.ShapeDtypeStruct((RADIX, frames, ROWS, 2 * depth), jnp.bfloat16),
        ],
        compiler_params=pltpu.CompilerParams(vmem_limit_bytes=VMEM),
        cost_estimate=busy(frames / FRAMES),
    )(row_block, volts, prototype, *tables)


def slot_kernel(row_branch, hi_c, hi_s, lo_c, lo_s, *rest):
    chunks, (out, table, total) = rest[:-3], rest[-3:]
    depth = chunks[0].shape[3] // 2
    for a in range(hi_c.shape[1]):
        high_c, high_s = hi_c[:, a : a + 1], hi_s[:, a : a + 1]
        table[:, a * LANES : (a + 1) * LANES] = (high_c * lo_c[...] - high_s * lo_s[...]).astype(table.dtype)
        table[:, depth + a * LANES : depth + (a + 1) * LANES] = (
            high_s * lo_c[...] + high_c * lo_s[...]
        ).astype(table.dtype)
    total[...] = jnp.zeros_like(total)

    def branch(b, carry):
        rows = jnp.concatenate([c[b].reshape(c.shape[1] * c.shape[2], c.shape[3]) for c in chunks], axis=0)
        got = lax.dot_general(table[...], rows, NT, preferred_element_type=jnp.float32)
        total[...] = jnp.where(row_branch[...] == b, got, total[...])
        return carry

    lax.fori_loop(0, RADIX, branch, 0)
    per = out.shape[1]
    for d in range(out.shape[0]):
        out[d] = total[d * per : (d + 1) * per].astype(out.dtype)


def slot_tables(row_channel, row_filled, row_turned):
    depth = NCH // RADIX
    coarse = jnp.arange(depth // LANES, dtype=jnp.int32) * LANES
    fine = jnp.arange(LANES, dtype=jnp.int32)
    whole = row_channel - row_channel % RADIX
    hi_c, hi_s = phase(whole[:, None] * coarse[None, :] + row_turned[:, None] * (NCH // 4), NCH)
    lo_c, lo_s = phase(whole[:, None] * fine[None, :], NCH)
    scaling = row_filled.astype(jnp.float32)[:, None] * (1.0 / math.sqrt(NCH))
    return (row_channel % RADIX)[:, None], hi_c * scaling, hi_s * scaling, lo_c, lo_s


def slot_spectra(tables, chunks, per):
    rows = tables[0].shape[0]
    samples = sum(c.shape[1] * c.shape[2] for c in chunks)
    return pl.pallas_call(
        slot_kernel,
        out_shape=jax.ShapeDtypeStruct((rows // per, per, samples), jnp.bfloat16),
        scratch_shapes=[
            pltpu.VMEM((rows, chunks[0].shape[3]), jnp.bfloat16),
            pltpu.VMEM((rows, samples), jnp.float32),
        ],
        compiler_params=pltpu.CompilerParams(vmem_limit_bytes=VMEM),
        cost_estimate=busy(1),
    )(*tables, *chunks)


def correlate(pieces, halves, lanes):
    sb_count, near, far, sub, _ = pieces[0][0].shape
    half = FRAMES * lanes
    each = near * sb_count
    block = each * halves * sub
    signals = far * block

    def kernel(*refs):
        parts, (out, held, turned, made, in_sems, out_sems) = refs[: len(pieces)], refs[len(pieces) :]
        coming = [[] for _ in range(far)]
        for index, (_, which, first, frames) in enumerate(pieces):
            for q in range(far):
                for x in range(near):
                    for part in range(2):
                        src = parts[index].at[:, x, q, :, pl.ds(part * frames * lanes, frames * lanes)]
                        at = pl.ds(part * half + first * lanes, frames * lanes)
                        dst = held.at[q, pl.ds(x * sb_count, sb_count), which, :, at]
                        sem = in_sems.at[((index * far + q) * near + x) * 2 + part]
                        coming[q].append(pltpu.make_async_copy(src, dst, sem))
        for copies in coming:
            for copy in copies:
                copy.start()

        def rows_of(i):
            return pl.ds(i * block, block)

        inverse = 1.0 / half
        going = [[], []]
        slot = 0
        for i in range(far):
            for copy in coming[i]:
                copy.wait()
            left = held[i].reshape(block, 2 * half)
            turned[:, :half] = left[:, half:]
            turned[:, half:] = -left[:, :half]
            at_i = rows_of(i)
            for j in range(i + 1):
                right = held[j].reshape(block, 2 * half)
                at_j = rows_of(j)
                for copy in going[slot]:
                    copy.wait()
                going[slot] = []
                for part, rows in enumerate((left, turned[...])):
                    got = lax.dot_general(rows, right, NT, preferred_element_type=jnp.float32) * inverse
                    made[slot, part, 0] = got
                    going[slot].append(
                        pltpu.make_async_copy(
                            made.at[slot, part, 0], out.at[part, at_i, at_j], out_sems.at[slot, part, 0]
                        )
                    )
                    if i != j:
                        made[slot, part, 1] = got.T if part == 0 else -got.T
                        going[slot].append(
                            pltpu.make_async_copy(
                                made.at[slot, part, 1], out.at[part, at_j, at_i], out_sems.at[slot, part, 1]
                            )
                        )
                for copy in going[slot]:
                    copy.start()
                slot = 1 - slot
        for copies in going:
            for copy in copies:
                copy.wait()

    return pl.pallas_call(
        kernel,
        in_specs=[pl.BlockSpec(memory_space=pl.ANY)] * len(pieces),
        out_specs=pl.BlockSpec(memory_space=pl.ANY),
        out_shape=jax.ShapeDtypeStruct((2, signals, signals), jnp.float32),
        scratch_shapes=[
            pltpu.VMEM((far, each, halves, sub, 2 * half), jnp.bfloat16),
            pltpu.VMEM((block, 2 * half), jnp.bfloat16),
            pltpu.VMEM((2, 2, 2, block, block), jnp.float32),
            pltpu.SemaphoreType.DMA((2 * far * near * len(pieces),)),
            pltpu.SemaphoreType.DMA((2, 2, 2)),
        ],
        compiler_params=pltpu.CompilerParams(vmem_limit_bytes=VMEM // 2),
        cost_estimate=NO_COST,
    )(*[piece[0] for piece in pieces])


def weight_kernel(channel, delays, gains, out):
    beams = delays.shape[0]
    turns = delays[...] * (channel[pl.program_id(0)].astype(jnp.float32) * (1.0 / NCH))
    part = turns - jnp.floor(turns + 0.5)
    square = part * part
    cos_t = jnp.full_like(part, TWO_PI**16 / math.factorial(16))
    sin_t = jnp.full_like(part, -(TWO_PI**15) / math.factorial(15))
    for power in range(14, -1, -2):
        sign = -1.0 if power % 4 == 2 else 1.0
        cos_t = cos_t * square + sign * TWO_PI**power / math.factorial(power)
        if power > 0:
            sign = -1.0 if (power - 1) % 4 == 3 else 1.0
            sin_t = sin_t * square + sign * TWO_PI ** (power - 1) / math.factorial(power - 1)
    scaled = gains[...] * (1.0 / math.sqrt(gains.shape[1]))
    out[0, :beams] = (scaled * cos_t).astype(out.dtype)
    out[0, beams:] = (-scaled * sin_t * part).astype(out.dtype)


def beam_weights(channel, delays, gains):
    beams, listed = delays.shape
    slots = channel.shape[0]
    return pl.pallas_call(
        weight_kernel,
        grid=(slots,),
        in_specs=[
            pl.BlockSpec(memory_space=pltpu.SMEM),
            pl.BlockSpec(delays.shape, lambda i: (0, 0)),
            pl.BlockSpec(gains.shape, lambda i: (0, 0)),
        ],
        out_specs=pl.BlockSpec((1, 2 * beams, listed), lambda i: (i, 0, 0)),
        out_shape=jax.ShapeDtypeStruct((slots, 2 * beams, listed), jnp.bfloat16),
        cost_estimate=NO_COST,
    )(channel, delays, gains)


def combine(spectra, chooser, weights, sub):
    slots, beams2, listed = weights.shape
    beams = beams2 // 2
    rows = 2 * slots
    senders = spectra.shape[0]
    halves = spectra.shape[2] // (FRAMES * sub)
    count = LANES // sub
    inner = senders // count
    groups = halves * inner
    tiles = 2 * listed // LANES

    def kernel(spectrum, choose, weight_hbm, out, ordered, picked, weight, sem):
        coming = pltpu.make_async_copy(weight_hbm, weight, sem)
        coming.start()
        lane_ids = lax.broadcasted_iota(jnp.int32, (rows, LANES), 1)
        for h in range(halves):
            for q in range(inner):
                for t in range(FRAMES // count):
                    lane = h * FRAMES * sub + t * LANES
                    pieces = [
                        spectrum[q * count + i, :, lane : lane + LANES].astype(jnp.float32) for i in range(count)
                    ]
                    for f, piece in enumerate(swap_blocks(pieces, lane_ids)):
                        top = (t * count + f) * rows
                        group = (h * inner + q) * LANES
                        ordered[top : top + rows, group : group + LANES] = piece
        acc = jnp.dot(ordered[...].astype(jnp.bfloat16), choose[...], preferred_element_type=jnp.float32)
        for lane in range(tiles):
            picked[lane] = acc[:, lane * LANES : (lane + 1) * LANES]
        coming.wait()
        for i in range(slots):
            chosen = [
                jnp.concatenate(
                    [
                        picked[p * tiles // 2 + lane, pl.ds(part * slots + i, FRAMES, rows), :]
                        for lane in range(tiles // 2)
                    ],
                    axis=1,
                )
                for p in range(2)
                for part in range(2)
            ]
            stacked = jnp.concatenate(chosen, axis=0).astype(jnp.bfloat16)
            mixed = lax.dot_general(stacked, weight[i], NT, preferred_element_type=jnp.float32)
            for p in range(2):
                at = 2 * FRAMES * p
                of_re, of_im = mixed[at : at + FRAMES], mixed[at + FRAMES : at + 2 * FRAMES]
                out[0, i, 0, :, p * beams : (p + 1) * beams] = of_re[:, :beams] - of_im[:, beams:]
                out[0, i, 1, :, p * beams : (p + 1) * beams] = of_im[:, :beams] + of_re[:, beams:]

    return pl.pallas_call(
        kernel,
        in_specs=[pl.BlockSpec(memory_space=pltpu.VMEM)] * 2 + [pl.BlockSpec(memory_space=pl.ANY)],
        out_shape=jax.ShapeDtypeStruct((1, slots, 2, FRAMES, 2 * beams), jnp.float32),
        scratch_shapes=[
            pltpu.VMEM((FRAMES * rows, groups * LANES), jnp.float32),
            pltpu.VMEM((tiles, FRAMES * rows, LANES), jnp.float32),
            pltpu.VMEM(weights.shape, weights.dtype),
            pltpu.SemaphoreType.DMA,
        ],
        compiler_params=pltpu.CompilerParams(vmem_limit_bytes=VMEM),
        cost_estimate=NO_COST,
    )(spectra, chooser, weights)


def body(volts, prototype, beam_channels, station_index, delays, gains, assign):
    sig_dev = volts.shape[1]
    far, near, sb_count = lax.axis_size("far"), lax.axis_size("near"), lax.axis_size("sb")
    far_here, near_here, sb_here = [lax.axis_index(name).astype(jnp.int32) for name in ("far", "near", "sb")]
    st_count = far * near
    devices = st_count * sb_count
    group = NCH // devices
    fine = group // RADIX
    constants = transform_tables()
    barrier = lax.optimization_barrier

    def exchange(x):
        return lax.all_to_all(x, ("sb", "near", "far"), split_axis=0, concat_axis=0, tiled=True)

    share = sig_dev // sb_count
    sub = min(share, ROWS)
    halves = max(1, share // ROWS)
    inside = (sb_here * share) % ROWS
    unit = max(1, LANES // group)
    early = max(unit, EARLY // unit * unit)
    plan = [(0, 0, early), (0, early, FRAMES - early)] + [(h, 0, FRAMES) for h in range(1, halves)]

    def channels_of(c, here):
        which, first, frames = plan[c]
        row_block = (here * share // ROWS + which)[None]
        out, kept = channelise(row_block, volts, prototype, constants, first, frames, far)
        if sub < ROWS:
            out = lax.dynamic_slice_in_dim(out, inside, sub, axis=3)
        inner = st_count // RADIX
        if inner > 1:
            out = out.reshape(sb_count, near // inner, far, sub, 2 * frames, RADIX, inner, fine)
            out = out.transpose(0, 1, 6, 2, 3, 4, 5, 7)
        return out.reshape(devices, sub, -1), kept

    lists = (assign, beam_channels, station_index)
    here = sb_here
    out, kept = channels_of(0, here)
    branches, arrived = [kept], []
    for c in range(1, len(plan)):
        out, here, lists, arrived[-1:] = barrier((out, here, lists, arrived[-1:]))
        arrived.append(exchange(out))
        out, kept = channels_of(c, here)
        branches.append(kept)

    assign, beam_channels, station_index = barrier((lists, kept))[0]
    per_dev = SLOTS // st_count
    owners = assign[:, 0]
    taken = (owners[:, None] == jnp.arange(sb_count, dtype=jnp.int32)[None, :]).astype(jnp.int32)
    position = jnp.sum(taken * jnp.cumsum(taken, axis=0), axis=1) - 1
    place = owners * SLOTS + position
    slot_ids = (
        jnp.arange(sb_count, dtype=jnp.int32)[:, None, None, None] * SLOTS
        + jnp.arange(near, dtype=jnp.int32)[:, None, None] * per_dev
        + jnp.arange(far, dtype=jnp.int32)[:, None] * (near * per_dev)
        + jnp.arange(per_dev, dtype=jnp.int32)
    ).reshape(-1)
    picker = (place[None, :] == slot_ids[:, None]).astype(jnp.int32)
    filled = jnp.sum(picker, axis=1)
    slot_channel = jnp.sum(picker * beam_channels[None, :], axis=1)

    def by_row(values):
        return jnp.broadcast_to(values.reshape(devices, 1, per_dev), (devices, 2, per_dev)).reshape(-1)

    turned = jnp.broadcast_to(jnp.arange(2, dtype=jnp.int32)[None, :, None], (devices, 2, per_dev)).reshape(-1)
    own = ((sb_here * near + near_here) * far + far_here) * per_dev
    mine = lax.dynamic_slice_in_dim(slot_channel, own, per_dev)
    tables = slot_tables(by_row(slot_channel), by_row(filled), turned)
    spectra = slot_spectra(tables, branches, 2 * per_dev)
    if sub < ROWS:
        spectra = spectra.reshape(devices, 2 * per_dev, FRAMES, ROWS)
        spectra = lax.dynamic_slice_in_dim(spectra, inside, sub, axis=3).reshape(devices, 2 * per_dev, -1)

    out, spectra, mine, arrived[-1:] = barrier((out, spectra, mine, arrived[-1:]))
    arrived.append(exchange(out))
    weights = beam_weights(mine, delays, gains)
    signal_ids = (
        jnp.arange(halves, dtype=jnp.int32)[:, None, None, None, None] * sub
        + jnp.arange(sb_count, dtype=jnp.int32)[:, None, None, None] * share
        + jnp.arange(near, dtype=jnp.int32)[:, None, None] * sig_dev
        + jnp.arange(far, dtype=jnp.int32)[:, None] * (near * sig_dev)
        + jnp.arange(sub, dtype=jnp.int32)
    ).reshape(-1)
    wanted = (station_index[None, :] * 2 + jnp.arange(2, dtype=jnp.int32)[:, None]).reshape(-1)
    chooser = (signal_ids[:, None] == wanted[None, :]).astype(jnp.bfloat16)

    spectra, weights, chooser, arrived[-1:] = barrier((spectra, weights, chooser, arrived[-1:]))
    slot_received = exchange(spectra)
    arrived = [x.reshape(sb_count, near, far, sub, -1) for x in arrived]
    if halves == 1:
        arrived = [x.transpose(2, 1, 0, 3, 4).reshape(1, 1, far, near * sb_count * sub, -1) for x in arrived]
    visibility = correlate([(x, *part) for x, part in zip(arrived, plan)], halves, group)
    signals = visibility.shape[1]
    beam_out = combine(slot_received, chooser, weights, sub)
    return (visibility.reshape(2, 1, 1, signals, signals), beam_out)


def solution(mesh):
    st_count, sb_count = mesh.shape["st"], mesh.shape["sb"]
    far = math.gcd(4, st_count)
    planes = Mesh(mesh.devices.reshape(far, st_count // far, sb_count), ("far", "near", "sb"))
    st = ("far", "near")
    in_specs = (P(None, st, None), P(), P(), P(), P(), P(), P())
    out_specs = (P(None, "sb", st, None, None), P("sb", st, None, None, None))
    return jax.shard_map(body, mesh=planes, in_specs=in_specs, out_specs=out_specs, check_vma=False)
```
